32 devices in a mesh: section: 2 (over x), dp: 4 (over z), mp: 4 (over y, core).
Axes of the slice: x: 2, y: 2, z: 4, core: 2. Of those that a mesh axis runs over, the one named last changes fastest.
Arguments:
- x_visible: bfloat16 [8, 512, 768], P('dp', 'mp'), may hold values from -6 to 6
- resolution: int32 [8], P('dp'), may hold values from 0 to 1, as said below
- visible_index: int32 [8, 512], P('dp'), may hold values from 0 to 2047, as said below
- enc_qkv_w: bfloat16 [768, 3, 768], P(('section', 'dp'), None, 'mp'), may hold values from -0.21875 to 0.21875
- enc_out_w: bfloat16 [768, 768], P('mp', ('section', 'dp')), may hold values from -0.875 to 0.875
- enc_up_w: bfloat16 [768, 3072], P(('section', 'dp'), 'mp'), may hold values from -0.21875 to 0.21875
- enc_down_w: bfloat16 [3072, 768], P('mp', ('section', 'dp')), may hold values from -0.109375 to 0.109375
- enc_gains: float32 [2, 768], replicated, may hold values from 0.1 to 1.9
- enc_shifts: float32 [2, 768], replicated, may hold values from -1.8 to 1.8
- projection: bfloat16 [768, 512], replicated, may hold values from -0.21875 to 0.21875
- mask_token: float32 [512], replicated, may hold values from -5 to 5
- dec_qkv_w: bfloat16 [512, 3, 512], P(('section', 'dp'), None, 'mp'), may hold values from -0.25 to 0.25
- dec_out_w: bfloat16 [512, 512], P('mp', ('section', 'dp')), may hold values from -1.5 to 1.5
- dec_up_w: bfloat16 [512, 2048], P(('section', 'dp'), 'mp'), may hold values from -0.25 to 0.25
- dec_down_w: bfloat16 [2048, 512], P('mp', ('section', 'dp')), may hold values from -0.125 to 0.125
- dec_gains: float32 [2, 512], replicated, may hold values from 0.1 to 1.9
- dec_shifts: float32 [2, 512], replicated, may hold values from -1.8 to 1.8
- cotangent: bfloat16 [8, 2048, 512], P('dp', 'mp'), may hold values from -6 to 6
Outputs:
- decoded: bfloat16 [8, 2048, 512], P('dp', 'mp', 'section')
- input_grad: float32 [8, 512, 768], P('dp', 'mp', 'section')
- enc_qkv_grad: float32 [768, 3, 768], P(('section', 'dp'), None, 'mp')
- enc_out_grad: float32 [768, 768], P('mp', ('section', 'dp'))
- enc_up_grad: float32 [768, 3072], P(('section', 'dp'), 'mp')
- enc_down_grad: float32 [3072, 768], P('mp', ('section', 'dp'))
- enc_gains_grad: float32 [2, 768], replicated
- enc_shifts_grad: float32 [2, 768], replicated
- projection_grad: float32 [768, 512], replicated
- mask_grad: float32 [512], replicated
- dec_qkv_grad: float32 [512, 3, 512], P(('section', 'dp'), None, 'mp')
- dec_out_grad: float32 [512, 512], P('mp', ('section', 'dp'))
- dec_up_grad: float32 [512, 2048], P(('section', 'dp'), 'mp')
- dec_down_grad: float32 [2048, 512], P('mp', ('section', 'dp'))
- dec_gains_grad: float32 [2, 512], replicated
- dec_shifts_grad: float32 [2, 512], replicated
The draws below stay inside these ranges and needn't reach their ends.
Inputs may be any that keep to these rules, and one draw needn't show every extreme that they name: `resolution`: 1 selects the 32 x 64 grid, 0 the 16 x 32 grid; samples 2k and 2k + 1 hold at least one 1 for each k. `visible_index`: for a big-grid sample the 512 entries are distinct positions below 2048; for a small-grid sample the first 128 entries are distinct positions below 512 and the others are 0. Position p lies in row p // width and column p % width of its grid.
All inputs are finite; a program needn't handle non-finite values.
Results may differ from the reference program's by a relative error of at most 0.018.
Values may be sent and summed in bfloat16 or wider, within the bound.
A program may use at most 256 MiB of HBM per device.

```python
import jax
import jax.numpy as jnp
from jax import lax

D_ENC = 768
HD_ENC = 64
FF_ENC = 3072
D_DEC = 512
HD_DEC = 32
FF_DEC = 2048
COLS_SMALL = 32
COLS_BIG = 64
MICRO = 2
PATCHES = 2048
SMALL_PATCHES = 512
VIS = 512
VIS_SMALL = 128
SAMPLES = 8


def resolution_draw(key):
    coarse = jax.random.randint(jax.random.fold_in(key, 11), (SAMPLES,), 0, 2)
    forced = jax.random.randint(jax.random.fold_in(key, 12), (SAMPLES // MICRO,), 0, MICRO)
    position_in_group = jnp.arange(SAMPLES) % MICRO
    return jnp.where(position_in_group == jnp.repeat(forced, MICRO), 1, coarse).astype(jnp.int32)


def draw_resolution(key, part):
    shared = resolution_draw(key)
    return shared


def draw_visible_index(key, part):
    levels = resolution_draw(key)
    key = jax.random.fold_in(key, 5)
    sample_keys = jax.random.split(key, SAMPLES)

    def one_sample(sample_key, grid_level):
        grid_limit = jnp.where(grid_level == 1, PATCHES, SMALL_PATCHES)
        drawn_count = jnp.where(grid_level == 1, VIS, VIS_SMALL)
        rank_values = jax.random.permutation(sample_key, PATCHES)
        order_keys = jnp.where(jnp.arange(PATCHES) < grid_limit, rank_values, rank_values + PATCHES)
        picked = jnp.argsort(order_keys)[:VIS]
        return jnp.where(jnp.arange(VIS) < drawn_count, picked, 0).astype(jnp.int32)
    return jax.vmap(one_sample)(sample_keys, levels)


def level_of(own_key, extent, cuts, low, largest):
    def one(position, shards_of):
        draws = jax.random.uniform(jax.random.fold_in(jax.random.fold_in(own_key, 6), position), (shards_of,), jnp.float32, low / len(cuts), largest / len(cuts))
        return jnp.repeat(jnp.exp(draws), extent[position] // shards_of).reshape((-1,) + (1,) * (len(extent) - position - 1))

    factor_of = one(*cuts[0])
    for cut in cuts[1:]:
        factor_of = factor_of * one(*cut)
    return factor_of


def bell_draw(own_key, extent, width, reach, pieces=(), kind=jnp.bfloat16):
    result = jax.random.normal(own_key, extent, jnp.float32) * width
    if len(pieces) > 0:
        result = level_of(own_key, extent, pieces, -0.22, 0.18) * result
    return jnp.clip(result, min=-reach, max=reach).astype(kind)


def setup_inputs(seed: int = 0) -> dict:
    streams_of = jax.random.split(jax.random.key(seed), 19)
    x_visible = bell_draw(streams_of[0], (SAMPLES, VIS, D_ENC), 1.0, 6.0, ((0, 4), (1, 4)))
    resolution = draw_resolution(jax.random.fold_in(streams_of[18], 71), 0)
    visible_index = draw_visible_index(jax.random.fold_in(streams_of[18], 71), 0)
    enc_qkv_w = bell_draw(streams_of[3], (D_ENC, 3, D_ENC), D_ENC ** -0.5, 0.21875, ((0, 8), (2, 4)))
    enc_out_w = bell_draw(streams_of[4], (D_ENC, D_ENC), (D_ENC // 16) ** -0.5, 0.875, ((0, 4), (1, 8)))
    enc_up_w = bell_draw(streams_of[5], (D_ENC, FF_ENC), D_ENC ** -0.5, 0.21875, ((0, 8), (1, 4)))
    enc_down_w = bell_draw(streams_of[6], (FF_ENC, D_ENC), FF_ENC ** -0.5, 0.109375, ((0, 4), (1, 8)))
    enc_gains = jnp.clip(1.0 + 0.18 * jax.random.normal(streams_of[7], (2, D_ENC), jnp.float32), 0.1, 1.9)
    enc_shifts = bell_draw(streams_of[8], (2, D_ENC), 0.3, 1.8, (), jnp.float32)
    projection = bell_draw(streams_of[9], (D_ENC, D_DEC), D_ENC ** -0.5, 0.21875)
    mask_token = bell_draw(streams_of[10], (D_DEC,), 1.0, 5.0, (), jnp.float32)
    dec_qkv_w = bell_draw(streams_of[11], (D_DEC, 3, D_DEC), D_DEC ** -0.5, 0.25, ((0, 8), (2, 4)))
    dec_out_w = bell_draw(streams_of[12], (D_DEC, D_DEC), (D_DEC // 32) ** -0.5, 1.5, ((0, 4), (1, 8)))
    dec_up_w = bell_draw(streams_of[13], (D_DEC, FF_DEC), D_DEC ** -0.5, 0.25, ((0, 8), (1, 4)))
    dec_down_w = bell_draw(streams_of[14], (FF_DEC, D_DEC), FF_DEC ** -0.5, 0.125, ((0, 4), (1, 8)))
    dec_gains = jnp.clip(1.0 + 0.18 * jax.random.normal(streams_of[15], (2, D_DEC), jnp.float32), 0.1, 1.9)
    dec_shifts = bell_draw(streams_of[16], (2, D_DEC), 0.3, 1.8, (), jnp.float32)
    cotangent = bell_draw(streams_of[17], (SAMPLES, PATCHES, D_DEC), 1.0, 6.0, ((0, 4), (1, 4)))
    return dict(x_visible=x_visible, resolution=resolution, visible_index=visible_index, enc_qkv_w=enc_qkv_w, enc_out_w=enc_out_w, enc_up_w=enc_up_w, enc_down_w=enc_down_w, enc_gains=enc_gains, enc_shifts=enc_shifts, projection=projection, mask_token=mask_token, dec_qkv_w=dec_qkv_w, dec_out_w=dec_out_w, dec_up_w=dec_up_w, dec_down_w=dec_down_w, dec_gains=dec_gains, dec_shifts=dec_shifts, cotangent=cotangent)


PRECISE = lax.Precision.HIGHEST

@jax.custom_vjp
def low(v):
    return lax.optimization_barrier(v.astype(jnp.bfloat16)).astype(jnp.float32)

@jax.custom_vjp
def low_back(v):
    return v

def low_keep(v):
    return (low(v), None)

def low_pass(kept, grad):
    return (grad,)

def back_keep(v):
    return (v, None)

def back_low(kept, grad):
    return (low(grad),)
low.defvjp(low_keep, low_pass)
low_back.defvjp(back_keep, back_low)

def layer_norm(values, gain_row, shift_row):
    centre = values - lax.optimization_barrier(jnp.mean(values, axis=-1, keepdims=True))
    spread_sq = lax.optimization_barrier(jnp.mean(centre * centre, axis=-1, keepdims=True))
    return centre * lax.rsqrt(spread_sq + 1e-06) * gain_row + shift_row

def sincos_table(positions, grid_width, model_width):
    quarter = model_width // 4
    frequency = 10000.0 ** (-jnp.arange(quarter, dtype=jnp.float32) / quarter)
    rows_at = (positions // grid_width).astype(jnp.float32)
    cols_at = (positions % grid_width).astype(jnp.float32)
    row_angle = rows_at[:, None] * frequency[None, :]
    col_angle = cols_at[:, None] * frequency[None, :]
    return jnp.concatenate([jnp.sin(row_angle), jnp.cos(row_angle), jnp.sin(col_angle), jnp.cos(col_angle)], axis=-1)

def whole_block(stream, qkv_weight, out_weight, up_weight, down_weight, gain_rows, shift_rows, key_live, head_dim):
    length, model_width = stream.shape
    head_count = model_width // head_dim
    normed = low(layer_norm(stream, gain_rows[0], shift_rows[0]))
    qkv_rows = jnp.dot(normed, qkv_weight.reshape(model_width, 3 * model_width), precision=PRECISE)
    qkv_rows = low_back(low(qkv_rows)).reshape(length, 3, head_count, head_dim)
    queries = qkv_rows[:, 0]
    key_rows = qkv_rows[:, 1]
    value_rows = qkv_rows[:, 2]
    raw_scores = low_back(jnp.einsum('qhd,khd->hqk', queries, key_rows, precision=PRECISE))
    scores = jnp.where(key_live[None, None, :], raw_scores * head_dim ** (-0.5), -1e+30)
    weights = low(jax.nn.softmax(scores, axis=-1))
    context = jnp.einsum('hqk,khd->qhd', weights, value_rows, precision=PRECISE).reshape(length, model_width)
    context = low_back(low(context))
    attended = low_back(jnp.dot(context, out_weight, precision=PRECISE))
    middle = stream + attended
    normed_mid = low(layer_norm(middle, gain_rows[1], shift_rows[1]))
    hidden = low_back(jnp.dot(normed_mid, up_weight, precision=PRECISE))
    active = low(jax.nn.gelu(hidden, approximate=False))
    return middle + low_back(jnp.dot(active, down_weight, precision=PRECISE))

def reference(x_visible, resolution, visible_index, enc_qkv_w, enc_out_w, enc_up_w, enc_down_w, enc_gains, enc_shifts, projection, mask_token, dec_qkv_w, dec_out_w, dec_up_w, dec_down_w, dec_gains, dec_shifts, cotangent):
    params = (enc_qkv_w.astype(jnp.float32), enc_out_w.astype(jnp.float32), enc_up_w.astype(jnp.float32), enc_down_w.astype(jnp.float32), enc_gains.astype(jnp.float32), enc_shifts.astype(jnp.float32), projection.astype(jnp.float32), mask_token.astype(jnp.float32), dec_qkv_w.astype(jnp.float32), dec_out_w.astype(jnp.float32), dec_up_w.astype(jnp.float32), dec_down_w.astype(jnp.float32), dec_gains.astype(jnp.float32), dec_shifts.astype(jnp.float32))

    def forward(param_set, stream_all):

        def one_sample(packed):
            stream, grid_level, chosen = packed
            shown_count = jnp.where(grid_level == 1, VIS, VIS_SMALL)
            grid_width = jnp.where(grid_level == 1, COLS_BIG, COLS_SMALL)
            filled = jnp.where(grid_level == 1, PATCHES, SMALL_PATCHES)
            seen_valid = jnp.arange(VIS) < shown_count
            grid_valid = jnp.arange(PATCHES) < filled
            encoded = whole_block(stream, param_set[0], param_set[1], param_set[2], param_set[3], param_set[4], param_set[5], seen_valid, HD_ENC)
            lowered = low_back(low(jnp.dot(low(encoded), param_set[6], precision=PRECISE)))
            place_table = ((jnp.arange(PATCHES)[:, None] == chosen[None, :]) & seen_valid[None, :]).astype(jnp.float32)
            placed = jnp.dot(place_table, lowered, precision=PRECISE)
            seen_count = lax.optimization_barrier(jnp.sum(place_table, axis=1, keepdims=True))
            live_rows = grid_valid.astype(jnp.float32)[:, None]
            start_rows = low_back(placed + (live_rows - seen_count) * param_set[7] + live_rows * sincos_table(jnp.arange(PATCHES), grid_width, D_DEC))
            decoded_rows = whole_block(start_rows, param_set[8], param_set[9], param_set[10], param_set[11], param_set[12], param_set[13], grid_valid, HD_DEC)
            return decoded_rows * live_rows
        return lax.map(jax.checkpoint(one_sample), (stream_all, resolution, visible_index))
    decoded, pull_back = jax.vjp(forward, params, x_visible.astype(jnp.float32))
    param_grads, input_grad = pull_back(cotangent.astype(jnp.float32))
    return (decoded.astype(jnp.bfloat16), input_grad, param_grads[0], param_grads[1], param_grads[2], param_grads[3], param_grads[4], param_grads[5], param_grads[6], param_grads[7], param_grads[8], param_grads[9], param_grads[10], param_grads[11], param_grads[12], param_grads[13])
```

```python
import functools
import math

import jax
import jax.numpy as jnp
import numpy as np
from jax import lax
from jax.experimental import pallas as pl
from jax.experimental.pallas import tpu as pltpu
from jax.sharding import PartitionSpec as P

HD_ENC = 64
HD_DEC = 32
COLS_SMALL = 32
COLS_BIG = 64
PATCHES = 2048
SMALL_PATCHES = 512
VIS = 512
VIS_SMALL = 128

MESH = pl.DeviceIdType.MESH
bf = jnp.bfloat16
f32 = jnp.float32
LOG2E = 1.4426950408889634
NEG = -1e30


def nn(a, b):
    return lax.dot_general(a, b, (((1,), (0,)), ((), ())), preferred_element_type=f32)


def nt(a, b):
    return lax.dot_general(a, b, (((1,), (1,)), ((), ())), preferred_element_type=f32)


def tn(a, b):
    return lax.dot_general(a, b, (((0,), (0,)), ((), ())), preferred_element_type=f32)


def norm_stats(stream):
    centre = stream - jnp.mean(stream, axis=-1, keepdims=True)
    inverse = lax.rsqrt(jnp.mean(centre * centre, axis=-1, keepdims=True) + 1e-06)
    return centre * inverse, inverse


def normalize(stream, gain, shift):
    scaled, _ = norm_stats(stream)
    return scaled * gain + shift


def normalize_back(stream, gain, grad_out):
    scaled, inverse = norm_stats(stream)
    f = grad_out * gain
    grad_in = inverse * (
        f
        - jnp.mean(f, axis=-1, keepdims=True)
        - scaled * jnp.mean(f * scaled, axis=-1, keepdims=True)
    )
    return (
        grad_in,
        jnp.sum(grad_out * scaled, axis=0, keepdims=True),
        jnp.sum(grad_out, axis=0, keepdims=True),
    )


def gelu_and_slope(a):
    x = jnp.abs(a) * 0.7071067811865476
    t = 1.0 / (1.0 + 0.3275911 * x)
    e = jnp.exp2(x * x * (-LOG2E))
    poly = ((((1.061405429 * t - 1.453152027) * t + 1.421413741) * t - 0.284496736) * t + 0.254829592) * t
    tail = 0.5 * poly * e
    phi = jnp.where(a >= 0, 1.0 - tail, tail)
    return a * phi, phi + a * e * 0.3989422804014327


class Ctx:
    def __init__(self, ss, rs, dp):
        self.ss, self.rs, self.n, self.dp = ss, rs, 0, dp
        self.s = lax.axis_index("section")
        self.d = lax.axis_index("dp")
        self.m = lax.axis_index("mp")
        m = self.m
        self.lo = lax.rem(m, 2)
        self.hi = m // 2
        self.m1 = m + 1 - 2 * self.lo
        self.m2 = lax.rem(m + 2, 4)
        self.m3 = lax.rem(self.m1 + 2, 4)
        self.core = {"mp": self.m1}
        self.y = {"mp": self.m2}
        self.x = {"section": 1 - self.s}
        self.pending = []

    def z(self, k):
        return {"dp": lax.rem(self.d + k, self.dp)}

    def barrier(self, peers):
        b = pltpu.get_barrier_semaphore()
        for p in peers:
            pl.semaphore_signal(b, inc=1, device_id=p, device_id_type=MESH)
        pl.semaphore_wait(b, len(peers))

    def send(self, src, dst, dev):
        i = self.n
        self.n += 1
        c = pltpu.make_async_remote_copy(
            src_ref=src,
            dst_ref=dst,
            send_sem=self.ss.at[i],
            recv_sem=self.rs.at[i],
            device_id=dev,
            device_id_type=MESH,
        )
        c.start()
        self.pending.append(c)
        return c

    def drain(self):
        for c in self.pending:
            c.wait_send()
        self.pending = []


class GatherMp:
    def __init__(self, cx, buf):
        self.cx, self.buf = cx, buf
        m = cx.m
        self.c2 = cx.send(buf.at[m], buf.at[m], cx.y)
        self.c1 = cx.send(buf.at[m], buf.at[m], cx.core)

    def forward(self):
        cx, buf = self.cx, self.buf
        self.c2.wait_recv()
        self.c3 = cx.send(buf.at[cx.m2], buf.at[cx.m2], cx.core)

    def near(self):
        self.c1.wait_recv()

    def far(self):
        self.c3.wait_recv()

    def finish(self):
        self.forward()
        self.near()
        self.far()


def reduce_mp(cx, part, stage, recv):
    stage[0] = part[cx.m3].astype(bf)
    c3 = cx.send(stage.at[0], recv.at[0], cx.core)
    stage[1] = part[cx.m1].astype(bf)
    c1 = cx.send(stage.at[1], recv.at[1], cx.core)
    c3.wait_recv()
    stage[2] = (part[cx.m2] + recv[0].astype(f32)).astype(bf)
    c2 = cx.send(stage.at[2], recv.at[2], cx.y)
    c1.wait_recv()
    own = part[cx.m] + recv[1].astype(f32)
    c2.wait_recv()
    return own + recv[2].astype(f32)


class GatherW:
    def __init__(self, cx, shard, whole):
        self.cx, self.whole, self.rows = cx, whole, shard.shape[0]
        own = self.at(cx.s, cx.d)
        self.zs = [cx.send(shard, own, cx.z(k)) for k in range(1, cx.dp)]
        self.xs = [cx.send(shard, own, cx.x)]
        own[...] = shard[...]

    def at(self, s, d):
        start = (s * self.cx.dp + d) * self.rows
        return self.whole.at[pl.ds(pl.multiple_of(start, 16), self.rows)]

    def forward(self):
        cx = self.cx
        for k in range(1, cx.dp):
            self.zs[k - 1].wait_recv()
            block = self.at(cx.s, lax.rem(cx.d + cx.dp - k, cx.dp))
            self.xs.append(cx.send(block, block, cx.x))

    def finish(self):
        for c in self.xs:
            c.wait_recv()


class ScatterW:
    def __init__(self, cx, rows, out, xs, xr, zs, zr):
        self.cx, self.rows, self.out = cx, rows, out
        self.xs, self.xr, self.zs, self.zr = xs, xr, zs, zr

    def section(self, s):
        size = self.cx.dp * self.rows
        return pl.ds(pl.multiple_of(s * size, 16), size)

    def start(self, part):
        cx = self.cx
        self.part = part
        self.xs[...] = part[self.section(1 - cx.s), :].astype(bf)
        self.cx_copy = cx.send(self.xs, self.xr, cx.x)

    def middle(self):
        cx, rows = self.cx, self.rows
        self.cx_copy.wait_recv()
        total = self.part[self.section(cx.s), :] + self.xr[...].astype(f32)
        self.zs[...] = total.astype(bf)
        self.copies = []
        for k in range(1, cx.dp):
            to = lax.rem(cx.d + k, cx.dp)
            block = self.zs.at[pl.ds(pl.multiple_of(to * rows, 16), rows)]
            self.copies.append(cx.send(block, self.zr.at[k - 1], cx.z(k)))

    def finish(self):
        cx, rows = self.cx, self.rows
        start = (cx.s * cx.dp + cx.d) * rows
        mine = pl.ds(pl.multiple_of(cx.d * rows, 16), rows)
        own = self.part[pl.ds(pl.multiple_of(start, 16), rows), :] + self.xr[mine, :].astype(f32)
        for k in range(1, cx.dp):
            self.copies[k - 1].wait_recv()
            own = own + self.zr[k - 1].astype(f32)
        self.out[...] = own


def iota(shape, dim):
    return lax.broadcasted_iota(jnp.int32, shape, dim)


def enc_forward_kernel(dp, gather, *refs):
    it = iter(refs)
    take = lambda n: [next(it) for _ in range(n)]
    res, x_all, gains, shifts, proj = take(5)
    shards = take(6)
    if gather:
        wa, wb, wc, wd, we, wf = take(6)
    else:
        wa, wb, wc = shards[:3]
        wd, we, wf = take(3)
    n1, n2, qkv, ctx, slope, active, mid_out, top_out, low_all = take(9)
    ss, rs, part, stage, recv = take(5)
    cx = Ctx(ss, rs, dp)
    peers = [cx.core, cx.y]
    if gather:
        peers += [cx.x] + [cx.z(k) for k in range(1, dp)]
    cx.barrier(peers)
    if gather:
        ga = GatherW(cx, shards[0], wa)
    stream = x_all[cx.s].astype(f32)
    n1[cx.m] = normalize(stream, gains[0:1, :], shifts[0:1, :]).astype(bf)
    g1 = GatherMp(cx, n1)
    if gather:
        gb = GatherW(cx, shards[1], wb)
        gc = GatherW(cx, shards[2], wc)
    g1.finish()
    if gather:
        ga.forward()
        gd = GatherW(cx, shards[3], wd.at[0])
        ge = GatherW(cx, shards[4], we.at[0])
        gf = GatherW(cx, shards[5], wf.at[0])
        ga.finish()
    rows = n1.shape[1]
    total = 4 * rows
    width = n1.shape[2]
    n1_all = n1[...].reshape(total, width)
    qkv[...] = nn(n1_all, wa[...]).astype(bf)
    if gather:
        gb.forward()
    shown = jnp.where(res[cx.s] == 1, VIS, VIS_SMALL)
    bias = jnp.where(iota((1, total), 1) < shown, 0.0, NEG)
    scale2 = HD_ENC**-0.5 * LOG2E
    heads = (width // 4) // HD_ENC
    pieces = [jnp.zeros((total, HD_ENC), bf)]
    for h in range(heads):
        q = qkv[:, h * HD_ENC : (h + 1) * HD_ENC]
        k = qkv[:, (heads + h) * HD_ENC : (heads + h + 1) * HD_ENC]
        v = qkv[:, (2 * heads + h) * HD_ENC : (2 * heads + h + 1) * HD_ENC]
        sc = nt(q, k) + bias
        top = jnp.max(sc, axis=1, keepdims=True)
        e = jnp.exp2((sc - top) * scale2)
        tot = jnp.sum(e, axis=1, keepdims=True)
        pieces.append((nn(e.astype(bf), v) / tot).astype(bf))
    ctx[...] = jnp.concatenate(pieces, axis=1)
    if gather:
        gc.forward()
    cpad = ctx.shape[1]
    part[...] = nt(ctx[...], wa[:, width - cpad :]).reshape(part.shape)
    mid = stream + reduce_mp(cx, part, stage.at[0], recv.at[0])
    mid_out[...] = mid
    n2[cx.m] = normalize(mid, gains[1:2, :], shifts[1:2, :]).astype(bf)
    g2 = GatherMp(cx, n2)
    if gather:
        gb.finish()
    g2.finish()
    hid = nn(n2[...].reshape(total, width), wb[...])
    act, slo = gelu_and_slope(hid)
    active[...] = act.astype(bf)
    slope[...] = slo.astype(bf)
    if gather:
        gd.forward()
        gc.finish()
    part[...] = nt(active[...], wc[...]).reshape(part.shape)
    top = (mid_out[...] + reduce_mp(cx, part, stage.at[1], recv.at[1])).astype(bf)
    top_out[...] = top
    low_all[cx.m] = nn(top, proj[...]).astype(bf)
    g3 = GatherMp(cx, low_all)
    if gather:
        ge.forward()
        gf.forward()
        gd.finish()
        yd = cx.send(wd.at[0], wd.at[1], cx.y)
    else:
        for w, sh in zip((wd, we, wf), shards[3:]):
            w[0] = sh[...]
        yd = cx.send(wd.at[0], wd.at[1], cx.y)
    g3.finish()
    if gather:
        ge.finish()
    ye = cx.send(we.at[0], we.at[1], cx.y)
    if gather:
        gf.finish()
    yf = cx.send(wf.at[0], wf.at[1], cx.y)
    yd.wait_recv()
    ye.wait_recv()
    yf.wait_recv()
    cx.drain()


def vm(n):
    return [pl.BlockSpec(memory_space=pltpu.VMEM)] * n


SMEM = pl.BlockSpec(memory_space=pltpu.SMEM)


def sds(shape, dtype):
    return jax.ShapeDtypeStruct(shape, dtype)


def params(cid):
    return pltpu.CompilerParams(collective_id=cid, has_side_effects=True, vmem_limit_bytes=60 << 20)


def enc_forward(dp, gather, res, x, gains, shifts, proj, shards, de, dd):
    rows, width = x.shape[1:]
    total = 4 * rows
    slots = (4, rows, width)
    outs = []
    if gather:
        outs += [sds((de, shards[i].shape[1]), bf) for i in range(3)]
    outs += [sds((2, dd, shards[i].shape[1]), bf) for i in range(3, 6)]
    wide = shards[1].shape[1]
    outs += [
        sds(slots, bf),
        sds(slots, bf),
        sds((total, width), bf),
        sds((total, 256), bf),
        sds((total, wide), bf),
        sds((total, wide), bf),
        sds((rows, width), f32),
        sds((rows, width), bf),
        sds((4, rows, dd), bf),
    ]
    got = pl.pallas_call(
        functools.partial(enc_forward_kernel, dp, gather),
        out_shape=outs,
        in_specs=[SMEM] + vm(10),
        out_specs=vm(len(outs)),
        scratch_shapes=[
            pltpu.SemaphoreType.DMA((80,)),
            pltpu.SemaphoreType.DMA((80,)),
            pltpu.VMEM(slots, f32),
            pltpu.VMEM((2, 3, rows, width), bf),
            pltpu.VMEM((2, 3, rows, width), bf),
        ],
        compiler_params=params(1),
        name="enc_forward",
    )(res, x, gains, shifts, proj, *shards)
    if not gather:
        got = list(shards[:3]) + list(got)
    return got[:6], got[6:]


def dec_kernel(dp, *refs):
    it = iter(refs)
    take = lambda n: [next(it) for _ in range(n)]
    res, chosen_row, chosen_col, low_all, table, cot, gains, shifts, token, wd, we, wf = take(12)
    out, glow, gd, ge, gf, small = take(6)
    ss, rs = take(2)
    (n1, n2, gm, gmid_low, qg, kg, vg, gg, vtx, kt, ct, dqt, lse, acc_s, top_s, ctx, active, slope) = take(18)
    (dkv, mid_s, start_s, res_s, part, stage, recv, fstage, frecv, far, prod, pstage, precv, masks) = take(14)
    cx = Ctx(ss, rs, dp)
    cx.barrier([cx.core, cx.y, cx.x])
    rows, width = n1.shape[1:]
    m, lo, hi, s = cx.m, cx.lo, cx.hi, cx.s
    big = res[s] == 1
    shown = jnp.where(big, VIS, VIS_SMALL)
    filled = jnp.where(big, PATCHES, SMALL_PATCHES)
    pos_col = iota((rows, 1), 0) + m * rows
    live = jnp.where(pos_col < filled, 1.0, 0.0)
    gm[lo] = (cot[s].astype(f32) * live).astype(bf)
    cgm = cx.send(gm.at[lo], gm.at[lo], cx.core)
    vis = chosen_row.shape[-1]
    place = jnp.where((pos_col == chosen_row[s]) & (iota((1, vis), 1) < shown), 1.0, 0.0)
    seen = jnp.sum(place, axis=1, keepdims=True)
    weight = live - seen
    placed = nn(place.astype(bf), low_all[...].reshape(vis, width))
    half = width // 2
    nb, ns = rows // COLS_BIG, rows // COLS_SMALL
    rb = table[pl.ds(pl.multiple_of(m * nb, 8), nb), :]
    rsm = table[pl.ds(pl.multiple_of(m * ns, 8), ns), :]
    big_rows = jnp.broadcast_to(rb[:, None, :], (nb, COLS_BIG, half)).reshape(rows, half)
    small_rows = jnp.broadcast_to(rsm[:, None, :], (ns, COLS_SMALL, half)).reshape(rows, half)
    big_cols = jnp.broadcast_to(table[0:COLS_BIG, :][None], (nb, COLS_BIG, half)).reshape(rows, half)
    small_cols = jnp.broadcast_to(table[0:COLS_SMALL, :][None], (ns, COLS_SMALL, half)).reshape(rows, half)
    base = placed + weight * token[...]
    start_s[:, :half] = base[:, :half] + live * jnp.where(big, big_rows, small_rows)
    start_s[:, half:] = base[:, half:] + live * jnp.where(big, big_cols, small_cols)
    n1[m] = normalize(start_s[...], gains[0:1, :], shifts[0:1, :]).astype(bf)
    g1 = GatherMp(cx, n1)

    lane = iota((1, 256), 1)
    for j in range(4):
        head_lane = (lane < 128) & (lane // 32 == j)
        off = lane - (128 + 8 * j)
        masks[0, j] = jnp.where(head_lane | ((off >= 0) & (off < 3)) | (lane == 160), 1.0, 0.0).astype(bf)
        masks[1, j] = jnp.where(head_lane | ((off >= 0) & (off < 2)), 1.0, 0.0).astype(bf)
    aug = iota((1, 128), 1)
    total = 4 * rows
    key_bias = jnp.where(iota((total, 1), 0) < filled, 0.0, NEG)
    kaug = jnp.where(aug == 32, key_bias, jnp.where(aug < 32, 1.0, 0.0)).astype(bf)
    vaug = jnp.broadcast_to(jnp.where(aug < 32, 1.0, 0.0), (total, 128)).astype(bf)
    qaug = jnp.broadcast_to(jnp.where(aug == 32, 1.0, 0.0), (2 * rows, 128)).astype(bf)
    for g in range(2):
        kg[g, :, 128:] = kaug
        vg[g, :, 128:] = vaug
        qg[g, :, 128:] = qaug
    vtx[:, 32:, :] = jnp.ones((8, 16, total), bf)
    lse[...] = jnp.zeros_like(lse)

    def keys_values(i):
        at = pl.ds(pl.multiple_of(i * rows, 128), rows)
        for g in range(2):
            kv = nn(n1[i], wd[g, :, 128:384])
            kg[g, at, :128] = kv[:, :128].astype(bf)
            vg[g, at, :128] = kv[:, 128:].astype(bf)
            kvt = kv.T.astype(bf)
            for j in range(4):
                kt[4 * g + j, :, at] = kvt[32 * j : 32 * j + 32]
                vtx[4 * g + j, 0:32, at] = kvt[128 + 32 * j : 160 + 32 * j]

    g1.near()
    for r in range(2):
        for g in range(2):
            qg[g, r * rows : (r + 1) * rows, :128] = nn(n1[2 * hi + r], wd[g, :, :128]).astype(bf)
    keys_values(cx.m)
    keys_values(cx.m1)
    c2 = HD_DEC**-0.5 * LOG2E

    def head_pass(first, last, blocks):
        def body(h, _):
            g, j = h // 4, lax.rem(h, 4)
            if first:
                top, acc = None, None
            else:
                top, acc = top_s[h], acc_s[h]
            for i in blocks:
                at = pl.ds(pl.multiple_of(i * rows, 128), rows)
                sc = nt(kg[g, at, :] * masks[0, j], qg[g])
                mj = jnp.max(sc, axis=0, keepdims=True)
                new = mj if top is None else jnp.maximum(top, mj)
                p = jnp.exp2((sc - new) * c2).astype(bf)
                o = nn(vtx[h, :, at], p)
                acc = o if acc is None else acc * jnp.exp2((top - new) * c2) + o
                top = new
            if last:
                tot = acc[32:33, :]
                ct[h] = acc[:32, :] / tot
                at = pl.ds(pl.multiple_of(8 * j, 8), 8)
                lse[g, at, :] = jnp.broadcast_to(top + jnp.log(tot) * (LOG2E / c2), (8, top.shape[1]))
            else:
                top_s[h] = top
                acc_s[h] = acc
            return 0

        lax.fori_loop(0, 8, body, 0)

    head_pass(True, False, (cx.m, cx.m1))
    g1.forward()
    keys_values(cx.m2)
    g1.far()
    keys_values(cx.m3)
    head_pass(False, True, (cx.m2, cx.m3))
    for g in range(2):
        ctx[:, 128 * g : 128 * g + 128] = ct[4 * g : 4 * g + 4].reshape(128, 2 * rows).T.astype(bf)

    def reduce_core(slot, compute):
        fstage[slot] = compute(1 - lo).astype(bf)
        c = cx.send(fstage.at[slot], frecv.at[slot], cx.core)
        own = compute(lo)
        c.wait_recv()
        return own + frecv[slot].astype(f32)

    def chip_rows(r):
        return pl.ds(pl.multiple_of(r * rows, 128), rows)

    def out_rows(r):
        return sum(nt(ctx[chip_rows(r), 128 * g : 128 * g + 128], wd[g, :, 384:]) for g in range(2))

    mid = start_s[...] + reduce_core(0, out_rows)
    mid_s[...] = mid
    n2[lo] = normalize(mid, gains[1:2, :], shifts[1:2, :]).astype(bf)
    cn2 = cx.send(n2.at[lo], n2.at[lo], cx.core)

    def mlp_rows(r):
        at = chip_rows(r)
        x = n2[r]
        y = None
        for g in range(2):
            a, b = gelu_and_slope(nn(x, we[g]))
            cols = slice(width * g, width * (g + 1))
            a = a.astype(bf)
            active[at, cols] = a
            slope[at, cols] = b.astype(bf)
            t = nt(a, wf[g])
            y = t if y is None else y + t
        return y

    res_s[...] = mlp_rows(lo)
    cn2.wait_recv()
    fstage[1] = mlp_rows(1 - lo).astype(bf)
    c = cx.send(fstage.at[1], frecv.at[1], cx.core)

    cgm.wait_recv()

    def mlp_back_rows(r):
        at = chip_rows(r)
        y = None
        for g in range(2):
            cols = slice(width * g, width * (g + 1))
            ga = nn(gm[r], wf[g])
            gh = (ga * slope[at, cols].astype(f32)).astype(bf)
            slope[at, cols] = gh
            t = nt(gh, we[g])
            y = t if y is None else y + t
        return y

    fstage[2] = mlp_back_rows(1 - lo).astype(bf)
    cb = cx.send(fstage.at[2], frecv.at[2], cx.core)
    c.wait_recv()
    result = mid_s[...] + res_s[...] + frecv[1].astype(f32)
    produced = (result * live).astype(bf)
    prod[0] = produced[:, :half]
    prod[1] = produced[:, half:]
    out[s] = prod[s]
    cprod = cx.send(prod.at[1 - s], out.at[s], cx.x)
    own = mlp_back_rows(lo)
    gm_all = gm[...].reshape(2 * rows, width)
    for g in range(2):
        cols = slice(width * g, width * (g + 1))
        gf[g] = tn(gm_all, active[:, cols])
    cb.wait_recv()
    grad_mid, gain_mid, shift_mid = normalize_back(mid_s[...], gains[1:2, :], own + frecv[2].astype(f32))
    gmid = gm[lo].astype(f32) + grad_mid
    mid_s[...] = gmid
    gmid_low[lo] = gmid.astype(bf)
    cgmid = cx.send(gmid_low.at[lo], gmid_low.at[lo], cx.core)
    n2_all = n2[...].reshape(2 * rows, width)
    for g in range(2):
        cols = slice(width * g, width * (g + 1))
        ge[g] = tn(n2_all, slope[:, cols])
    cgmid.wait_recv()
    gmid_all = gmid_low[...].reshape(2 * rows, width)
    sel = jnp.where(iota((128, 128), 0) // 32 == iota((128, 128), 1) // 8, 1.0, 0.0).astype(bf)
    lane128 = iota((1, 128), 1)
    t8 = lax.rem(lane128, 8)
    for g in range(2):
        gcg = nn(gmid_all, wd[g, :, 384:]).astype(bf)
        gg[g, :, :128] = gcg
        prodd = gcg.astype(f32) * ctx[:, 128 * g : 128 * g + 128].astype(f32)
        ph = prodd.astype(bf)
        plow = (prodd - ph.astype(f32)).astype(bf)
        delta = nn(ph, sel) + nn(plow, sel)
        dh = delta.astype(bf).astype(f32)
        daug = jnp.where(t8 == 0, -dh, jnp.where(t8 == 1, dh - delta, 0.0))
        gg[g, :, 128:] = jnp.where(lane128 < 32, daug, 0.0).astype(bf)
        gd[g, :, 384:] = tn(gmid_all, ctx[:, 128 * g : 128 * g + 128])
        lt = lse[g].T
        h1 = lt.astype(bf).astype(f32)
        h2 = (lt - h1).astype(bf).astype(f32)
        h3 = lt - h1 - h2
        laug = jnp.where(t8 == 0, -h1, jnp.where(t8 == 1, -h2, jnp.where(t8 == 2, -h3, 0.0)))
        laug = jnp.where(lane128 == 32, 1.0, jnp.where(lane128 < 32, laug, 0.0))
        qg[g, :, 128:] = laug.astype(bf)

    scale = HD_DEC**-0.5
    dqt[...] = jnp.zeros_like(dqt)
    head_lane = lane128 // 32

    def back_pass(blocks):
        def body(h, _):
            g, j = h // 4, lax.rem(h, 4)
            mine = head_lane == j
            for i in blocks:
                at = pl.ds(pl.multiple_of(i * rows, 128), rows)
                st = nt(kg[g, at, :] * masks[0, j], qg[g])
                dpt = nt(vg[g, at, :] * masks[1, j], gg[g])
                p = jnp.exp2(st * c2)
                ds = (p * dpt).astype(bf)
                dv = nn(p.astype(bf), gg[g, :, :128])
                dk = nn(ds, qg[g, :, :128]) * scale
                dkv[g, at, :128] = jnp.where(mine, dk, dkv[g, at, :128].astype(f32)).astype(bf)
                dkv[g, at, 128:] = jnp.where(mine, dv, dkv[g, at, 128:].astype(f32)).astype(bf)
                dqt[h] += nn(kt[h, :, at], ds)
            return 0

        lax.fori_loop(0, 8, body, 0)

    dkv[...] = jnp.zeros_like(dkv)
    back_pass((cx.m2, cx.m3))

    def far_rows(r):
        at = pl.ds(pl.multiple_of((2 * (1 - hi) + r) * rows, 128), rows)
        return sum(nt(dkv[g, at, :], wd[g, :, 128:384]) for g in range(2))

    far[0] = reduce_core(3, far_rows).astype(bf)
    cfar = cx.send(far.at[0], far.at[1], cx.y)
    back_pass((cx.m, cx.m1))
    for g in range(2):
        ctx[:, 128 * g : 128 * g + 128] = (dqt[4 * g : 4 * g + 4].reshape(128, 2 * rows).T * scale).astype(bf)

    def near_rows(r):
        at = pl.ds(pl.multiple_of((2 * hi + r) * rows, 128), rows)
        return sum(
            nt(ctx[chip_rows(r), 128 * g : 128 * g + 128], wd[g, :, :128]) + nt(dkv[g, at, :], wd[g, :, 128:384])
            for g in range(2)
        )

    near = reduce_core(4, near_rows)
    cfar.wait_recv()
    grad_in, gain_in, shift_in = normalize_back(start_s[...], gains[0:1, :], near + far[1].astype(f32))
    gstart = (mid_s[...] + grad_in).astype(bf)
    token_term = jnp.sum(weight * gstart.astype(f32), axis=0, keepdims=True)
    small[0:1] = gain_in
    small[1:2] = gain_mid
    small[2:3] = shift_in
    small[3:4] = shift_mid
    small[4:5] = token_term
    small[5:8] = jnp.zeros((3, width), f32)
    pos_row = iota((1, rows), 1) + m * rows
    place_t = jnp.where((chosen_col[s] == pos_row) & (iota((vis, 1), 0) < shown), 1.0, 0.0).astype(bf)
    part[...] = nn(place_t, gstart).reshape(part.shape)
    n1_chip = n1[pl.ds(2 * hi, 2)].reshape(2 * rows, width)
    for g in range(2):
        gd[g, :, :128] = tn(n1_chip, ctx[:, 128 * g : 128 * g + 128])
        gd[g, :, 128:384] = tn(n1[...].reshape(total, width), dkv[g])
    glow[...] = reduce_mp(cx, part, pstage, precv).astype(bf)
    cprod.wait_recv()
    cx.drain()


def decoder(dp, res, chosen_row, chosen_col, low_all, table, cot, gains, shifts, token, wd, we, wf):
    rows, width = cot.shape[1:]
    vis = chosen_row.shape[-1]
    total, chip = 4 * rows, 2 * rows
    outs = [
        sds((2, rows, width // 2), bf),
        sds((vis // 4, width), bf),
        sds(wd.shape, f32),
        sds(we.shape, f32),
        sds(wf.shape, f32),
        sds((8, width), f32),
    ]
    V = pltpu.VMEM
    return pl.pallas_call(
        functools.partial(dec_kernel, dp),
        out_shape=outs,
        in_specs=[SMEM] + vm(11),
        out_specs=vm(len(outs)),
        scratch_shapes=[
            pltpu.SemaphoreType.DMA((32,)),
            pltpu.SemaphoreType.DMA((32,)),
            V((4, rows, width), bf),
            V((2, rows, width), bf),
            V((2, rows, width), bf),
            V((2, rows, width), bf),
            V((2, chip, 256), bf),
            V((2, total, 256), bf),
            V((2, total, 256), bf),
            V((2, chip, 256), bf),
            V((8, 48, total), bf),
            V((8, 32, total), bf),
            V((8, 32, chip), f32),
            V((8, 32, chip), f32),
            V((2, 128, chip), f32),
            V((8, 48, chip), f32),
            V((8, 1, chip), f32),
            V((chip, 256), bf),
            V((chip, 2 * width), bf),
            V((chip, 2 * width), bf),
            V((2, total, 256), bf),
            V((rows, width), f32),
            V((rows, width), f32),
            V((rows, width), f32),
            V((4, vis // 4, width), f32),
            V((1,), f32) if False else V((8, 128), f32),
            V((8, 128), f32),
            V((5, rows, width), bf),
            V((5, rows, width), bf),
            V((2, rows, width), bf),
            V((2, rows, width // 2), bf),
            V((3, vis // 4, width), bf),
            V((3, vis // 4, width), bf),
            V((2, 4, 1, 256), bf),
        ],
        compiler_params=params(2),
        name="decoder",
    )(res, chosen_row, chosen_col, low_all, table, cot, gains, shifts, token, wd, we, wf)


def enc_backward_kernel(dp, gather, *refs):
    it = iter(refs)
    take = lambda n: [next(it) for _ in range(n)]
    res, x_all, gains, proj, wa, wb, wc, n1, n2, qkv, ctx, slope, active, mid, top, glow, dd, de, df, dsmall = take(20)
    gin, out_a, out_b, out_c, out_d, out_e, out_f, small, pout = take(9)
    ss, rs, gm, gmid_low, gqkv, part, stage, recv, gbuf, yst, yrc = take(11)
    if gather:
        exs, exr, ezs, ezr, dxs, dxr, dzs, dzr, ga, gb, gc, smr, smz, pst, prc, pz, pacc = take(17)
    else:
        (gmid_half,) = take(1)
        ga, gb, gc = out_a, out_b, out_c
    if gather:
        (gmid_half,) = take(1)
    cx = Ctx(ss, rs, dp)
    peers = [cx.core, cx.y, cx.x]
    if gather:
        peers += [cx.z(k) for k in range(1, dp)]
    cx.barrier(peers)
    m, s = cx.m, cx.s
    rows, width = n1.shape[1:]
    total = 4 * rows
    g_top = nt(glow[...], proj[...])
    gm[m] = g_top.astype(bf)
    g1 = GatherMp(cx, gm)
    ys = []
    for i, src in enumerate((df, de, dd)):
        yst[i] = src[1].astype(bf)
        ys.append(cx.send(yst.at[i], yrc.at[i], cx.y))
    g1.finish()
    gm_all = gm[...].reshape(total, width)
    gact = nn(gm_all, wc[...])
    gh = (gact * slope[...].astype(f32)).astype(bf)
    part[...] = nt(gh, wb[...]).reshape(part.shape)
    gb[...] = tn(n2[...].reshape(total, width), gh)
    gc[...] = tn(gm_all, active[...])
    g_n2 = reduce_mp(cx, part, stage.at[0], recv.at[0])
    grad_mid, gain_mid, shift_mid = normalize_back(mid[...], gains[1:2, :], g_n2)
    gmid = g_top + grad_mid
    gmid_half[...] = gmid
    gmid_low[m] = gmid.astype(bf)
    g2 = GatherMp(cx, gmid_low)
    sc = []
    if gather:
        er, dr = x_rows(wa, dp), x_rows(wd_shape(dd), dp)
        sb = ScatterW(cx, er, out_b, exs.at[0], exr.at[0], ezs.at[0], ezr.at[0])
        sb.start(gb)
        scc = ScatterW(cx, er, out_c, exs.at[1], exr.at[1], ezs.at[1], ezr.at[1])
        scc.start(gc)
    dsum = []
    for i, src in enumerate((df, de, dd)):
        ys[i].wait_recv()
        gbuf[i] = src[0] + yrc[i].astype(f32)
        if gather:
            o = (out_f, out_e, out_d)[i]
            q = ScatterW(cx, dr, o, dxs.at[i], dxr.at[i], dzs.at[i], dzr.at[i])
            q.start(gbuf.at[i])
            dsum.append(q)
        else:
            (out_f, out_e, out_d)[i][...] = gbuf[i]
    p_part = tn(top[...], glow[...])
    if gather:
        pr = ProjSum(cx, pst, prc, pz, pacc, pout)
        pr.core(p_part)
    else:
        pout[...] = p_part
    g2.finish()
    gmid_all = gmid_low[...].reshape(total, width)
    cpad = ctx.shape[1]
    gcx = nn(gmid_all, wa[:, width - cpad :]).astype(bf)
    shown = jnp.where(res[s] == 1, VIS, VIS_SMALL)
    bias = jnp.where(iota((1, total), 1) < shown, 0.0, NEG)
    scale = HD_ENC**-0.5
    scale2 = scale * LOG2E
    heads = (width // 4) // HD_ENC
    for h in range(heads):
        q = qkv[:, h * HD_ENC : (h + 1) * HD_ENC]
        k = qkv[:, (heads + h) * HD_ENC : (heads + h + 1) * HD_ENC]
        v = qkv[:, (2 * heads + h) * HD_ENC : (2 * heads + h + 1) * HD_ENC]
        go = gcx[:, (h + 1) * HD_ENC : (h + 2) * HD_ENC]
        co = ctx[:, (h + 1) * HD_ENC : (h + 2) * HD_ENC]
        scr = nt(q, k) + bias
        e = jnp.exp2((scr - jnp.max(scr, axis=1, keepdims=True)) * scale2)
        p = e / jnp.sum(e, axis=1, keepdims=True)
        delta = jnp.sum(go.astype(f32) * co.astype(f32), axis=1, keepdims=True)
        gs = (p * (nt(go, v) - delta) * scale).astype(bf)
        gqkv[:, h * HD_ENC : (h + 1) * HD_ENC] = nn(gs, k).astype(bf)
        gqkv[:, (heads + h) * HD_ENC : (heads + h + 1) * HD_ENC] = tn(gs, q).astype(bf)
        gqkv[:, (2 * heads + h) * HD_ENC : (2 * heads + h + 1) * HD_ENC] = tn(p.astype(bf), go).astype(bf)
        if gather and h == 0:
            sb.middle()
            pr.y()
        if gather and h == 1:
            scc.middle()
    gqkv[:, 3 * heads * HD_ENC :] = jnp.zeros((total, width - 3 * heads * HD_ENC), bf)
    part[...] = nt(gqkv[...], wa[...]).reshape(part.shape)
    n1_all = n1[...].reshape(total, width)
    cut = width - cpad
    ga[:, :cut] = tn(n1_all, gqkv[:, :cut])
    ga[:, cut:] = tn(n1_all, gqkv[:, cut:]) + tn(gmid_all, ctx[...])
    if gather:
        sa = ScatterW(cx, er, out_a, exs.at[2], exr.at[2], ezs.at[2], ezr.at[2])
        sa.start(ga)
    g_n1 = reduce_mp(cx, part, stage.at[1], recv.at[1])
    stream = x_all[s].astype(f32)
    grad_in, gain_in, shift_in = normalize_back(stream, gains[0:1, :], g_n1)
    grad = gmid_half[...] + grad_in
    half = width // 2
    part[0, :, :half] = grad[:, :half]
    part[1, :, :half] = grad[:, half:]
    gin[s] = part[s, :, :half]
    cin = cx.send(part.at[1 - s, :, pl.ds(0, half)], gin.at[s], cx.x)
    dw = dsmall.shape[1]
    vec = jnp.concatenate(
        [
            gain_in,
            gain_mid,
            shift_in,
            shift_mid,
            jnp.zeros((4, width), f32),
            jnp.concatenate([dsmall[...], jnp.zeros((8, width - dw), f32)], axis=1),
        ],
        axis=0,
    )
    if gather:
        smr[0] = vec
        c = cx.send(smr.at[0], smr.at[1], cx.core)
        pr.x()
        for q in dsum:
            q.middle()
        c.wait_recv()
        smr[2] = smr[0] + smr[1]
        c = cx.send(smr.at[2], smr.at[3], cx.y)
        sa.middle()
        c.wait_recv()
        smr[4] = smr[2] + smr[3]
        c = cx.send(smr.at[4], smr.at[5], cx.x)
        pr.z()
        c.wait_recv()
        smz[cx.d] = smr[4] + smr[5]
        cs = [cx.send(smz.at[cx.d], smz.at[cx.d], cx.z(k)) for k in range(1, dp)]
        pr.back_x()
        sb.finish()
        scc.finish()
        pr.back_y()
        for q in dsum:
            q.finish()
        for c in cs:
            c.wait_recv()
        small[...] = sum_in_order(smz, dp)
        pr.back_core()
        sa.finish()
        pr.finish()
    else:
        small[...] = vec
    cin.wait_recv()
    cx.drain()


def sum_in_order(ref, n):
    out = ref[0]
    for i in range(1, n):
        out = out + ref[i]
    return out


def x_rows(w, dp):
    return w.shape[0] // (2 * dp)


class wd_shape:
    def __init__(self, ref):
        self.shape = ref.shape[1:]


class ProjSum:
    def __init__(self, cx, st, rc, zb, acc, out):
        self.cx, self.st, self.rc, self.zb, self.acc, self.out = cx, st, rc, zb, acc, out
        self.R = out.shape[0]

    def rows(self, start, size):
        return pl.ds(pl.multiple_of(start, 16), size)

    def core(self, part):
        cx, R = self.cx, self.R
        h = R // 2
        self.acc[...] = part
        self.o1 = cx.lo * h
        self.st[0:h] = self.acc[self.rows((1 - cx.lo) * h, h), :].astype(bf)
        self.c = cx.send(self.st.at[pl.ds(0, h)], self.rc.at[pl.ds(0, h)], cx.core)

    def step(self, prev_at, prev_size, base, bit, dev):
        cx, R = self.cx, self.R
        self.c.wait_recv()
        off = R - 2 * prev_size
        mine = self.rows(prev_at, prev_size)
        self.acc[mine, :] = self.acc[mine, :] + self.rc[off : off + prev_size, :].astype(f32)
        h = prev_size // 2
        noff = R - 2 * h
        self.st[noff : noff + h] = self.acc[self.rows(prev_at + (1 - bit) * h, h), :].astype(bf)
        self.c = cx.send(self.st.at[pl.ds(noff, h)], self.rc.at[pl.ds(noff, h)], dev)
        return prev_at + bit * h

    def y(self):
        self.o2 = self.step(self.o1, self.R // 2, 0, self.cx.hi, self.cx.y)

    def x(self):
        self.o3 = self.step(self.o2, self.R // 4, 0, self.cx.s, self.cx.x)

    def z(self):
        cx, R = self.cx, self.R
        size = R // 8
        self.c.wait_recv()
        off = R - 2 * size
        self.zb[cx.d] = self.acc[self.rows(self.o3, size), :] + self.rc[off : off + size, :].astype(f32)
        self.cs = [cx.send(self.zb.at[cx.d], self.zb.at[cx.d], cx.z(k)) for k in range(1, cx.dp)]

    def back_x(self):
        cx, R = self.cx, self.R
        for c in self.cs:
            c.wait_recv()
        at = self.rows(self.o3, R // 8)
        self.out[at, :] = sum_in_order(self.zb, cx.dp)
        self.c = cx.send(self.out.at[at], self.out.at[at], cx.x)

    def back_y(self):
        self.c.wait_recv()
        at = self.rows(self.o2, self.R // 4)
        self.c = self.cx.send(self.out.at[at], self.out.at[at], self.cx.y)

    def back_core(self):
        self.c.wait_recv()
        at = self.rows(self.o1, self.R // 2)
        self.c = self.cx.send(self.out.at[at], self.out.at[at], self.cx.core)

    def finish(self):
        self.c.wait_recv()


def enc_backward(dp, gather, res, x, gains, proj, weights, saved, glow, dgrads, dsmall):
    wa, wb, wc = weights
    n1, n2, qkv, ctx, slope, active, mid, top = saved
    rows, width = x.shape[1:]
    total = 4 * rows
    V = pltpu.VMEM
    dd = dgrads[0].shape
    if gather:
        er, dr = wa.shape[0] // (2 * dp), dd[1] // (2 * dp)
    else:
        er, dr = wa.shape[0], dd[1]
    outs = [sds((2, rows, width // 2), f32)]
    outs += [sds((er, w.shape[1]), f32) for w in weights]
    outs += [sds((dr, dd[2]), f32)] * 3
    outs += [sds((16, width), f32), sds(proj.shape, f32)]
    slots = (4, rows, width)
    scratch = [
        pltpu.SemaphoreType.DMA((96,)),
        pltpu.SemaphoreType.DMA((96,)),
        V(slots, bf),
        V(slots, bf),
        V((total, width), bf),
        V(slots, f32),
        V((2, 3, rows, width), bf),
        V((2, 3, rows, width), bf),
        V((3,) + dd[1:], f32),
        V((3,) + dd[1:], bf),
        V((3,) + dd[1:], bf),
    ]
    if gather:
        cols = wa.shape[1]
        scratch += [
            V((3, dp * er, cols), bf),
            V((3, dp * er, cols), bf),
            V((3, dp * er, cols), bf),
            V((3, dp - 1, er, cols), bf),
            V((3, dp * dr, dd[2]), bf),
            V((3, dp * dr, dd[2]), bf),
            V((3, dp * dr, dd[2]), bf),
            V((3, dp - 1, dr, dd[2]), bf),
            V(wa.shape, f32),
            V(wb.shape, f32),
            V(wc.shape, f32),
            V((6, 16, width), f32),
            V((dp, 16, width), f32),
            V(proj.shape, bf),
            V(proj.shape, bf),
            V((dp, proj.shape[0] // 8, proj.shape[1]), f32),
            V(proj.shape, f32),
        ]
    scratch += [V((rows, width), f32)]
    return pl.pallas_call(
        functools.partial(enc_backward_kernel, dp, gather),
        out_shape=outs,
        in_specs=[SMEM] + vm(19),
        out_specs=vm(len(outs)),
        scratch_shapes=scratch,
        compiler_params=params(3),
        name="enc_backward",
    )(res, x, gains, proj, wa, wb, wc, n1, n2, qkv, ctx, slope, active, mid, top, glow, *dgrads, dsmall)


def position_table(count, quarter):
    freq = (np.float32(10000.0) ** (-np.arange(quarter, dtype=np.float32) / np.float32(quarter))).astype(np.float32)
    angle = (np.arange(count, dtype=np.float32)[:, None] * freq[None, :]).astype(np.float32).astype(np.float64)
    return np.concatenate([np.sin(angle), np.cos(angle)], axis=1).astype(np.float32)


def per_device(
    x_visible,
    resolution,
    visible_index,
    enc_qkv_w,
    enc_out_w,
    enc_up_w,
    enc_down_w,
    enc_gains,
    enc_shifts,
    projection,
    mask_token,
    dec_qkv_w,
    dec_out_w,
    dec_up_w,
    dec_down_w,
    dec_gains,
    dec_shifts,
    cotangent,
):
    dp = lax.axis_size("dp")
    over = ("section", "dp")
    er, dr = enc_qkv_w.shape[0], dec_qkv_w.shape[0]
    de, dd = projection.shape
    ec, dc = enc_qkv_w.shape[2], dec_qkv_w.shape[2]
    gather = er % 16 == 0 and dr % 16 == 0
    shards = [
        jnp.concatenate([enc_qkv_w.reshape(er, 3 * ec), enc_out_w.T], axis=1),
        enc_up_w,
        enc_down_w.T,
        jnp.concatenate([dec_qkv_w.reshape(dr, 3 * dc), dec_out_w.T], axis=1),
        dec_up_w,
        dec_down_w.T,
    ]
    if not gather:
        shards = [lax.all_gather(w, over, axis=0, tiled=True) for w in shards]
    weights, saved = enc_forward(
        dp, gather, resolution, x_visible, enc_gains, enc_shifts, projection, shards, de, dd
    )
    table = jnp.asarray(position_table(COLS_BIG, dd // 4))
    out, glow, gd, ge, gf, dsmall = decoder(
        dp,
        resolution,
        visible_index[:, None, :],
        visible_index[:, :, None],
        saved[8],
        table,
        cotangent,
        dec_gains,
        dec_shifts,
        mask_token[None, :],
        *weights[3:],
    )
    gin, ga, gb, gc, hd, he, hf, small, pgrad = enc_backward(
        dp,
        gather,
        resolution,
        x_visible,
        enc_gains,
        projection,
        weights[:3],
        saved[:8],
        glow,
        (gd, ge, gf),
        dsmall,
    )
    if not gather:
        ga, gb, gc, hd, he, hf = [
            lax.psum_scatter(g, over, scatter_dimension=0, tiled=True) for g in (ga, gb, gc, hd, he, hf)
        ]
        small, pgrad = lax.psum((small, pgrad), ("section", "dp", "mp"))
    return (
        out,
        gin,
        ga[:, : 3 * ec].reshape(er, 3, ec),
        ga[:, 3 * ec :].T,
        gb,
        gc.T,
        small[0:2],
        small[2:4],
        pgrad,
        small[12, :dd],
        hd[:, : 3 * dc].reshape(dr, 3, dc),
        hd[:, 3 * dc :].T,
        he,
        hf.T,
        small[8:10, :dd],
        small[10:12, :dd],
    )


def solution(mesh):
    matrix_in = P(("section", "dp"), "mp")
    matrix_out = P("mp", ("section", "dp"))
    qkv = P(("section", "dp"), None, "mp")
    return jax.shard_map(
        per_device,
        mesh=mesh,
        in_specs=(
            P("dp", "mp", None),
            P("dp"),
            P("dp", None),
            qkv,
            matrix_out,
            matrix_in,
            matrix_out,
            P(),
            P(),
            P(),
            P(),
            qkv,
            matrix_out,
            matrix_in,
            matrix_out,
            P(),
            P(),
            P("dp", "mp", None),
        ),
        out_specs=(
            P("dp", "mp", "section"),
            P("dp", "mp", "section"),
            qkv,
            matrix_out,
            matrix_in,
            matrix_out,
            P(),
            P(),
            P(),
            P(),
            qkv,
            matrix_out,
            matrix_in,
            matrix_out,
            P(),
            P(),
        ),
        check_vma=False,
    )
```

```python
import functools
import math

import jax
import jax.numpy as jnp
import numpy as np
from jax import lax
from jax.experimental import pallas as pl
from jax.experimental.pallas import tpu as pltpu
from jax.sharding import PartitionSpec as P

HD_ENC = 64
HD_DEC = 32
COLS_SMALL = 32
COLS_BIG = 64
PATCHES = 2048
SMALL_PATCHES = 512
VIS = 512
VIS_SMALL = 128

MESH = pl.DeviceIdType.MESH
bf = jnp.bfloat16
f32 = jnp.float32
LOG2E = 1.4426950408889634
NEG = -1e30


def nn(a, b):
    return lax.dot_general(a, b, (((1,), (0,)), ((), ())), preferred_element_type=f32)


def nt(a, b):
    return lax.dot_general(a, b, (((1,), (1,)), ((), ())), preferred_element_type=f32)


def tn(a, b):
    return lax.dot_general(a, b, (((0,), (0,)), ((), ())), preferred_element_type=f32)


def norm_stats(stream):
    centre = stream - jnp.mean(stream, axis=-1, keepdims=True)
    inverse = lax.rsqrt(jnp.mean(centre * centre, axis=-1, keepdims=True) + 1e-06)
    return centre * inverse, inverse


def normalize(stream, gain, shift):
    scaled, _ = norm_stats(stream)
    return scaled * gain + shift


def normalize_back(stream, gain, grad_out):
    scaled, inverse = norm_stats(stream)
    f = grad_out * gain
    grad_in = inverse * (
        f
        - jnp.mean(f, axis=-1, keepdims=True)
        - scaled * jnp.mean(f * scaled, axis=-1, keepdims=True)
    )
    return (
        grad_in,
        jnp.sum(grad_out * scaled, axis=0, keepdims=True),
        jnp.sum(grad_out, axis=0, keepdims=True),
    )


def gelu_and_slope(a):
    x = jnp.abs(a) * 0.7071067811865476
    t = 1.0 / (1.0 + 0.3275911 * x)
    e = jnp.exp2(x * x * (-LOG2E))
    poly = ((((1.061405429 * t - 1.453152027) * t + 1.421413741) * t - 0.284496736) * t + 0.254829592) * t
    tail = 0.5 * poly * e
    phi = jnp.where(a >= 0, 1.0 - tail, tail)
    return a * phi, phi + a * e * 0.3989422804014327


class Ctx:
    def __init__(self, ss, rs, dp):
        self.ss, self.rs, self.n, self.dp = ss, rs, 0, dp
        self.s = lax.axis_index("section")
        self.d = lax.axis_index("dp")
        self.m = lax.axis_index("mp")
        m = self.m
        self.lo = lax.rem(m, 2)
        self.hi = m // 2
        self.m1 = m + 1 - 2 * self.lo
        self.m2 = lax.rem(m + 2, 4)
        self.m3 = lax.rem(self.m1 + 2, 4)
        self.core = {"mp": self.m1}
        self.y = {"mp": self.m2}
        self.x = {"section": 1 - self.s}
        self.pending = []

    def z(self, k):
        return {"dp": lax.rem(self.d + k, self.dp)}

    def barrier(self, peers):
        b = pltpu.get_barrier_semaphore()
        for p in peers:
            pl.semaphore_signal(b, inc=1, device_id=p, device_id_type=MESH)
        pl.semaphore_wait(b, len(peers))

    def send(self, src, dst, dev):
        i = self.n
        self.n += 1
        c = pltpu.make_async_remote_copy(
            src_ref=src,
            dst_ref=dst,
            send_sem=self.ss.at[i],
            recv_sem=self.rs.at[i],
            device_id=dev,
            device_id_type=MESH,
        )
        c.start()
        self.pending.append(c)
        return c

    def drain(self):
        for c in self.pending:
            c.wait_send()
        self.pending = []


class GatherMp:
    def __init__(self, cx, buf):
        self.cx, self.buf = cx, buf
        m = cx.m
        self.c2 = cx.send(buf.at[m], buf.at[m], cx.y)
        self.c1 = cx.send(buf.at[m], buf.at[m], cx.core)

    def forward(self):
        cx, buf = self.cx, self.buf
        self.c2.wait_recv()
        self.c3 = cx.send(buf.at[cx.m2], buf.at[cx.m2], cx.core)

    def near(self):
        self.c1.wait_recv()

    def far(self):
        self.c3.wait_recv()

    def finish(self):
        self.forward()
        self.near()
        self.far()


class ReduceMp:
    def __init__(self, cx, part, stage, recv):
        self.cx, self.part, self.stage, self.recv = cx, part, stage, recv
        stage[0] = part[cx.m3].astype(bf)
        self.c3 = cx.send(stage.at[0], recv.at[0], cx.core)
        stage[1] = part[cx.m1].astype(bf)
        self.c1 = cx.send(stage.at[1], recv.at[1], cx.core)

    def middle(self):
        cx = self.cx
        self.c3.wait_recv()
        self.stage[2] = (self.part[cx.m2] + self.recv[0].astype(f32)).astype(bf)
        self.c2 = cx.send(self.stage.at[2], self.recv.at[2], cx.y)

    def finish(self):
        self.c1.wait_recv()
        own = self.part[self.cx.m] + self.recv[1].astype(f32)
        self.c2.wait_recv()
        return own + self.recv[2].astype(f32)


def reduce_mp(cx, part, stage, recv):
    r = ReduceMp(cx, part, stage, recv)
    r.middle()
    return r.finish()


class GatherW:
    def __init__(self, cx, shard, whole):
        self.cx, self.whole, self.rows = cx, whole, shard.shape[0]
        own = self.at(cx.s, cx.d)
        self.zs = [cx.send(shard, own, cx.z(k)) for k in range(1, cx.dp)]
        self.xs = [cx.send(shard, own, cx.x)]
        own[...] = shard[...]

    def at(self, s, d):
        start = (s * self.cx.dp + d) * self.rows
        return self.whole.at[pl.ds(pl.multiple_of(start, 16), self.rows)]

    def forward(self):
        cx = self.cx
        for k in range(1, cx.dp):
            self.zs[k - 1].wait_recv()
            block = self.at(cx.s, lax.rem(cx.d + cx.dp - k, cx.dp))
            self.xs.append(cx.send(block, block, cx.x))

    def finish(self):
        for c in self.xs:
            c.wait_recv()


class RelayW:
    def __init__(self, cx, shard, whole):
        self.cx, self.whole, self.rows = cx, whole, shard.shape[0]
        dp, d = cx.dp, cx.d
        self.base = cx.n
        cx.n += 4 * dp
        self.own = self.at(cx.s, d)

        @pl.when(d < dp - 1)
        def _():
            self.make(shard, self.own, 1, {"dp": d + 1}).start()

        @pl.when(d > 0)
        def _():
            self.make(shard, self.own, dp + 1, {"dp": d - 1}).start()

        self.make(shard, self.own, 2 * dp, cx.x).start()
        self.own[...] = shard[...]

    def at(self, s, d):
        start = (s * self.cx.dp + d) * self.rows
        return self.whole.at[pl.ds(pl.multiple_of(start, 16), self.rows)]

    def make(self, src, dst, i, dev):
        cx, i = self.cx, self.base + i
        return pltpu.make_async_remote_copy(
            src_ref=src,
            dst_ref=dst,
            send_sem=cx.ss.at[i],
            recv_sem=cx.rs.at[i],
            device_id=dev,
            device_id_type=MESH,
        )

    def hop(self, k):
        cx, dp, d = self.cx, self.cx.dp, self.cx.d

        @pl.when(d >= k)
        def _():
            b = self.at(cx.s, jnp.maximum(d - k, 0))
            self.make(b, b, k, cx.x).wait_recv()

            @pl.when(d < dp - 1)
            def _():
                self.make(b, b, k + 1, {"dp": d + 1}).start()

            self.make(b, b, 2 * dp + k, cx.x).start()

        @pl.when(d + k < dp)
        def _():
            b = self.at(cx.s, jnp.minimum(d + k, dp - 1))
            self.make(b, b, dp + k, cx.x).wait_recv()

            @pl.when(d > 0)
            def _():
                self.make(b, b, dp + k + 1, {"dp": d - 1}).start()

            self.make(b, b, 3 * dp + k, cx.x).start()

    def finish(self):
        cx, dp, d = self.cx, self.cx.dp, self.cx.d
        other = lambda e: self.at(1 - cx.s, jnp.clip(e, 0, dp - 1))
        self.make(self.own, other(d), 2 * dp, cx.x).wait_recv()
        for k in range(1, dp):

            @pl.when(d >= k)
            def _():
                self.make(self.own, other(d - k), 2 * dp + k, cx.x).wait_recv()

            @pl.when(d + k < dp)
            def _():
                self.make(self.own, other(d + k), 3 * dp + k, cx.x).wait_recv()

    def drain(self):
        cx, dp, d = self.cx, self.cx.dp, self.cx.d
        own = self.own
        self.make(own, own, 2 * dp, cx.x).wait_send()
        for k in range(1, dp):

            @pl.when(d >= k)
            def _():
                self.make(own, own, 2 * dp + k, cx.x).wait_send()

            @pl.when(d + k < dp)
            def _():
                self.make(own, own, 3 * dp + k, cx.x).wait_send()

            @pl.when((d < dp - 1) & (d >= k - 1))
            def _():
                self.make(own, own, k, cx.x).wait_send()

            @pl.when((d > 0) & (d + k - 1 < dp))
            def _():
                self.make(own, own, dp + k, cx.x).wait_send()


class Local:
    def __init__(self, sems):
        self.sems, self.n, self.pending = sems, 0, []

    def start(self, src, dst):
        c = pltpu.make_async_copy(src, dst, self.sems.at[self.n])
        self.n += 1
        c.start()
        self.pending.append(c)
        return c

    def drain(self):
        for c in self.pending:
            c.wait()


class ScatterW:
    def __init__(self, cx, rows, own, xs, xr, zs, zr):
        self.cx, self.rows, self.own = cx, rows, own
        self.xs, self.xr, self.zs, self.zr = xs, xr, zs, zr

    def start(self, theirs):
        self.xs[...] = theirs.astype(bf)
        self.cx_copy = self.cx.send(self.xs, self.xr, self.cx.x)

    def middle(self):
        cx, rows = self.cx, self.rows
        self.cx_copy.wait_recv()
        self.zs[...] = (self.own[...] + self.xr[...].astype(f32)).astype(bf)
        self.copies = []
        for k in range(1, cx.dp):
            to = lax.rem(cx.d + k, cx.dp)
            block = self.zs.at[pl.ds(pl.multiple_of(to * rows, 16), rows)]
            self.copies.append(cx.send(block, self.zr.at[k - 1], cx.z(k)))

    def finish(self):
        cx, rows = self.cx, self.rows
        mine = pl.ds(pl.multiple_of(cx.d * rows, 16), rows)
        own = self.own[mine, :] + self.xr[mine, :].astype(f32)
        for k in range(1, cx.dp):
            self.copies[k - 1].wait_recv()
            own = own + self.zr[k - 1].astype(f32)
        return own


def scatter_scratch(count, dp, rows, cols):
    half = dp * rows
    return [
        pltpu.VMEM((count, half, cols), bf),
        pltpu.VMEM((count, half, cols), bf),
        pltpu.VMEM((count, half, cols), bf),
        pltpu.VMEM((count, dp - 1, rows, cols), bf),
    ]


def iota(shape, dim):
    return lax.broadcasted_iota(jnp.int32, shape, dim)


def enc_forward_kernel(dp, gather, *refs):
    it = iter(refs)
    take = lambda n: [next(it) for _ in range(n)]
    res, x_all, gains, shifts, proj = take(5)
    if gather:
        eqkv, eout, eup, edown, dqkv, dout = take(6)
        ha, hb, hc = take(3)
    else:
        wa, wb, wc, wd_in = take(4)
    wd, h1, h2, hq, hctx, hslope, hact, hmid, top_out, low_all = take(10)
    ss, rs, ls, part, stage, recv, n1, n2, qkv, ctx, slope, active, mid_s = take(13)
    if gather:
        wa, wb, wc, sa, sd = take(5)
    cx = Ctx(ss, rs, dp)
    lc = Local(ls)
    peers = [cx.core, cx.y]
    if gather:
        peers += [cx.x] + [cx.z(k) for k in range(1, dp)]
        wide = eqkv.shape[2]
        for t in range(3):
            sa[:, t * wide : (t + 1) * wide] = eqkv[t]
        sa[:, 3 * wide :] = eout[...].astype(f32).T.astype(bf)
        wide = dqkv.shape[2]
        for t in range(3):
            sd[:, t * wide : (t + 1) * wide] = dqkv[t]
        sd[:, 3 * wide :] = dout[...]
    cx.barrier(peers)
    if gather:
        ga = RelayW(cx, sa, wa)
    stream = x_all[cx.s].astype(f32)
    n1[cx.m] = normalize(stream, gains[0:1, :], shifts[0:1, :]).astype(bf)
    g1 = GatherMp(cx, n1)
    if gather:
        gb = RelayW(cx, eup, wb)
        ga.hop(1)
        gc = RelayW(cx, edown, wc)
        ga.hop(2)
        gb.hop(1)
    g1.finish()
    lc.start(n1, h1)
    if gather:
        ga.hop(3)
        gd = RelayW(cx, sd, wd.at[0])
        gb.hop(2)
        gc.hop(1)
        ga.finish()
        lc.start(wa, ha)
    rows = n1.shape[1]
    total = 4 * rows
    width = n1.shape[2]
    n1_all = n1[...].reshape(total, width)
    qkv[...] = nn(n1_all, wa[...]).astype(bf)
    lc.start(qkv, hq)
    if gather:
        gb.hop(3)
        gc.hop(2)
        gd.hop(1)
    shown = jnp.where(res[cx.s] == 1, VIS, VIS_SMALL)
    bias = jnp.where(iota((1, total), 1) < shown, 0.0, NEG)
    scale2 = HD_ENC**-0.5 * LOG2E
    heads = (width // 4) // HD_ENC
    pieces = [jnp.zeros((total, HD_ENC), bf)]
    for h in range(heads):
        q = qkv[:, h * HD_ENC : (h + 1) * HD_ENC]
        k = qkv[:, (heads + h) * HD_ENC : (heads + h + 1) * HD_ENC]
        v = qkv[:, (2 * heads + h) * HD_ENC : (2 * heads + h + 1) * HD_ENC]
        sc = nt(q, k) + bias
        top = jnp.max(sc, axis=1, keepdims=True)
        e = jnp.exp2((sc - top) * scale2)
        tot = jnp.sum(e, axis=1, keepdims=True)
        pieces.append((nn(e.astype(bf), v) / tot).astype(bf))
        if gather and h == 1:
            gc.hop(3)
            gd.hop(2)
    ctx[...] = jnp.concatenate(pieces, axis=1)
    lc.start(ctx, hctx)
    cpad = ctx.shape[1]
    part[...] = nt(ctx[...], wa[:, width - cpad :]).reshape(part.shape)
    mid = stream + reduce_mp(cx, part, stage.at[0], recv.at[0])
    mid_s[...] = mid
    lc.start(mid_s, hmid)
    n2[cx.m] = normalize(mid, gains[1:2, :], shifts[1:2, :]).astype(bf)
    g2 = GatherMp(cx, n2)
    if gather:
        gd.hop(3)
        gb.finish()
        lc.start(wb, hb)
    g2.finish()
    lc.start(n2, h2)
    hid = nn(n2[...].reshape(total, width), wb[...])
    act, slo = gelu_and_slope(hid)
    active[...] = act.astype(bf)
    slope[...] = slo.astype(bf)
    lc.start(active, hact)
    lc.start(slope, hslope)
    if gather:
        gc.finish()
        lc.start(wc, hc)
    part[...] = nt(active[...], wc[...]).reshape(part.shape)
    top = (mid_s[...] + reduce_mp(cx, part, stage.at[1], recv.at[1])).astype(bf)
    top_out[...] = top
    low_all[cx.m] = nn(top, proj[...]).astype(bf)
    g3 = GatherMp(cx, low_all)
    if gather:
        gd.finish()
    else:
        wd[0] = wd_in[...]
    g3.finish()
    yd = cx.send(wd.at[0], wd.at[1], cx.y)
    yd.wait_recv()
    cx.drain()
    if gather:
        for g in (ga, gb, gc, gd):
            g.drain()
    lc.drain()


def vm(n):
    return [pl.BlockSpec(memory_space=pltpu.VMEM)] * n


def anywhere(n):
    return [pl.BlockSpec(memory_space=pl.ANY)] * n


SMEM = pl.BlockSpec(memory_space=pltpu.SMEM)


def sds(shape, dtype):
    return jax.ShapeDtypeStruct(shape, dtype)


def params(cid):
    return pltpu.CompilerParams(collective_id=cid, has_side_effects=True, vmem_limit_bytes=60 << 20)


def enc_forward(dp, gather, res, x, gains, shifts, proj, shards, de, dd, wide, dwide):
    rows, width = x.shape[1:]
    total = 4 * rows
    slots = (4, rows, width)
    V = pltpu.VMEM
    outs = []
    if gather:
        outs += [sds((de, de), bf), sds((de, wide), bf), sds((de, wide), bf)]
    outs += [sds((2, dd, dwide), bf)]
    big = [sds(slots, bf), sds(slots, bf), sds((total, width), bf), sds((total, 256), bf)]
    big += [sds((total, wide), bf), sds((total, wide), bf), sds((rows, width), f32)]
    outs += big + [sds((rows, width), bf), sds((4, rows, dd), bf)]
    scratch = [
        pltpu.SemaphoreType.DMA((96,)),
        pltpu.SemaphoreType.DMA((96,)),
        pltpu.SemaphoreType.DMA((16,)),
        V(slots, f32),
        V((2, 3, rows, width), bf),
        V((2, 3, rows, width), bf),
    ] + [V(b.shape, b.dtype) for b in big]
    if gather:
        scratch += [V(o.shape, bf) for o in outs[:3]]
        scratch += [V((shards[2].shape[0], de), bf), V((shards[5].shape[0], dwide), bf)]
    got = pl.pallas_call(
        functools.partial(enc_forward_kernel, dp, gather),
        out_shape=outs,
        in_specs=[SMEM] + vm(4 + len(shards)),
        out_specs=anywhere(3 if gather else 0) + vm(1) + anywhere(7) + vm(2),
        scratch_shapes=scratch,
        compiler_params=params(1),
        name="enc_forward",
    )(res, x, gains, shifts, proj, *shards)
    if not gather:
        got = list(shards[:3]) + list(got)
    return got[:4], got[4:]


def dec_kernel(dp, gather, *refs):
    it = iter(refs)
    take = lambda n: [next(it) for _ in range(n)]
    res, chosen, low_all, table, cot, gains, shifts, token, wd, e_in, f_in = take(11)
    out, glow, gd_own, gd_far, out_e, out_f, small = take(7)
    ss, rs, we, wf, place_s, own_e, own_f, yst, yrc = take(9)
    if gather:
        dxs, dxr, dzs, dzr = take(4)
    (n1, n2, gm, gmid_low, qg, kg, vg, gg, vtx, kt, ct, dqt, lse, acc_s, top_s, ctx, active, slope) = take(18)
    (dkv, mid_s, start_s, res_s, part, fstage, frecv, far, prod, pstage, precv, masks) = take(12)
    cx = Ctx(ss, rs, dp)
    cx.barrier([cx.core, cx.y, cx.x] + ([cx.z(k) for k in range(1, dp)] if gather else []))
    rows, width = n1.shape[1:]
    m, lo, hi, s = cx.m, cx.lo, cx.hi, cx.s
    big = res[s] == 1
    shown = jnp.where(big, VIS, VIS_SMALL)
    filled = jnp.where(big, PATCHES, SMALL_PATCHES)
    pos_col = iota((rows, 1), 0) + m * rows
    live = jnp.where(pos_col < filled, 1.0, 0.0)
    gm[lo] = (cot[s].astype(f32) * live).astype(bf)
    cgm = cx.send(gm.at[lo], gm.at[lo], cx.core)
    if gather:
        gat_e = GatherW(cx, e_in, we.at[0])
        gat_f = GatherW(cx, f_in, wf.at[0])
    else:
        we[0] = e_in[...]
        wf[0] = f_in[...]
    vis = chosen.shape[-1]
    place = jnp.where((pos_col == chosen[pl.ds(s, 1), :]) & (iota((1, vis), 1) < shown), 1.0, 0.0)
    seen = jnp.sum(place, axis=1, keepdims=True)
    weight = live - seen
    place_s[...] = place.astype(bf)
    placed = nn(place_s[...], low_all[...].reshape(vis, width))
    half = width // 2
    nb, ns = rows // COLS_BIG, rows // COLS_SMALL
    rb = table[pl.ds(pl.multiple_of(m * nb, 8), nb), :]
    rsm = table[pl.ds(pl.multiple_of(m * ns, 8), ns), :]
    big_rows = jnp.broadcast_to(rb[:, None, :], (nb, COLS_BIG, half)).reshape(rows, half)
    small_rows = jnp.broadcast_to(rsm[:, None, :], (ns, COLS_SMALL, half)).reshape(rows, half)
    big_cols = jnp.broadcast_to(table[0:COLS_BIG, :][None], (nb, COLS_BIG, half)).reshape(rows, half)
    small_cols = jnp.broadcast_to(table[0:COLS_SMALL, :][None], (ns, COLS_SMALL, half)).reshape(rows, half)
    base = placed + weight * token[...]
    start_s[:, :half] = base[:, :half] + live * jnp.where(big, big_rows, small_rows)
    start_s[:, half:] = base[:, half:] + live * jnp.where(big, big_cols, small_cols)
    n1[m] = normalize(start_s[...], gains[0:1, :], shifts[0:1, :]).astype(bf)
    g1 = GatherMp(cx, n1)

    lane = iota((1, 256), 1)
    for j in range(4):
        head_lane = (lane < 128) & (lane // 32 == j)
        off = lane - (128 + 8 * j)
        masks[0, j] = jnp.where(head_lane | ((off >= 0) & (off < 3)) | (lane == 160), 1.0, 0.0).astype(bf)
        masks[1, j] = jnp.where(head_lane | ((off >= 0) & (off < 2)), 1.0, 0.0).astype(bf)
    aug = iota((1, 128), 1)
    total = 4 * rows
    key_bias = jnp.where(iota((total, 1), 0) < filled, 0.0, NEG)
    kaug = jnp.where(aug == 32, key_bias, jnp.where(aug < 32, 1.0, 0.0)).astype(bf)
    vaug = jnp.broadcast_to(jnp.where(aug < 32, 1.0, 0.0), (total, 128)).astype(bf)
    qaug = jnp.broadcast_to(jnp.where(aug == 32, 1.0, 0.0), (2 * rows, 128)).astype(bf)
    for g in range(2):
        kg[g, :, 128:] = kaug
        vg[g, :, 128:] = vaug
        qg[g, :, 128:] = qaug
    vtx[:, 32:, :] = jnp.ones((8, 16, total), bf)
    lse[...] = jnp.zeros_like(lse)

    def keys_values(i):
        at = pl.ds(pl.multiple_of(i * rows, 128), rows)
        for g in range(2):
            kv = nn(n1[i], wd[g, :, 128:384])
            kg[g, at, :128] = kv[:, :128].astype(bf)
            vg[g, at, :128] = kv[:, 128:].astype(bf)
            kvt = kv.T.astype(bf)
            for j in range(4):
                kt[4 * g + j, :, at] = kvt[32 * j : 32 * j + 32]
                vtx[4 * g + j, 0:32, at] = kvt[128 + 32 * j : 160 + 32 * j]

    g1.near()
    for r in range(2):
        for g in range(2):
            qg[g, r * rows : (r + 1) * rows, :128] = nn(n1[2 * hi + r], wd[g, :, :128]).astype(bf)
    keys_values(cx.m)
    keys_values(cx.m1)
    c2 = HD_DEC**-0.5 * LOG2E

    def head_pass(first, last, blocks, heads):
        def body(h, _):
            g, j = h // 4, lax.rem(h, 4)
            if first:
                top, acc = None, None
            else:
                top, acc = top_s[h], acc_s[h]
            for i in blocks:
                at = pl.ds(pl.multiple_of(i * rows, 128), rows)
                sc = nt(kg[g, at, :] * masks[0, j], qg[g])
                mj = jnp.max(sc, axis=0, keepdims=True)
                new = mj if top is None else jnp.maximum(top, mj)
                p = jnp.exp2((sc - new) * c2).astype(bf)
                o = nn(vtx[h, :, at], p)
                acc = o if acc is None else acc * jnp.exp2((top - new) * c2) + o
                top = new
            if last:
                tot = acc[32:33, :]
                ct[h] = acc[:32, :] / tot
                at = pl.ds(pl.multiple_of(8 * j, 8), 8)
                lse[g, at, :] = jnp.broadcast_to(top + jnp.log(tot) * (LOG2E / c2), (8, top.shape[1]))
            else:
                top_s[h] = top
                acc_s[h] = acc
            return 0

        lax.fori_loop(*heads, body, 0)

    if gather:
        gat_e.forward()
    head_pass(True, False, (cx.m, cx.m1), (0, 4))
    g1.forward()
    if gather:
        gat_f.forward()
    head_pass(True, False, (cx.m, cx.m1), (4, 8))
    keys_values(cx.m2)
    g1.far()
    keys_values(cx.m3)
    if gather:
        gat_e.finish()
    ye = cx.send(we.at[0], we.at[1], cx.y)
    head_pass(False, True, (cx.m2, cx.m3), (0, 4))
    if gather:
        gat_f.finish()
    yf = cx.send(wf.at[0], wf.at[1], cx.y)
    head_pass(False, True, (cx.m2, cx.m3), (4, 8))
    for g in range(2):
        ctx[:, 128 * g : 128 * g + 128] = ct[4 * g : 4 * g + 4].reshape(128, 2 * rows).T.astype(bf)

    def reduce_core(slot, compute):
        fstage[slot] = compute(1 - lo).astype(bf)
        c = cx.send(fstage.at[slot], frecv.at[slot], cx.core)
        own = compute(lo)
        c.wait_recv()
        return own + frecv[slot].astype(f32)

    def chip_rows(r):
        return pl.ds(pl.multiple_of(r * rows, 128), rows)

    def out_rows(r):
        return sum(nt(ctx[chip_rows(r), 128 * g : 128 * g + 128], wd[g, :, 384:]) for g in range(2))

    mid = start_s[...] + reduce_core(0, out_rows)
    mid_s[...] = mid
    n2[lo] = normalize(mid, gains[1:2, :], shifts[1:2, :]).astype(bf)
    cn2 = cx.send(n2.at[lo], n2.at[lo], cx.core)

    def mlp_rows(r):
        at = chip_rows(r)
        x = n2[r]
        y = None
        for g in range(2):
            a, b = gelu_and_slope(nn(x, we[g]))
            cols = slice(width * g, width * (g + 1))
            a = a.astype(bf)
            active[at, cols] = a
            slope[at, cols] = b.astype(bf)
            t = nt(a, wf[g])
            y = t if y is None else y + t
        return y

    ye.wait_recv()
    yf.wait_recv()
    res_s[...] = mlp_rows(lo)
    cn2.wait_recv()
    fstage[1] = mlp_rows(1 - lo).astype(bf)
    c = cx.send(fstage.at[1], frecv.at[1], cx.core)

    cgm.wait_recv()

    def mlp_back_rows(r):
        at = chip_rows(r)
        y = None
        for g in range(2):
            cols = slice(width * g, width * (g + 1))
            ga = nn(gm[r], wf[g])
            gh = (ga * slope[at, cols].astype(f32)).astype(bf)
            slope[at, cols] = gh
            t = nt(gh, we[g])
            y = t if y is None else y + t
        return y

    fstage[2] = mlp_back_rows(1 - lo).astype(bf)
    cb = cx.send(fstage.at[2], frecv.at[2], cx.core)
    c.wait_recv()
    result = mid_s[...] + res_s[...] + frecv[1].astype(f32)
    produced = (result * live).astype(bf)
    prod[0] = produced[:, :half]
    prod[1] = produced[:, half:]
    out[s] = prod[s]
    cprod = cx.send(prod.at[1 - s], out.at[s], cx.x)
    own = mlp_back_rows(lo)
    gm_all = gm[...].reshape(2 * rows, width)
    yst[0] = tn(gm_all, active[:, width:]).astype(bf)
    cyf = cx.send(yst.at[0], yrc.at[0], cx.y)
    cb.wait_recv()
    grad_mid, gain_mid, shift_mid = normalize_back(mid_s[...], gains[1:2, :], own + frecv[2].astype(f32))
    gmid = gm[lo].astype(f32) + grad_mid
    mid_s[...] = gmid
    gmid_low[lo] = gmid.astype(bf)
    cgmid = cx.send(gmid_low.at[lo], gmid_low.at[lo], cx.core)
    n2_all = n2[...].reshape(2 * rows, width)
    yst[1] = tn(n2_all, slope[:, width:]).astype(bf)
    cye = cx.send(yst.at[1], yrc.at[1], cx.y)
    own_f[...] = tn(gm_all, active[:, :width])
    own_e[...] = tn(n2_all, slope[:, :width])
    cgmid.wait_recv()
    gmid_all = gmid_low[...].reshape(2 * rows, width)
    sel = jnp.where(iota((128, 128), 0) // 32 == iota((128, 128), 1) // 8, 1.0, 0.0).astype(bf)
    lane128 = iota((1, 128), 1)
    t8 = lax.rem(lane128, 8)
    for g in range(2):
        gcg = nn(gmid_all, wd[g, :, 384:]).astype(bf)
        gg[g, :, :128] = gcg
        prodd = gcg.astype(f32) * ctx[:, 128 * g : 128 * g + 128].astype(f32)
        ph = prodd.astype(bf)
        plow = (prodd - ph.astype(f32)).astype(bf)
        delta = nn(ph, sel) + nn(plow, sel)
        dh = delta.astype(bf).astype(f32)
        daug = jnp.where(t8 == 0, -dh, jnp.where(t8 == 1, dh - delta, 0.0))
        gg[g, :, 128:] = jnp.where(lane128 < 32, daug, 0.0).astype(bf)
        gd_out = tn(gmid_all, ctx[:, 128 * g : 128 * g + 128])
        if g == 0:
            gd_own[:, 384:] = gd_out
        else:
            gd_far[:, 384:] = gd_out.astype(bf)
        lt = lse[g].T
        h1 = lt.astype(bf).astype(f32)
        h2 = (lt - h1).astype(bf).astype(f32)
        h3 = lt - h1 - h2
        laug = jnp.where(t8 == 0, -h1, jnp.where(t8 == 1, -h2, jnp.where(t8 == 2, -h3, 0.0)))
        laug = jnp.where(lane128 == 32, 1.0, jnp.where(lane128 < 32, laug, 0.0))
        qg[g, :, 128:] = laug.astype(bf)

    scale = HD_DEC**-0.5
    dqt[...] = jnp.zeros_like(dqt)
    head_lane = lane128 // 32

    def back_pass(blocks, heads):
        def body(h, _):
            g, j = h // 4, lax.rem(h, 4)
            mine = head_lane == j
            for i in blocks:
                at = pl.ds(pl.multiple_of(i * rows, 128), rows)
                st = nt(kg[g, at, :] * masks[0, j], qg[g])
                dpt = nt(vg[g, at, :] * masks[1, j], gg[g])
                p = jnp.exp2(st * c2)
                ds = (p * dpt).astype(bf)
                dv = nn(p.astype(bf), gg[g, :, :128])
                dk = nn(ds, qg[g, :, :128]) * scale
                dkv[g, at, :128] = jnp.where(mine, dk, dkv[g, at, :128].astype(f32)).astype(bf)
                dkv[g, at, 128:] = jnp.where(mine, dv, dkv[g, at, 128:].astype(f32)).astype(bf)
                dqt[h] += nn(kt[h, :, at], ds)
            return 0

        lax.fori_loop(*heads, body, 0)

    dkv[...] = jnp.zeros_like(dkv)
    back_pass((cx.m2, cx.m3), (0, 4))
    for c, own, o, i in ((cyf, own_f, out_f, 0), (cye, own_e, out_e, 1)):
        c.wait_recv()
        own[...] = own[...] + yrc[i].astype(f32)
        if not gather:
            o[...] = own[...]
    if gather:
        half_rows = width // 2
        mlp = []
        for own, i in ((own_f, 0), (own_e, 1)):
            at = pl.ds(pl.multiple_of(s * half_rows, 16), half_rows)
            q = ScatterW(cx, half_rows // dp, own.at[at], dxs.at[i], dxr.at[i], dzs.at[i], dzr.at[i])
            q.start(own[pl.ds(pl.multiple_of((1 - s) * half_rows, 16), half_rows), :])
            mlp.append(q)
    back_pass((cx.m2, cx.m3), (4, 8))
    if gather:
        for q in mlp:
            q.middle()

    def far_rows(r):
        at = pl.ds(pl.multiple_of((2 * (1 - hi) + r) * rows, 128), rows)
        return sum(nt(dkv[g, at, :], wd[g, :, 128:384]) for g in range(2))

    far[0] = reduce_core(3, far_rows).astype(bf)
    cfar = cx.send(far.at[0], far.at[1], cx.y)
    back_pass((cx.m, cx.m1), (0, 8))
    if gather:
        out_f[...] = mlp[0].finish()
        out_e[...] = mlp[1].finish()
    for g in range(2):
        ctx[:, 128 * g : 128 * g + 128] = (dqt[4 * g : 4 * g + 4].reshape(128, 2 * rows).T * scale).astype(bf)

    def near_rows(r):
        at = pl.ds(pl.multiple_of((2 * hi + r) * rows, 128), rows)
        return sum(
            nt(ctx[chip_rows(r), 128 * g : 128 * g + 128], wd[g, :, :128]) + nt(dkv[g, at, :], wd[g, :, 128:384])
            for g in range(2)
        )

    near = reduce_core(4, near_rows)
    cfar.wait_recv()
    grad_in, gain_in, shift_in = normalize_back(start_s[...], gains[0:1, :], near + far[1].astype(f32))
    gstart = (mid_s[...] + grad_in).astype(bf)
    token_term = jnp.sum(weight * gstart.astype(f32), axis=0, keepdims=True)
    small[0:1] = gain_in
    small[1:2] = gain_mid
    small[2:3] = shift_in
    small[3:4] = shift_mid
    small[4:5] = token_term
    small[5:8] = jnp.zeros((3, width), f32)
    part[...] = tn(place_s[...], gstart).reshape(part.shape)
    reduce = ReduceMp(cx, part, pstage, precv)
    n1_chip = n1[pl.ds(2 * hi, 2)].reshape(2 * rows, width)
    gd_own[:, :128] = tn(n1_chip, ctx[:, :128])
    reduce.middle()
    gd_far[:, :128] = tn(n1_chip, ctx[:, 128:]).astype(bf)
    n1_all = n1[...].reshape(total, width)
    gd_own[:, 128:384] = tn(n1_all, dkv[0])
    gd_far[:, 128:384] = tn(n1_all, dkv[1]).astype(bf)
    glow[...] = reduce.finish().astype(bf)
    cprod.wait_recv()
    cx.drain()


def decoder(dp, gather, res, chosen, low_all, table, cot, gains, shifts, token, wd, e_in, f_in):
    rows, width = cot.shape[1:]
    vis = chosen.shape[-1]
    total, chip = 4 * rows, 2 * rows
    square = (width, wd.shape[2])
    outs = [
        sds((2, rows, width // 2), bf),
        sds((vis // 4, width), bf),
        sds(square, f32),
        sds(square, bf),
        sds(e_in.shape, f32),
        sds(f_in.shape, f32),
        sds((8, width), f32),
    ]
    V = pltpu.VMEM
    extra = scatter_scratch(2, dp, e_in.shape[0], e_in.shape[1]) if gather else []
    return pl.pallas_call(
        functools.partial(dec_kernel, dp, gather),
        out_shape=outs,
        in_specs=[SMEM] + vm(10),
        out_specs=vm(len(outs)),
        scratch_shapes=[
            pltpu.SemaphoreType.DMA((64,)),
            pltpu.SemaphoreType.DMA((64,)),
            V(wd.shape, bf),
            V(wd.shape, bf),
            V((rows, vis), bf),
            V(square, f32),
            V(square, f32),
            V((2,) + square, bf),
            V((2,) + square, bf),
        ]
        + extra
        + [
            V((4, rows, width), bf),
            V((2, rows, width), bf),
            V((2, rows, width), bf),
            V((2, rows, width), bf),
            V((2, chip, 256), bf),
            V((2, total, 256), bf),
            V((2, total, 256), bf),
            V((2, chip, 256), bf),
            V((8, 48, total), bf),
            V((8, 32, total), bf),
            V((8, 32, chip), f32),
            V((8, 32, chip), f32),
            V((2, 128, chip), f32),
            V((8, 48, chip), f32),
            V((8, 1, chip), f32),
            V((chip, 256), bf),
            V((chip, 2 * width), bf),
            V((chip, 2 * width), bf),
            V((2, total, 256), bf),
            V((rows, width), f32),
            V((rows, width), f32),
            V((rows, width), f32),
            V((4, vis // 4, width), f32),
            V((5, rows, width), bf),
            V((5, rows, width), bf),
            V((2, rows, width), bf),
            V((2, rows, width // 2), bf),
            V((3, vis // 4, width), bf),
            V((3, vis // 4, width), bf),
            V((2, 4, 1, 256), bf),
        ],
        compiler_params=params(2),
        name="decoder",
    )(res, chosen, low_all, table, cot, gains, shifts, token, wd, e_in, f_in)


def enc_backward_kernel(dp, gather, *refs):
    it = iter(refs)
    take = lambda n: [next(it) for _ in range(n)]
    res, x_all, gains, proj, mid, top, glow, gd_own, gd_far, dsmall = take(10)
    hbm = take(9)
    gin, out_qkv, out_o, out_b, out_c, out_dqkv, out_do = take(7)
    eg, es, pout, mg, dg, dsh = take(6)
    ss, rs, ls = take(3)
    vmem = take(9)
    gm, gmid_low, gqkv, part, stage, recv, gbuf, yrc, gmid_half = take(9)
    if gather:
        exs, exr, ezs, ezr, dxs, dxr, dzs, dzr, own_w, smr, smz, pst, prc, pzs, pzr, pacc, pwhole = take(17)
    lc = Local(ls)
    loads = [lc.start(h, v) for h, v in zip(hbm, vmem)]
    wc, slope, wb, active, n2, wa, ctx, qkv, n1 = vmem
    cx = Ctx(ss, rs, dp)
    peers = [cx.core, cx.y, cx.x]
    if gather:
        peers += [cx.z(k) for k in range(1, dp)]
    cx.barrier(peers)
    m, s = cx.m, cx.s
    rows, width = gm.shape[1:]
    total = 4 * rows
    half = width // 2
    g_top = nt(glow[...], proj[...])
    gm[m] = g_top.astype(bf)
    g1 = GatherMp(cx, gm)
    cyd = cx.send(gd_far, yrc, cx.y)
    p_part = tn(top[...], glow[...])
    if gather:
        pr = ProjSum(cx, pst, prc, pzs, pzr, pacc, pwhole, pout)
        pr.core(p_part)
    else:
        pout[...] = p_part

    def grad_halves(i, terms, out):
        def rows_of(sec):
            at = pl.ds(pl.multiple_of(sec * half, 128), half)
            sums = []
            for cols in terms:
                t = None
                for left, right in cols:
                    y = tn(left[:, :, at].reshape(total, half), right)
                    t = y if t is None else t + y
                sums.append(t)
            return sums[0] if len(sums) == 1 else jnp.concatenate(sums, axis=1)

        if gather:
            q = ScatterW(cx, half // dp, own_w.at[i], exs.at[i], exr.at[i], ezs.at[i], ezr.at[i])
            q.start(rows_of(1 - s))
            own_w[i] = rows_of(s)
            return q
        for sec in (0, 1):
            out[sec * half : (sec + 1) * half] = rows_of(jnp.int32(sec))

    g1.finish()
    gm_all = gm[...].reshape(total, width)
    loads[0].wait()
    loads[1].wait()
    gh = (nn(gm_all, wc[...]) * slope[...].astype(f32)).astype(bf)
    loads[2].wait()
    part[...] = nt(gh, wb[...]).reshape(part.shape)
    if gather:
        pr.y()
    r1 = ReduceMp(cx, part, stage.at[0], recv.at[0])
    cyd.wait_recv()
    gbuf[...] = gd_own[...] + yrc[...].astype(f32)
    if gather:
        hd = gbuf.shape[0] // 2
        dxs_own = pl.ds(pl.multiple_of(s * hd, 16), hd)
        qd = ScatterW(cx, hd // dp, gbuf.at[dxs_own], dxs, dxr, dzs, dzr)
        qd.start(gbuf[pl.ds(pl.multiple_of((1 - s) * hd, 16), hd), :])
    r1.middle()
    loads[3].wait()
    loads[4].wait()
    qc = grad_halves(2, [[(gm, active[...])]], out_c)
    if gather:
        pr.x()
    g_n2 = r1.finish()
    grad_mid, gain_mid, shift_mid = normalize_back(mid[...], gains[1:2, :], g_n2)
    gmid = g_top + grad_mid
    gmid_half[...] = gmid
    gmid_low[m] = gmid.astype(bf)
    g2 = GatherMp(cx, gmid_low)
    qb = grad_halves(1, [[(n2, gh)]], out_b)
    if gather:
        pr.z()
    g2.finish()
    for c in loads[5:]:
        c.wait()
    gmid_all = gmid_low[...].reshape(total, width)
    cpad = ctx.shape[1]
    cut = width - cpad
    gcx = nn(gmid_all, wa[:, cut:]).astype(bf)
    shown = jnp.where(res[s] == 1, VIS, VIS_SMALL)
    bias = jnp.where(iota((1, total), 1) < shown, 0.0, NEG)
    scale = HD_ENC**-0.5
    scale2 = scale * LOG2E
    heads = (width // 4) // HD_ENC
    for h in range(heads):
        q = qkv[:, h * HD_ENC : (h + 1) * HD_ENC]
        k = qkv[:, (heads + h) * HD_ENC : (heads + h + 1) * HD_ENC]
        v = qkv[:, (2 * heads + h) * HD_ENC : (2 * heads + h + 1) * HD_ENC]
        go = gcx[:, (h + 1) * HD_ENC : (h + 2) * HD_ENC]
        co = ctx[:, (h + 1) * HD_ENC : (h + 2) * HD_ENC]
        scr = nt(q, k) + bias
        e = jnp.exp2((scr - jnp.max(scr, axis=1, keepdims=True)) * scale2)
        p = e / jnp.sum(e, axis=1, keepdims=True)
        delta = jnp.sum(go.astype(f32) * co.astype(f32), axis=1, keepdims=True)
        gs = (p * (nt(go, v) - delta) * scale).astype(bf)
        gqkv[:, h * HD_ENC : (h + 1) * HD_ENC] = nn(gs, k).astype(bf)
        gqkv[:, (heads + h) * HD_ENC : (heads + h + 1) * HD_ENC] = tn(gs, q).astype(bf)
        gqkv[:, (2 * heads + h) * HD_ENC : (2 * heads + h + 1) * HD_ENC] = tn(p.astype(bf), go).astype(bf)
        if gather and h == 0:
            qd.middle()
            pr.back_z()
        if gather and h == 1:
            qc.middle()
        if gather and h == 2:
            pr.back_x()
    gqkv[:, 3 * heads * HD_ENC :] = jnp.zeros((total, width - 3 * heads * HD_ENC), bf)
    part[...] = nt(gqkv[...], wa[...]).reshape(part.shape)
    r2 = ReduceMp(cx, part, stage.at[1], recv.at[1])
    r2.middle()
    qa = grad_halves(0, [[(n1, gqkv[:, :cut])], [(n1, gqkv[:, cut:]), (gmid_low, ctx[...])]], out_qkv)
    if gather:
        pr.back_y()
        qb.middle()
    g_n1 = r2.finish()
    stream = x_all[s].astype(f32)
    grad_in, gain_in, shift_in = normalize_back(stream, gains[0:1, :], g_n1)
    grad = gmid_half[...] + grad_in
    part[0, :, :half] = grad[:, :half]
    part[1, :, :half] = grad[:, half:]
    gin[s] = part[s, :, :half]
    cin = cx.send(part.at[1 - s, :, pl.ds(0, half)], gin.at[s], cx.x)
    dw = dsmall.shape[1]
    vec = jnp.concatenate(
        [
            gain_in,
            gain_mid,
            shift_in,
            shift_mid,
            jnp.zeros((4, width), f32),
            jnp.concatenate([dsmall[...], jnp.zeros((8, width - dw), f32)], axis=1),
        ],
        axis=0,
    )
    if gather:
        smr[0] = vec
        c = cx.send(smr.at[0], smr.at[1], cx.core)
        c.wait_recv()
        smr[2] = smr[0] + smr[1]
        c = cx.send(smr.at[2], smr.at[3], cx.y)
        g = qd.finish()
        unit = out_dqkv.shape[2]
        for t in range(3):
            out_dqkv[t] = g[:, t * unit : (t + 1) * unit]
        out_do[...] = g[:, 3 * unit :]
        c.wait_recv()
        smr[4] = smr[2] + smr[3]
        c = cx.send(smr.at[4], smr.at[5], cx.x)
        pr.back_core()
        c.wait_recv()
        smz[cx.d] = smr[4] + smr[5]
        cs = [cx.send(smz.at[cx.d], smz.at[cx.d], cx.z(k)) for k in range(1, dp)]
        out_c[...] = qc.finish()
        for c in cs:
            c.wait_recv()
        vec = sum_in_order(smz, dp)
        qa.middle()
        out_b[...] = qb.finish()
        pr.finish()
        g = qa.finish()
        unit = out_qkv.shape[2]
        for t in range(3):
            out_qkv[t] = g[:, t * unit : (t + 1) * unit]
        out_o[...] = g[:, 3 * unit :].T
    else:
        out_dqkv[...] = gbuf[...]
        out_do[...] = jnp.zeros(out_do.shape, f32)
        out_o[...] = jnp.zeros(out_o.shape, f32)
    eg[...] = vec[0:2]
    es[...] = vec[2:4]
    dg[...] = vec[8:10, :dw]
    dsh[...] = vec[10:12, :dw]
    mg[...] = vec[12:13, :dw]
    cin.wait_recv()
    cx.drain()


def sum_in_order(ref, n):
    out = ref[0]
    for i in range(1, n):
        out = out + ref[i]
    return out


class ProjSum:
    def __init__(self, cx, st, rc, zs, zr, acc, whole, out):
        self.cx, self.st, self.rc, self.zs, self.zr = cx, st, rc, zs, zr
        self.acc, self.whole, self.out = acc, whole, out
        self.R, self.C = out.shape

    def rows(self, start, size):
        return pl.ds(pl.multiple_of(start, 16), size)

    def core(self, part):
        cx, R = self.cx, self.R
        h = R // 2
        self.acc[...] = part
        self.o1 = cx.lo * h
        self.st[0:h] = self.acc[self.rows((1 - cx.lo) * h, h), :].astype(bf)
        self.c = cx.send(self.st.at[pl.ds(0, h)], self.rc.at[pl.ds(0, h)], cx.core)

    def step(self, prev_at, prev_size, bit, dev):
        cx, R = self.cx, self.R
        self.c.wait_recv()
        off = R - 2 * prev_size
        mine = self.rows(prev_at, prev_size)
        self.acc[mine, :] = self.acc[mine, :] + self.rc[off : off + prev_size, :].astype(f32)
        h = prev_size // 2
        noff = R - 2 * h
        self.st[noff : noff + h] = self.acc[self.rows(prev_at + (1 - bit) * h, h), :].astype(bf)
        self.c = cx.send(self.st.at[pl.ds(noff, h)], self.rc.at[pl.ds(noff, h)], dev)
        return prev_at + bit * h

    def y(self):
        self.o2 = self.step(self.o1, self.R // 2, self.cx.hi, self.cx.y)

    def x(self):
        self.o3 = self.step(self.o2, self.R // 4, self.cx.s, self.cx.x)

    def z(self):
        cx, R = self.cx, self.R
        size, unit = R // 8, self.C // cx.dp
        self.c.wait_recv()
        off = R - 2 * size
        total = self.acc[self.rows(self.o3, size), :] + self.rc[off : off + size, :].astype(f32)
        for e in range(cx.dp):
            self.zs[e] = total[:, e * unit : (e + 1) * unit].astype(bf)
        self.cs = []
        for k in range(1, cx.dp):
            to = lax.rem(cx.d + k, cx.dp)
            self.cs.append(cx.send(self.zs.at[to], self.zr.at[k - 1], cx.z(k)))

    def back_z(self):
        cx = self.cx
        unit = self.C // cx.dp
        total = self.zs[cx.d].astype(f32)
        for k in range(1, cx.dp):
            self.cs[k - 1].wait_recv()
            total = total + self.zr[k - 1].astype(f32)
        at = self.whole.at[self.rows(self.o3, self.R // 8), pl.ds(pl.multiple_of(cx.d * unit, 128), unit)]
        at[...] = total.astype(bf)
        self.cs = [cx.send(at, at, cx.z(k)) for k in range(1, cx.dp)]

    def back_x(self):
        for c in self.cs:
            c.wait_recv()
        at = self.rows(self.o3, self.R // 8)
        self.c = self.cx.send(self.whole.at[at], self.whole.at[at], self.cx.x)

    def back_y(self):
        self.c.wait_recv()
        at = self.rows(self.o2, self.R // 4)
        self.c = self.cx.send(self.whole.at[at], self.whole.at[at], self.cx.y)

    def back_core(self):
        self.c.wait_recv()
        at = self.rows(self.o1, self.R // 2)
        self.c = self.cx.send(self.whole.at[at], self.whole.at[at], self.cx.core)

    def finish(self):
        self.c.wait_recv()
        self.out[...] = self.whole[...].astype(f32)


def enc_backward(dp, gather, res, x, gains, proj, weights, saved, glow, gd_own, gd_far, dsmall, ec, dc):
    wa, wb, wc = weights
    n1, n2, qkv, ctx, slope, active, mid, top = saved
    rows, width = x.shape[1:]
    total = 4 * rows
    V = pltpu.VMEM
    dd, dw = gd_own.shape
    er, dr = wa.shape[0] // (2 * dp), dd // (2 * dp)
    outs = [sds((2, rows, width // 2), f32)]
    if gather:
        outs += [sds((3, er, ec), f32), sds((ec, er), f32), sds((er, wb.shape[1]), f32), sds((er, wc.shape[1]), f32)]
        outs += [sds((3, dr, dc), f32), sds((dr, dc), f32)]
    else:
        outs += [sds(wa.shape, f32), sds((8, 128), f32), sds(wb.shape, f32), sds(wc.shape, f32)]
        outs += [sds((dd, dw), f32), sds((8, 128), f32)]
    outs += [sds((2, width), f32), sds((2, width), f32), sds(proj.shape, f32)]
    outs += [sds((1, dd), f32), sds((2, dd), f32), sds((2, dd), f32)]
    slots = (4, rows, width)
    hbm = (wc, slope, wb, active, n2, wa, ctx, qkv, n1)
    scratch = [
        pltpu.SemaphoreType.DMA((80,)),
        pltpu.SemaphoreType.DMA((80,)),
        pltpu.SemaphoreType.DMA((16,)),
    ]
    scratch += [V(a.shape, a.dtype) for a in hbm]
    scratch += [
        V(slots, bf),
        V(slots, bf),
        V((total, width), bf),
        V(slots, f32),
        V((2, 3, rows, width), bf),
        V((2, 3, rows, width), bf),
        V((dd, dw), f32),
        V((dd, dw), bf),
        V((rows, width), f32),
    ]
    if gather:
        scratch += scatter_scratch(3, dp, er, wa.shape[1])
        scratch += [V(r.shape[1:], r.dtype) for r in scatter_scratch(1, dp, dr, dw)]
        scratch += [
            V((3, dp * er, wa.shape[1]), f32),
            V((6, 16, width), f32),
            V((dp, 16, width), f32),
            V(proj.shape, bf),
            V(proj.shape, bf),
            V((dp, proj.shape[0] // 8, proj.shape[1] // dp), bf),
            V((dp - 1, proj.shape[0] // 8, proj.shape[1] // dp), bf),
            V(proj.shape, f32),
            V(proj.shape, bf),
        ]
    return pl.pallas_call(
        functools.partial(enc_backward_kernel, dp, gather),
        out_shape=outs,
        in_specs=[SMEM] + vm(9) + anywhere(9),
        out_specs=vm(len(outs)),
        scratch_shapes=scratch,
        compiler_params=params(3),
        name="enc_backward",
    )(res, x, gains, proj, mid, top, glow, gd_own, gd_far, dsmall, *hbm)


def place_kernel(n, *refs):
    for i in range(n):
        refs[n + i][...] = refs[i][...]


def place_outputs(arrays):
    n = len(arrays)
    return pl.pallas_call(
        functools.partial(place_kernel, n),
        out_shape=[sds(a.shape, a.dtype) for a in arrays],
        in_specs=vm(n),
        out_specs=vm(n),
        compiler_params=pltpu.CompilerParams(vmem_limit_bytes=60 << 20),
        name="place_outputs",
    )(*arrays)


def position_table(count, quarter):
    freq = (np.float32(10000.0) ** (-np.arange(quarter, dtype=np.float32) / np.float32(quarter))).astype(np.float32)
    angle = (np.arange(count, dtype=np.float32)[:, None] * freq[None, :]).astype(np.float32).astype(np.float64)
    return np.concatenate([np.sin(angle), np.cos(angle)], axis=1).astype(np.float32)


def per_device(
    x_visible,
    resolution,
    visible_index,
    enc_qkv_w,
    enc_out_w,
    enc_up_w,
    enc_down_w,
    enc_gains,
    enc_shifts,
    projection,
    mask_token,
    dec_qkv_w,
    dec_out_w,
    dec_up_w,
    dec_down_w,
    dec_gains,
    dec_shifts,
    cotangent,
):
    dp = lax.axis_size("dp")
    over = ("section", "dp")
    er, dr = enc_qkv_w.shape[0], dec_qkv_w.shape[0]
    de, dd = projection.shape
    ec, dc = enc_qkv_w.shape[2], dec_qkv_w.shape[2]
    gather = er % 16 == 0 and dr % 16 == 0
    if gather:
        shards = [
            jnp.transpose(enc_qkv_w, (1, 0, 2)),
            enc_out_w,
            enc_up_w,
            enc_down_w.T,
            jnp.transpose(dec_qkv_w, (1, 0, 2)),
            dec_out_w.T,
        ]
        e_in, f_in = dec_up_w, dec_down_w.T
    else:
        whole = [
            lax.all_gather(w, over, axis=0, tiled=True)
            for w in (
                jnp.concatenate([enc_qkv_w.reshape(er, 3 * ec), enc_out_w.T], axis=1),
                enc_up_w,
                enc_down_w.T,
                jnp.concatenate([dec_qkv_w.reshape(dr, 3 * dc), dec_out_w.T], axis=1),
                dec_up_w,
                dec_down_w.T,
            )
        ]
        shards, (e_in, f_in) = whole[:4], whole[4:]
    weights, saved = enc_forward(
        dp,
        gather,
        resolution,
        x_visible,
        enc_gains,
        enc_shifts,
        projection,
        shards,
        de,
        dd,
        enc_up_w.shape[1],
        dec_up_w.shape[1],
    )
    table = jnp.asarray(position_table(COLS_BIG, dd // 4))
    out, glow, gd_own, gd_far, ge, gf, dsmall = decoder(
        dp,
        gather,
        resolution,
        visible_index,
        saved[8],
        table,
        cotangent,
        dec_gains,
        dec_shifts,
        mask_token[None, :],
        weights[3],
        e_in,
        f_in,
    )
    back = enc_backward(
        dp,
        gather,
        resolution,
        x_visible,
        enc_gains,
        projection,
        weights[:3],
        saved[:8],
        glow,
        gd_own,
        gd_far,
        dsmall,
        ec,
        dc,
    )
    if gather:
        got = place_outputs((out, ge, gf) + tuple(back))
        out, ge, gf, gin, gqkv, go, gb, gc, hqkv, ho, eg, es, pg, mg, dg, ds = got
        gqkv = jnp.transpose(gqkv, (1, 0, 2))
        hqkv = jnp.transpose(hqkv, (1, 0, 2))
        ho = ho.T
    else:
        gin, ga, _, gb, gc, hd, _, eg, es, pg, mg, dg, ds = back
        ga, gb, gc, hd, ge, gf = [
            lax.psum_scatter(g, over, scatter_dimension=0, tiled=True) for g in (ga, gb, gc, hd, ge, gf)
        ]
        eg, es, pg, mg, dg, ds = lax.psum((eg, es, pg, mg, dg, ds), ("section", "dp", "mp"))
        gqkv, go = ga[:, : 3 * ec].reshape(er, 3, ec), ga[:, 3 * ec :].T
        hqkv, ho = hd[:, : 3 * dc].reshape(dr, 3, dc), hd[:, 3 * dc :].T
    return (out, gin, gqkv, go, gb, gc.T, eg, es, pg, mg[0], hqkv, ho, ge, gf.T, dg, ds)


def solution(mesh):
    matrix_in = P(("section", "dp"), "mp")
    matrix_out = P("mp", ("section", "dp"))
    qkv = P(("section", "dp"), None, "mp")
    return jax.shard_map(
        per_device,
        mesh=mesh,
        in_specs=(
            P("dp", "mp", None),
            P("dp"),
            P("dp", None),
            qkv,
            matrix_out,
            matrix_in,
            matrix_out,
            P(),
            P(),
            P(),
            P(),
            qkv,
            matrix_out,
            matrix_in,
            matrix_out,
            P(),
            P(),
            P("dp", "mp", None),
        ),
        out_specs=(
            P("dp", "mp", "section"),
            P("dp", "mp", "section"),
            qkv,
            matrix_out,
            matrix_in,
            matrix_out,
            P(),
            P(),
            P(),
            P(),
            qkv,
            matrix_out,
            matrix_in,
            matrix_out,
            P(),
            P(),
        ),
        check_vma=False,
    )
```

```python
import functools
import math

import jax
import jax.numpy as jnp
import numpy as np
from jax import lax
from jax.experimental import pallas as pl
from jax.experimental.pallas import tpu as pltpu
from jax.sharding import PartitionSpec as P

HD_ENC = 64
HD_DEC = 32
COLS_SMALL = 32
COLS_BIG = 64
PATCHES = 2048
SMALL_PATCHES = 512
VIS = 512
VIS_SMALL = 128

MESH = pl.DeviceIdType.MESH
bf = jnp.bfloat16
f32 = jnp.float32
LOG2E = 1.4426950408889634
NEG = -1e30


def nn(a, b):
    return lax.dot_general(a, b, (((1,), (0,)), ((), ())), preferred_element_type=f32)


def nt(a, b):
    return lax.dot_general(a, b, (((1,), (1,)), ((), ())), preferred_element_type=f32)


def tn(a, b):
    return lax.dot_general(a, b, (((0,), (0,)), ((), ())), preferred_element_type=f32)


def norm_stats(stream):
    centre = stream - jnp.mean(stream, axis=-1, keepdims=True)
    inverse = lax.rsqrt(jnp.mean(centre * centre, axis=-1, keepdims=True) + 1e-06)
    return centre * inverse, inverse


def normalize(stream, gain, shift):
    scaled, _ = norm_stats(stream)
    return scaled * gain + shift


def normalize_back(stream, gain, grad_out):
    scaled, inverse = norm_stats(stream)
    f = grad_out * gain
    grad_in = inverse * (
        f
        - jnp.mean(f, axis=-1, keepdims=True)
        - scaled * jnp.mean(f * scaled, axis=-1, keepdims=True)
    )
    return (
        grad_in,
        jnp.sum(grad_out * scaled, axis=0, keepdims=True),
        jnp.sum(grad_out, axis=0, keepdims=True),
    )


def gelu_and_slope(a):
    x = jnp.abs(a) * 0.7071067811865476
    t = 1.0 / (1.0 + 0.3275911 * x)
    e = jnp.exp2(x * x * (-LOG2E))
    poly = ((((1.061405429 * t - 1.453152027) * t + 1.421413741) * t - 0.284496736) * t + 0.254829592) * t
    tail = 0.5 * poly * e
    phi = jnp.where(a >= 0, 1.0 - tail, tail)
    return a * phi, phi + a * e * 0.3989422804014327


class Ctx:
    def __init__(self, ss, rs, dp):
        self.ss, self.rs, self.n, self.dp = ss, rs, 0, dp
        self.s = lax.axis_index("section")
        self.d = lax.axis_index("dp")
        self.m = lax.axis_index("mp")
        m = self.m
        self.lo = lax.rem(m, 2)
        self.hi = m // 2
        self.m1 = m + 1 - 2 * self.lo
        self.m2 = lax.rem(m + 2, 4)
        self.m3 = lax.rem(self.m1 + 2, 4)
        self.core = {"mp": self.m1}
        self.y = {"mp": self.m2}
        self.x = {"section": 1 - self.s}
        self.pending = []

    def z(self, k):
        return {"dp": lax.rem(self.d + k, self.dp)}

    def barrier(self, peers):
        b = pltpu.get_barrier_semaphore()
        for p in peers:
            pl.semaphore_signal(b, inc=1, device_id=p, device_id_type=MESH)
        pl.semaphore_wait(b, len(peers))

    def send(self, src, dst, dev):
        i = self.n
        self.n += 1
        c = pltpu.make_async_remote_copy(
            src_ref=src,
            dst_ref=dst,
            send_sem=self.ss.at[i],
            recv_sem=self.rs.at[i],
            device_id=dev,
            device_id_type=MESH,
        )
        c.start()
        self.pending.append(c)
        return c

    def sent(self, c):
        c.wait_send()
        self.pending = [p for p in self.pending if p is not c]

    def drain(self):
        for c in self.pending:
            c.wait_send()
        self.pending = []


class GatherMp:
    def __init__(self, cx, buf):
        self.cx, self.buf = cx, buf
        m = cx.m
        self.c2 = cx.send(buf.at[m], buf.at[m], cx.y)
        self.c1 = cx.send(buf.at[m], buf.at[m], cx.core)

    def forward(self):
        cx, buf = self.cx, self.buf
        self.c2.wait_recv()
        self.c3 = cx.send(buf.at[cx.m2], buf.at[cx.m2], cx.core)

    def near(self):
        self.c1.wait_recv()

    def far(self):
        self.c3.wait_recv()

    def finish(self):
        self.forward()
        self.near()
        self.far()


class ReduceMp:
    def __init__(self, cx, part, stage, recv):
        self.cx, self.part, self.stage, self.recv = cx, part, stage, recv
        stage[0] = part[cx.m3].astype(bf)
        self.c3 = cx.send(stage.at[0], recv.at[0], cx.core)
        stage[1] = part[cx.m1].astype(bf)
        self.c1 = cx.send(stage.at[1], recv.at[1], cx.core)

    def middle(self):
        cx = self.cx
        self.c3.wait_recv()
        self.stage[2] = (self.part[cx.m2] + self.recv[0].astype(f32)).astype(bf)
        self.c2 = cx.send(self.stage.at[2], self.recv.at[2], cx.y)

    def finish(self):
        self.c1.wait_recv()
        own = self.part[self.cx.m] + self.recv[1].astype(f32)
        self.c2.wait_recv()
        return own + self.recv[2].astype(f32)


def reduce_mp(cx, part, stage, recv):
    r = ReduceMp(cx, part, stage, recv)
    r.middle()
    return r.finish()


class GatherW:
    def __init__(self, cx, shard, whole):
        self.cx, self.whole, self.rows = cx, whole, shard.shape[0]
        own = self.at(cx.s, cx.d)
        self.zs = [cx.send(shard, own, cx.z(k)) for k in range(1, cx.dp)]
        self.xs = [cx.send(shard, own, cx.x)]
        own[...] = shard[...]

    def at(self, s, d):
        start = (s * self.cx.dp + d) * self.rows
        return self.whole.at[pl.ds(pl.multiple_of(start, 16), self.rows)]

    def forward(self):
        cx = self.cx
        for k in range(1, cx.dp):
            self.zs[k - 1].wait_recv()
            block = self.at(cx.s, lax.rem(cx.d + cx.dp - k, cx.dp))
            self.xs.append(cx.send(block, block, cx.x))

    def finish(self):
        for c in self.xs:
            c.wait_recv()


class RelayW:
    def __init__(self, cx, shard, whole):
        self.cx, self.whole, self.rows = cx, whole, shard.shape[0]
        dp, d = cx.dp, cx.d
        self.base = cx.n
        cx.n += 4 * dp
        self.own = self.at(cx.s, d)

        @pl.when(d < dp - 1)
        def _():
            self.make(shard, self.own, 1, {"dp": d + 1}).start()

        @pl.when(d > 0)
        def _():
            self.make(shard, self.own, dp + 1, {"dp": d - 1}).start()

        self.make(shard, self.own, 2 * dp, cx.x).start()
        self.own[...] = shard[...]

    def at(self, s, d):
        start = (s * self.cx.dp + d) * self.rows
        return self.whole.at[pl.ds(pl.multiple_of(start, 16), self.rows)]

    def make(self, src, dst, i, dev):
        cx, i = self.cx, self.base + i
        return pltpu.make_async_remote_copy(
            src_ref=src,
            dst_ref=dst,
            send_sem=cx.ss.at[i],
            recv_sem=cx.rs.at[i],
            device_id=dev,
            device_id_type=MESH,
        )

    def hop(self, k):
        cx, dp, d = self.cx, self.cx.dp, self.cx.d

        @pl.when(d >= k)
        def _():
            b = self.at(cx.s, jnp.maximum(d - k, 0))
            self.make(b, b, k, cx.x).wait_recv()

            @pl.when(d < dp - 1)
            def _():
                self.make(b, b, k + 1, {"dp": d + 1}).start()

            self.make(b, b, 2 * dp + k, cx.x).start()

        @pl.when(d + k < dp)
        def _():
            b = self.at(cx.s, jnp.minimum(d + k, dp - 1))
            self.make(b, b, dp + k, cx.x).wait_recv()

            @pl.when(d > 0)
            def _():
                self.make(b, b, dp + k + 1, {"dp": d - 1}).start()

            self.make(b, b, 3 * dp + k, cx.x).start()

    def finish(self):
        cx, dp, d = self.cx, self.cx.dp, self.cx.d
        other = lambda e: self.at(1 - cx.s, jnp.clip(e, 0, dp - 1))
        self.make(self.own, other(d), 2 * dp, cx.x).wait_recv()
        for k in range(1, dp):

            @pl.when(d >= k)
            def _():
                self.make(self.own, other(d - k), 2 * dp + k, cx.x).wait_recv()

            @pl.when(d + k < dp)
            def _():
                self.make(self.own, other(d + k), 3 * dp + k, cx.x).wait_recv()

    def drain(self):
        cx, dp, d = self.cx, self.cx.dp, self.cx.d
        own = self.own
        self.make(own, own, 2 * dp, cx.x).wait_send()
        for k in range(1, dp):

            @pl.when(d >= k)
            def _():
                self.make(own, own, 2 * dp + k, cx.x).wait_send()

            @pl.when(d + k < dp)
            def _():
                self.make(own, own, 3 * dp + k, cx.x).wait_send()

            @pl.when((d < dp - 1) & (d >= k - 1))
            def _():
                self.make(own, own, k, cx.x).wait_send()

            @pl.when((d > 0) & (d + k - 1 < dp))
            def _():
                self.make(own, own, dp + k, cx.x).wait_send()


class Local:
    def __init__(self, sems):
        self.sems, self.n, self.pending = sems, 0, []

    def start(self, src, dst):
        c = pltpu.make_async_copy(src, dst, self.sems.at[self.n])
        self.n += 1
        c.start()
        self.pending.append(c)
        return c

    def drain(self):
        for c in self.pending:
            c.wait()


class ScatterW:
    def __init__(self, cx, rows, own, xs, xr, zs, zr):
        self.cx, self.rows, self.own = cx, rows, own
        self.xs, self.xr, self.zs, self.zr = xs, xr, zs, zr

    def start(self, theirs):
        self.xs[...] = theirs.astype(bf)
        self.c = self.cx.send(self.xs, self.xr, self.cx.x)

    def at(self, e):
        return pl.ds(pl.multiple_of(e * self.rows, 16), self.rows)

    def near(self):
        cx = self.cx
        self.c.wait_recv()
        low = lax.rem(cx.d, 2)
        for j in range(2):
            at = self.at(2 * j + 1 - low)
            self.zs[j] = (self.own[at, :] + self.xr[at, :].astype(f32)).astype(bf)
        self.c = cx.send(self.zs.at[pl.ds(0, 2)], self.zr.at[pl.ds(0, 2)], {"dp": cx.d + 1 - 2 * low})

    def far(self):
        cx = self.cx
        low, high = lax.rem(cx.d, 2), cx.d // 2
        self.c.wait_recv()
        at = self.at(2 * (1 - high) + low)
        total = self.own[at, :] + self.xr[at, :].astype(f32) + self.zr[1 - high].astype(f32)
        self.zs[2] = total.astype(bf)
        self.c = cx.send(self.zs.at[2], self.zr.at[2], cx.z(2))

    def finish(self):
        at = self.at(self.cx.d)
        own = self.own[at, :] + self.xr[at, :].astype(f32) + self.zr[self.cx.d // 2].astype(f32)
        self.c.wait_recv()
        return own + self.zr[2].astype(f32)


def scatter_scratch(dp, rows, cols):
    half = dp * rows
    return [
        pltpu.VMEM((half, cols), bf),
        pltpu.VMEM((half, cols), bf),
        pltpu.VMEM((3, rows, cols), bf),
        pltpu.VMEM((3, rows, cols), bf),
    ]


def iota(shape, dim):
    return lax.broadcasted_iota(jnp.int32, shape, dim)


def enc_forward_kernel(dp, gather, *refs):
    it = iter(refs)
    take = lambda n: [next(it) for _ in range(n)]
    res, x_all, gains, shifts, proj = take(5)
    if gather:
        eqkv, eout, eup, edown, dqkv, dout = take(6)
        ha, hb, hc = take(3)
    else:
        wa, wb, wc, wd_in = take(4)
    wd, h1, h2, hq, hctx, hslope, hact, hmid, top_out, low_all = take(10)
    ss, rs, ls, part, stage, recv, n1, n2, qkv, ctx, slope, active, mid_s = take(13)
    if gather:
        wa, wb, wc, sa, sd, sdf = take(6)
    cx = Ctx(ss, rs, dp)
    lc = Local(ls)
    peers = [cx.core, cx.y]
    if gather:
        peers += [cx.x] + [cx.z(k) for k in range(1, dp)]
        wide = eqkv.shape[2]
        for t in range(3):
            sa[:, t * wide : (t + 1) * wide] = eqkv[t]
        sa[:, 3 * wide :] = eout[...].astype(f32).T.astype(bf)
        wide = dqkv.shape[2]
        for t in range(3):
            sd[:, t * wide : (t + 1) * wide] = dqkv[t]
        sd[:, 3 * wide : 4 * wide] = dout[...]
        both = 4 * wide
    cx.barrier(peers)
    if gather:
        cut = sa.shape[1] // 2
        ga = RelayW(cx, sa.at[:, pl.ds(0, cut)], wa.at[:, pl.ds(0, cut)])
        ga2 = RelayW(cx, sa.at[:, pl.ds(cut, cut)], wa.at[:, pl.ds(cut, cut)])
    stream = x_all[cx.s].astype(f32)
    n1[cx.m] = normalize(stream, gains[0:1, :], shifts[0:1, :]).astype(bf)
    g1 = GatherMp(cx, n1)
    if gather:
        csd = cx.send(sd.at[:, pl.ds(0, both)], sdf, cx.y)
        ga.hop(1)
        ga2.hop(1)
        ga.hop(2)
        ga2.hop(2)
        gb = RelayW(cx, eup, wb)
    g1.finish()
    lc.start(n1, h1)
    if gather:
        ga.hop(3)
        ga2.hop(3)
        gc = RelayW(cx, edown, wc)
        gb.hop(1)
        ga.finish()
        ga2.finish()
        lc.start(wa, ha)
    rows = n1.shape[1]
    total = 4 * rows
    width = n1.shape[2]
    n1_all = n1[...].reshape(total, width)
    qkv[...] = nn(n1_all, wa[...]).astype(bf)
    lc.start(qkv, hq)
    if gather:
        gb.hop(2)
        gc.hop(1)
        csd.wait_recv()
        sd[:, both:] = sdf[...]
        gd = RelayW(cx, sd, wd)
    shown = jnp.where(res[cx.s] == 1, VIS, VIS_SMALL)
    bias = jnp.where(iota((1, total), 1) < shown, 0.0, NEG)
    scale2 = HD_ENC**-0.5 * LOG2E
    heads = (width // 4) // HD_ENC
    pieces = [jnp.zeros((total, HD_ENC), bf)]
    for h in range(heads):
        q = qkv[:, h * HD_ENC : (h + 1) * HD_ENC]
        k = qkv[:, (heads + h) * HD_ENC : (heads + h + 1) * HD_ENC]
        v = qkv[:, (2 * heads + h) * HD_ENC : (2 * heads + h + 1) * HD_ENC]
        sc = nt(q, k) + bias
        top = jnp.max(sc, axis=1, keepdims=True)
        e = jnp.exp2((sc - top) * scale2)
        tot = jnp.sum(e, axis=1, keepdims=True)
        pieces.append((nn(e.astype(bf), v) / tot).astype(bf))
        if gather and h == 0:
            gb.hop(3)
        if gather and h == 1:
            gc.hop(2)
    ctx[...] = jnp.concatenate(pieces, axis=1)
    lc.start(ctx, hctx)
    cpad = ctx.shape[1]
    part[...] = nt(ctx[...], wa[:, width - cpad :]).reshape(part.shape)
    r1 = ReduceMp(cx, part, stage.at[0], recv.at[0])
    if gather:
        gd.hop(1)
    r1.middle()
    if gather:
        gc.hop(3)
    mid = stream + r1.finish()
    mid_s[...] = mid
    lc.start(mid_s, hmid)
    n2[cx.m] = normalize(mid, gains[1:2, :], shifts[1:2, :]).astype(bf)
    g2 = GatherMp(cx, n2)
    if gather:
        gd.hop(2)
        gb.finish()
        lc.start(wb, hb)
    g2.finish()
    lc.start(n2, h2)
    hid = nn(n2[...].reshape(total, width), wb[...])
    act, slo = gelu_and_slope(hid)
    active[...] = act.astype(bf)
    slope[...] = slo.astype(bf)
    lc.start(active, hact)
    lc.start(slope, hslope)
    if gather:
        gc.finish()
        lc.start(wc, hc)
    part[...] = nt(active[...], wc[...]).reshape(part.shape)
    r2 = ReduceMp(cx, part, stage.at[1], recv.at[1])
    r2.middle()
    if gather:
        gd.hop(3)
    top = (mid_s[...] + r2.finish()).astype(bf)
    top_out[...] = top
    low_all[cx.m] = nn(top, proj[...]).astype(bf)
    g3 = GatherMp(cx, low_all)
    if gather:
        gd.finish()
    else:
        both = wd_in.shape[1]
        wd[:, :both] = wd_in[...]
        cd = cx.send(wd_in, wd.at[:, pl.ds(both, both)], cx.y)
        cd.wait_recv()
    g3.finish()
    cx.drain()
    if gather:
        for g in (ga, ga2, gb, gc, gd):
            g.drain()
    lc.drain()


def vm(n):
    return [pl.BlockSpec(memory_space=pltpu.VMEM)] * n


def anywhere(n):
    return [pl.BlockSpec(memory_space=pl.ANY)] * n


SMEM = pl.BlockSpec(memory_space=pltpu.SMEM)


def sds(shape, dtype):
    return jax.ShapeDtypeStruct(shape, dtype)


def params(cid):
    return pltpu.CompilerParams(collective_id=cid, has_side_effects=True, vmem_limit_bytes=60 << 20)


def enc_forward(dp, gather, res, x, gains, shifts, proj, shards, de, dd, wide, dwide):
    rows, width = x.shape[1:]
    total = 4 * rows
    slots = (4, rows, width)
    V = pltpu.VMEM
    outs = []
    if gather:
        outs += [sds((de, de), bf), sds((de, wide), bf), sds((de, wide), bf)]
    outs += [sds((dd, 2 * dwide), bf)]
    big = [sds(slots, bf), sds(slots, bf), sds((total, width), bf), sds((total, 256), bf)]
    big += [sds((total, wide), bf), sds((total, wide), bf), sds((rows, width), f32)]
    outs += big + [sds((rows, width), bf), sds((4, rows, dd), bf)]
    scratch = [
        pltpu.SemaphoreType.DMA((112,)),
        pltpu.SemaphoreType.DMA((112,)),
        pltpu.SemaphoreType.DMA((16,)),
        V(slots, f32),
        V((2, 3, rows, width), bf),
        V((2, 3, rows, width), bf),
    ] + [V(b.shape, b.dtype) for b in big]
    if gather:
        scratch += [V(o.shape, bf) for o in outs[:3]]
        scratch += [V((shards[2].shape[0], de), bf), V((shards[5].shape[0], 2 * dwide), bf)]
        scratch += [V((shards[5].shape[0], dwide), bf)]
    got = pl.pallas_call(
        functools.partial(enc_forward_kernel, dp, gather),
        out_shape=outs,
        in_specs=[SMEM] + vm(4 + len(shards)),
        out_specs=anywhere(3 if gather else 0) + vm(1) + anywhere(7) + vm(2),
        scratch_shapes=scratch,
        compiler_params=params(1),
        name="enc_forward",
    )(res, x, gains, shifts, proj, *shards)
    if not gather:
        got = list(shards[:3]) + list(got)
    return got[:4], got[4:]


def dec_kernel(dp, gather, *refs):
    it = iter(refs)
    take = lambda n: [next(it) for _ in range(n)]
    res, chosen, low_all, table, cot, gains, shifts, token, wd_both, e_in, f_in = take(11)
    out, glow, gd, out_e, out_f, small = take(6)
    ss, rs, we_both, wf_both, place_s, own_e, own_f, yst, yrc = take(9)
    if gather:
        se, sf, sfar = take(3)
        scat = (take(4), take(4))
    unit = wd_both.shape[1] // 2
    wd, we, wf = [[w.at[:, pl.ds(unit * g, unit)] for g in range(2)] for w in (wd_both, we_both, wf_both)]
    (n1, n2, gm, gmid_low, qg, kg, vg, gg, vtx, kt, dqt, lse, acc_s, top_s, ctx, active, slope) = take(17)
    ct = dqt
    (dkv, mid_s, start_s, res_s, part, fstage, frecv, far, prod, pstage, precv, masks) = take(12)
    sc_s, mx_s = take(2), take(2)
    cx = Ctx(ss, rs, dp)
    cx.barrier([cx.core, cx.y, cx.x] + ([cx.z(k) for k in range(1, dp)] if gather else []))
    rows, width = n1.shape[1:]
    m, lo, hi, s = cx.m, cx.lo, cx.hi, cx.s
    big = res[s] == 1
    shown = jnp.where(big, VIS, VIS_SMALL)
    filled = jnp.where(big, PATCHES, SMALL_PATCHES)
    pos_col = iota((rows, 1), 0) + m * rows
    live = jnp.where(pos_col < filled, 1.0, 0.0)
    gm[lo] = (cot[s].astype(f32) * live).astype(bf)
    cgm = cx.send(gm.at[lo], gm.at[lo], cx.core)
    if gather:
        cef = [cx.send(e_in, sfar.at[0], cx.y), cx.send(f_in, sfar.at[1], cx.y)]
        se[:, :unit] = e_in[...]
        sf[:, :unit] = f_in[...]
    else:
        we[0][...] = e_in[...]
        wf[0][...] = f_in[...]
        cef = [cx.send(e_in, we[1], cx.y), cx.send(f_in, wf[1], cx.y)]
    vis = chosen.shape[-1]
    place = jnp.where((pos_col == chosen[pl.ds(s, 1), :]) & (iota((1, vis), 1) < shown), 1.0, 0.0)
    seen = jnp.sum(place, axis=1, keepdims=True)
    weight = live - seen
    place_s[...] = place.astype(bf)
    placed = nn(place_s[...], low_all[...].reshape(vis, width))
    half = width // 2
    nb, ns = rows // COLS_BIG, rows // COLS_SMALL
    rb = table[pl.ds(pl.multiple_of(m * nb, 8), nb), :]
    rsm = table[pl.ds(pl.multiple_of(m * ns, 8), ns), :]
    big_rows = jnp.broadcast_to(rb[:, None, :], (nb, COLS_BIG, half)).reshape(rows, half)
    small_rows = jnp.broadcast_to(rsm[:, None, :], (ns, COLS_SMALL, half)).reshape(rows, half)
    big_cols = jnp.broadcast_to(table[0:COLS_BIG, :][None], (nb, COLS_BIG, half)).reshape(rows, half)
    small_cols = jnp.broadcast_to(table[0:COLS_SMALL, :][None], (ns, COLS_SMALL, half)).reshape(rows, half)
    base = placed + weight * token[...]
    start_s[:, :half] = base[:, :half] + live * jnp.where(big, big_rows, small_rows)
    start_s[:, half:] = base[:, half:] + live * jnp.where(big, big_cols, small_cols)
    n1[m] = normalize(start_s[...], gains[0:1, :], shifts[0:1, :]).astype(bf)
    g1 = GatherMp(cx, n1)

    lane = iota((1, 256), 1)
    for j in range(4):
        head_lane = (lane < 128) & (lane // 32 == j)
        off = lane - (128 + 8 * j)
        masks[0, j] = jnp.where(head_lane | ((off >= 0) & (off < 3)) | (lane == 160), 1.0, 0.0).astype(bf)
        masks[1, j] = jnp.where(head_lane | ((off >= 0) & (off < 2)), 1.0, 0.0).astype(bf)
    aug = iota((1, 128), 1)
    total = 4 * rows
    key_bias = jnp.where(iota((total, 1), 0) < filled, 0.0, NEG)
    kaug = jnp.where(aug == 32, key_bias, jnp.where(aug < 32, 1.0, 0.0)).astype(bf)
    vaug = jnp.broadcast_to(jnp.where(aug < 32, 1.0, 0.0), (total, 128)).astype(bf)
    qaug = jnp.broadcast_to(jnp.where(aug == 32, 1.0, 0.0), (2 * rows, 128)).astype(bf)
    for g in range(2):
        kg[g, :, 128:] = kaug
        vg[g, :, 128:] = vaug
        qg[g, :, 128:] = qaug
    vtx[:, 32:, :] = jnp.ones((8, 16, total), bf)

    def keys_values(i, groups):
        at = pl.ds(pl.multiple_of(i * rows, 128), rows)
        for g in groups:
            kv = nn(n1[i], wd[g][:, 128:384])
            kg[g, at, :128] = kv[:, :128].astype(bf)
            vg[g, at, :128] = kv[:, 128:].astype(bf)
            kvt = kv.T.astype(bf)
            for j in range(4):
                kt[4 * g + j, :, at] = kvt[32 * j : 32 * j + 32]
                vtx[4 * g + j, 0:32, at] = kvt[128 + 32 * j : 160 + 32 * j]

    g1.near()

    def near_rows_in(g):
        for r in range(2):
            qg[g, r * rows : (r + 1) * rows, :128] = nn(n1[2 * hi + r], wd[g][:, :128]).astype(bf)
        keys_values(cx.m, (g,))
        keys_values(cx.m1, (g,))

    if gather:
        gats = []
        for i, (sh, w) in enumerate(((se, we_both), (sf, wf_both))):
            cef[i].wait_recv()
            sh[:, unit:] = sfar[i]
            gats.append(GatherW(cx, sh, w))
    near_rows_in(0)
    near_rows_in(1)
    c2 = HD_DEC**-0.5 * LOG2E

    def score(h, i, to):
        g, j = h // 4, lax.rem(h, 4)
        at = pl.ds(pl.multiple_of(i * rows, 128), rows)
        sc = nt(kg[g, at, :] * masks[0, j], qg[g])
        sc_s[to][...] = sc
        mx_s[to][...] = jnp.max(sc, axis=0, keepdims=True)

    def head_pass(first, last, blocks, heads):
        def body(h, _):
            g, j = h // 4, lax.rem(h, 4)
            if first:
                top, acc = None, None
            else:
                top, acc = top_s[h], acc_s[h]
            ahead = ((h, blocks[1]), (jnp.minimum(h + 1, 7), blocks[0]))
            for n, i in enumerate(blocks):
                at = pl.ds(pl.multiple_of(i * rows, 128), rows)
                mj = mx_s[n][...]
                new = mj if top is None else jnp.maximum(top, mj)
                score(*ahead[n], 1 - n)
                p = jnp.exp2((sc_s[n][...] - new) * c2).astype(bf)
                o = nn(vtx[h, :, at], p)
                acc = o if acc is None else acc * jnp.exp2((top - new) * c2) + o
                top = new
            if last:
                tot = acc[32:33, :]
                ct[h] = acc[:32, :] / tot
                at = pl.ds(pl.multiple_of(8 * j, 8), 8)
                lse[g, at, :] = jnp.broadcast_to(top + jnp.log(tot) * (LOG2E / c2), (8, top.shape[1]))
            else:
                top_s[h] = top
                acc_s[h] = acc
            return 0

        lax.fori_loop(*heads, body, 0)

    score(jnp.int32(0), cx.m, 0)
    head_pass(True, False, (cx.m, cx.m1), (0, 4))
    g1.forward()
    if gather:
        gats[0].forward()
    head_pass(True, False, (cx.m, cx.m1), (4, 8))
    keys_values(cx.m2, (0, 1))
    g1.far()
    keys_values(cx.m3, (0, 1))
    score(jnp.int32(0), cx.m2, 0)
    head_pass(False, True, (cx.m2, cx.m3), (0, 4))
    if gather:
        gats[1].forward()
    head_pass(False, True, (cx.m2, cx.m3), (4, 8))
    for g in range(2):
        ctx[:, 128 * g : 128 * g + 128] = ct[4 * g : 4 * g + 4].reshape(128, 2 * rows).T.astype(bf)

    def chip_rows(r):
        return pl.ds(pl.multiple_of(r * rows, 128), rows)

    def out_rows(r):
        return sum(nt(ctx[chip_rows(r), 128 * g : 128 * g + 128], wd[g][:, 384:]) for g in range(2))

    fstage[0] = out_rows(1 - lo).astype(bf)
    co = cx.send(fstage.at[0], frecv.at[0], cx.core)
    mid = start_s[...] + out_rows(lo)
    co.wait_recv()
    mid = mid + frecv[0].astype(f32)
    mid_s[...] = mid
    n2[lo] = normalize(mid, gains[1:2, :], shifts[1:2, :]).astype(bf)
    cn2 = cx.send(n2.at[lo], n2.at[lo], cx.core)

    def mlp_rows(r):
        at = chip_rows(r)
        x = n2[r]
        y = None
        for g in range(2):
            a, b = gelu_and_slope(nn(x, we[g][...]))
            cols = slice(width * g, width * (g + 1))
            a = a.astype(bf)
            active[at, cols] = a
            slope[at, cols] = b.astype(bf)
            t = nt(a, wf[g][...])
            y = t if y is None else y + t
        return y

    if gather:
        for q in gats:
            q.finish()
    else:
        for c in cef:
            c.wait_recv()
    res_s[...] = mlp_rows(lo)
    cn2.wait_recv()
    fstage[1] = mlp_rows(1 - lo).astype(bf)
    c = cx.send(fstage.at[1], frecv.at[1], cx.core)

    cgm.wait_recv()

    def mlp_back_rows(r):
        at = chip_rows(r)
        y = None
        for g in range(2):
            cols = slice(width * g, width * (g + 1))
            ga = nn(gm[r], wf[g][...])
            gh = (ga * slope[at, cols].astype(f32)).astype(bf)
            slope[at, cols] = gh
            t = nt(gh, we[g][...])
            y = t if y is None else y + t
        return y

    fstage[2] = mlp_back_rows(1 - lo).astype(bf)
    cb = cx.send(fstage.at[2], frecv.at[2], cx.core)
    c.wait_recv()
    result = mid_s[...] + res_s[...] + frecv[1].astype(f32)
    produced = (result * live).astype(bf)
    prod[0] = produced[:, :half]
    prod[1] = produced[:, half:]
    out[s] = prod[s]
    cprod = cx.send(prod.at[1 - s], out.at[s], cx.x)
    own = mlp_back_rows(lo)
    half_rows = width // 2

    def start_scatter(left, right, own, i, out):
        def rows_of(sec):
            at = pl.ds(pl.multiple_of(sec * half_rows, 128), half_rows)
            return tn(left[:, :, at].reshape(2 * rows, half_rows), right[...])

        if gather:
            q = ScatterW(cx, half_rows // dp, own, *scat[i])
            q.start(rows_of(1 - s))
            own[...] = rows_of(s)
            return q
        for sec in (0, 1):
            t = rows_of(jnp.int32(sec))
            at = slice(sec * half_rows, (sec + 1) * half_rows)
            out[at] = t[:, :unit]
            yst[i, at] = t[:, unit:].astype(bf)
        return cx.send(yst.at[i], yrc.at[i], cx.y)

    q_f = start_scatter(gm, active, own_f, 0, out_f)
    cb.wait_recv()
    grad_mid, gain_mid, shift_mid = normalize_back(mid_s[...], gains[1:2, :], own + frecv[2].astype(f32))
    gmid = gm[lo].astype(f32) + grad_mid
    mid_s[...] = gmid
    gmid_low[lo] = gmid.astype(bf)
    cgmid = cx.send(gmid_low.at[lo], gmid_low.at[lo], cx.core)
    q_e = start_scatter(n2, slope, own_e, 1, out_e)
    cgmid.wait_recv()
    gmid_all = gmid_low[...].reshape(2 * rows, width)
    sel = jnp.where(iota((128, 128), 0) // 32 == iota((128, 128), 1) // 8, 1.0, 0.0).astype(bf)
    lane128 = iota((1, 128), 1)
    t8 = lax.rem(lane128, 8)
    for g in range(2):
        gcg = nn(gmid_all, wd[g][:, 384:]).astype(bf)
        gg[g, :, :128] = gcg
        prodd = gcg.astype(f32) * ctx[:, 128 * g : 128 * g + 128].astype(f32)
        ph = prodd.astype(bf)
        plow = (prodd - ph.astype(f32)).astype(bf)
        delta = nn(ph, sel) + nn(plow, sel)
        dh = delta.astype(bf).astype(f32)
        daug = jnp.where(t8 == 0, -dh, jnp.where(t8 == 1, dh - delta, 0.0))
        gg[g, :, 128:] = jnp.where(lane128 < 32, daug, 0.0).astype(bf)
        gd[:, unit * g + 384 : unit * g + 512] = tn(gmid_all, ctx[:, 128 * g : 128 * g + 128])
        lt = jnp.concatenate([lse[g].T, jnp.zeros((2 * rows, 96), f32)], axis=1)
        h1 = lt.astype(bf).astype(f32)
        h2 = (lt - h1).astype(bf).astype(f32)
        h3 = lt - h1 - h2
        laug = jnp.where(t8 == 0, -h1, jnp.where(t8 == 1, -h2, jnp.where(t8 == 2, -h3, 0.0)))
        laug = jnp.where(lane128 == 32, 1.0, jnp.where(lane128 < 32, laug, 0.0))
        qg[g, :, 128:] = laug.astype(bf)

    scale = HD_DEC**-0.5
    dqt[...] = jnp.zeros_like(dqt)
    head_lane = lane128 // 32

    def back_pass(blocks, heads):
        def body(h, _):
            g, j = h // 4, lax.rem(h, 4)
            mine = head_lane == j
            for i in blocks:
                at = pl.ds(pl.multiple_of(i * rows, 128), rows)
                st = nt(kg[g, at, :] * masks[0, j], qg[g])
                dpt = nt(vg[g, at, :] * masks[1, j], gg[g])
                p = jnp.exp2(st * c2)
                ds = (p * dpt).astype(bf)
                dv = nn(p.astype(bf), gg[g, :, :128])
                dk = nn(ds, qg[g, :, :128]) * scale
                dkv[g, at, :128] = jnp.where(mine, dk, dkv[g, at, :128].astype(f32)).astype(bf)
                dkv[g, at, 128:] = jnp.where(mine, dv, dkv[g, at, 128:].astype(f32)).astype(bf)
                dqt[h] += nn(kt[h, :, at], ds)
            return 0

        lax.fori_loop(*heads, body, 0)

    dkv[...] = jnp.zeros_like(dkv)
    back_pass((cx.m2, cx.m3), (0, 4))
    if gather:
        q_f.near()
    back_pass((cx.m2, cx.m3), (4, 8))
    if gather:
        q_f.far()
        q_e.near()

    def far_rows(r):
        at = pl.ds(pl.multiple_of((2 * (1 - hi) + r) * rows, 128), rows)
        return sum(nt(dkv[g, at, :], wd[g][:, 128:384]) for g in range(2))

    cx.sent(co)
    fstage[0] = far_rows(1 - lo).astype(bf)
    cf = cx.send(fstage.at[0], frecv.at[0], cx.core)
    res_s[...] = far_rows(lo)
    back_pass((cx.m, cx.m1), (0, 4))
    cf.wait_recv()
    far[0] = (res_s[...] + frecv[0].astype(f32)).astype(bf)
    cfar = cx.send(far.at[0], far.at[1], cx.y)
    if gather:
        q_e.far()
        t = q_f.finish()
        out_f[...] = t[:, :unit]
        yst[0] = t[:, unit:].astype(bf)
        cyf = cx.send(yst.at[0], yrc.at[0], cx.y)
    back_pass((cx.m, cx.m1), (4, 8))
    if gather:
        t = q_e.finish()
        out_e[...] = t[:, :unit]
        yst[1] = t[:, unit:].astype(bf)
        cye = cx.send(yst.at[1], yrc.at[1], cx.y)
    for g in range(2):
        ctx[:, 128 * g : 128 * g + 128] = (dqt[4 * g : 4 * g + 4].reshape(128, 2 * rows).T * scale).astype(bf)

    def near_rows(r):
        at = pl.ds(pl.multiple_of((2 * hi + r) * rows, 128), rows)
        return sum(
            nt(ctx[chip_rows(r), 128 * g : 128 * g + 128], wd[g][:, :128]) + nt(dkv[g, at, :], wd[g][:, 128:384])
            for g in range(2)
        )

    cx.sent(c)
    fstage[1] = near_rows(1 - lo).astype(bf)
    cn = cx.send(fstage.at[1], frecv.at[1], cx.core)
    near = near_rows(lo)
    n1_chip = n1[pl.ds(2 * hi, 2)].reshape(2 * rows, width)
    t = tn(n1_chip, ctx[...])
    gd[:, :128] = t[:, :128]
    gd[:, unit : unit + 128] = t[:, 128:]
    cn.wait_recv()
    near = near + frecv[1].astype(f32)
    cfar.wait_recv()
    grad_in, gain_in, shift_in = normalize_back(start_s[...], gains[0:1, :], near + far[1].astype(f32))
    gstart = (mid_s[...] + grad_in).astype(bf)
    token_term = jnp.sum(weight * gstart.astype(f32), axis=0, keepdims=True)
    small[0:1] = gain_in
    small[1:2] = gain_mid
    small[2:3] = shift_in
    small[3:4] = shift_mid
    small[4:5] = token_term
    small[5:8] = jnp.zeros((3, width), f32)
    part[...] = tn(place_s[...], gstart).reshape(part.shape)
    reduce = ReduceMp(cx, part, pstage, precv)
    n1_all = n1[...].reshape(total, width)
    gd[:, 128:384] = tn(n1_all, dkv[0])
    reduce.middle()
    gd[:, unit + 128 : unit + 384] = tn(n1_all, dkv[1])
    for c, o, i in ((cyf, out_f, 0), (cye, out_e, 1)) if gather else ((q_f, out_f, 0), (q_e, out_e, 1)):
        c.wait_recv()
        o[...] = o[...] + yrc[i].astype(f32)
    glow[...] = reduce.finish().astype(bf)
    cprod.wait_recv()
    cx.drain()


def decoder(dp, gather, res, chosen, low_all, table, cot, gains, shifts, token, wd, e_in, f_in):
    rows, width = cot.shape[1:]
    vis = chosen.shape[-1]
    total, chip = 4 * rows, 2 * rows
    unit = wd.shape[1] // 2
    half = (width // 2, 2 * unit)
    outs = [
        sds((2, rows, width // 2), bf),
        sds((vis // 4, width), bf),
        sds(wd.shape, f32),
        sds(e_in.shape, f32),
        sds(f_in.shape, f32),
        sds((8, width), f32),
    ]
    V = pltpu.VMEM
    extra = []
    if gather:
        pair = (e_in.shape[0], 2 * unit)
        extra = [V(pair, bf), V(pair, bf), V((2,) + e_in.shape, bf)] + 2 * scatter_scratch(dp, *pair)
    return pl.pallas_call(
        functools.partial(dec_kernel, dp, gather),
        out_shape=outs,
        in_specs=[SMEM] + vm(10),
        out_specs=vm(len(outs)),
        scratch_shapes=[
            pltpu.SemaphoreType.DMA((64,)),
            pltpu.SemaphoreType.DMA((64,)),
            V(wd.shape, bf),
            V(wd.shape, bf),
            V((rows, vis), bf),
            V(half, f32),
            V(half, f32),
            V((2,) + e_in.shape, bf),
            V((2,) + e_in.shape, bf),
        ]
        + extra
        + [
            V((4, rows, width), bf),
            V((2, rows, width), bf),
            V((2, rows, width), bf),
            V((2, rows, width), bf),
            V((2, chip, 256), bf),
            V((2, total, 256), bf),
            V((2, total, 256), bf),
            V((2, chip, 256), bf),
            V((8, 48, total), bf),
            V((8, 32, total), bf),
            V((8, 32, chip), f32),
            V((2, 32, chip), f32),
            V((8, 48, chip), f32),
            V((8, 1, chip), f32),
            V((chip, 256), bf),
            V((chip, 2 * width), bf),
            V((chip, 2 * width), bf),
            V((2, total, 256), bf),
            V((rows, width), f32),
            V((rows, width), f32),
            V((rows, width), f32),
            V((4, vis // 4, width), f32),
            V((3, rows, width), bf),
            V((3, rows, width), bf),
            V((2, rows, width), bf),
            V((2, rows, width // 2), bf),
            V((3, vis // 4, width), bf),
            V((3, vis // 4, width), bf),
            V((2, 4, 1, 256), bf),
            V((rows, chip), f32),
            V((rows, chip), f32),
            V((1, chip), f32),
            V((1, chip), f32),
        ],
        compiler_params=params(2),
        name="decoder",
    )(res, chosen, low_all, table, cot, gains, shifts, token, wd, e_in, f_in)


def enc_backward_kernel(dp, gather, *refs):
    it = iter(refs)
    take = lambda n: [next(it) for _ in range(n)]
    res, x_all, gains, proj, mid, top, glow, gd, dsmall = take(9)
    hbm = take(9)
    gin, out_qkv, out_o, out_b, out_c, out_dqkv, out_do = take(7)
    eg, es, pout, mg, dg, dsh = take(6)
    ss, rs, ls = take(3)
    vmem = take(9)
    gm, gmid_low, gqkv, part, stage, recv, gbuf, yst, yrc, gmid_half = take(10)
    if gather:
        scat = [take(4) for _ in range(5)]
        own_w = take(4)
        smr, smz, pst, prc, pzs, pzr, pacc, pwhole = take(8)
    lc = Local(ls)
    loads = [lc.start(h, v) for h, v in zip(hbm, vmem)]
    wc, slope, wb, active, n2, wa, ctx, qkv, n1 = vmem
    cx = Ctx(ss, rs, dp)
    peers = [cx.core, cx.y, cx.x]
    if gather:
        peers += [cx.z(k) for k in range(1, dp)]
    cx.barrier(peers)
    m, s = cx.m, cx.s
    rows, width = gm.shape[1:]
    total = 4 * rows
    half = width // 2
    g_top = nt(glow[...], proj[...])
    gm[m] = g_top.astype(bf)
    g1 = GatherMp(cx, gm)
    unit_d = gd.shape[1] // 2
    if gather:
        hd = gd.shape[0] // 2
        qd = ScatterW(cx, hd // dp, gbuf, *scat[4])
        qd.start(gd[pl.ds(pl.multiple_of((1 - s) * hd, 16), hd), :])
        gbuf[...] = gd[pl.ds(pl.multiple_of(s * hd, 16), hd), :]
    else:
        yst[...] = gd[:, unit_d:].astype(bf)
        cyd = cx.send(yst, yrc, cx.y)
    p_part = tn(top[...], glow[...])
    if gather:
        pr = ProjSum(cx, pst, prc, pzs, pzr, pacc, pwhole, pout)
        pr.core(p_part)
    else:
        pout[...] = p_part

    def grad_halves(i, terms, out):
        def rows_of(sec):
            at = pl.ds(pl.multiple_of(sec * half, 128), half)
            return sum(tn(left[:, :, at].reshape(total, half), right) for left, right in terms)

        if gather:
            q = ScatterW(cx, half // dp, own_w[i], *scat[i])
            q.start(rows_of(1 - s))
            own_w[i][...] = rows_of(s)
            return q
        for sec in (0, 1):
            out[sec * half : (sec + 1) * half] = rows_of(jnp.int32(sec))

    if gather:
        pr.y()
    g1.finish()
    gm_all = gm[...].reshape(total, width)
    loads[0].wait()
    loads[1].wait()
    gh = (nn(gm_all, wc[...]) * slope[...].astype(f32)).astype(bf)
    loads[2].wait()
    if gather:
        pr.x()
    part[...] = nt(gh, wb[...]).reshape(part.shape)
    r1 = ReduceMp(cx, part, stage.at[0], recv.at[0])
    if gather:
        pr.z()
    r1.middle()
    if gather:
        qd.near()
        pr.back_z()
    loads[3].wait()
    loads[4].wait()
    qc = grad_halves(2, [(gm, active[...])], out_c)
    if gather:
        pr.back_x()
    g_n2 = r1.finish()
    grad_mid, gain_mid, shift_mid = normalize_back(mid[...], gains[1:2, :], g_n2)
    gmid = g_top + grad_mid
    gmid_half[...] = gmid
    gmid_low[m] = gmid.astype(bf)
    g2 = GatherMp(cx, gmid_low)
    if gather:
        qd.far()
    qb = grad_halves(3, [(n2, gh)], out_b)
    g2.finish()
    for c in loads[5:]:
        c.wait()
    gmid_all = gmid_low[...].reshape(total, width)
    cpad = ctx.shape[1]
    cut = width - cpad
    gcx = nn(gmid_all, wa[:, cut:]).astype(bf)
    shown = jnp.where(res[s] == 1, VIS, VIS_SMALL)
    bias = jnp.where(iota((1, total), 1) < shown, 0.0, NEG)
    scale = HD_ENC**-0.5
    scale2 = scale * LOG2E
    heads = (width // 4) // HD_ENC
    for h in range(heads):
        q = qkv[:, h * HD_ENC : (h + 1) * HD_ENC]
        k = qkv[:, (heads + h) * HD_ENC : (heads + h + 1) * HD_ENC]
        v = qkv[:, (2 * heads + h) * HD_ENC : (2 * heads + h + 1) * HD_ENC]
        go = gcx[:, (h + 1) * HD_ENC : (h + 2) * HD_ENC]
        co = ctx[:, (h + 1) * HD_ENC : (h + 2) * HD_ENC]
        scr = nt(q, k) + bias
        e = jnp.exp2((scr - jnp.max(scr, axis=1, keepdims=True)) * scale2)
        p = e / jnp.sum(e, axis=1, keepdims=True)
        delta = jnp.sum(go.astype(f32) * co.astype(f32), axis=1, keepdims=True)
        gs = (p * (nt(go, v) - delta) * scale).astype(bf)
        gqkv[:, h * HD_ENC : (h + 1) * HD_ENC] = nn(gs, k).astype(bf)
        gqkv[:, (heads + h) * HD_ENC : (heads + h + 1) * HD_ENC] = tn(gs, q).astype(bf)
        gqkv[:, (2 * heads + h) * HD_ENC : (2 * heads + h + 1) * HD_ENC] = tn(p.astype(bf), go).astype(bf)
        if gather and h == 0:
            pr.back_y()
        if gather and h == 1:
            qc.near()
    gqkv[:, 3 * heads * HD_ENC :] = jnp.zeros((total, width - 3 * heads * HD_ENC), bf)
    part[...] = nt(gqkv[...], wa[...]).reshape(part.shape)
    r2 = ReduceMp(cx, part, stage.at[1], recv.at[1])
    cols = (pl.ds(0, cut), pl.ds(cut, cpad))
    outs = (None, None) if gather else [out_qkv.at[:, c] for c in cols]
    qa = grad_halves(0, [(n1, gqkv[:, :cut])], outs[0])
    r2.middle()
    if gather:
        qc.far()
    qa2 = grad_halves(1, [(n1, gqkv[:, cut:]), (gmid_low, ctx[...])], outs[1])
    if gather:
        pr.back_core()
        qb.near()
        g = qd.finish()
        gbuf[0 : yst.shape[0], :unit_d] = g[:, :unit_d]
        yst[...] = g[:, unit_d:].astype(bf)
        cyd = cx.send(yst, yrc, cx.y)
    g_n1 = r2.finish()
    stream = x_all[s].astype(f32)
    grad_in, gain_in, shift_in = normalize_back(stream, gains[0:1, :], g_n1)
    grad = gmid_half[...] + grad_in
    part[0, :, :half] = grad[:, :half]
    part[1, :, :half] = grad[:, half:]
    gin[s] = part[s, :, :half]
    cin = cx.send(part.at[1 - s, :, pl.ds(0, half)], gin.at[s], cx.x)
    dw = dsmall.shape[1]
    vec = jnp.concatenate(
        [
            gain_in,
            gain_mid,
            shift_in,
            shift_mid,
            jnp.zeros((4, width), f32),
            jnp.concatenate([dsmall[...], jnp.zeros((8, width - dw), f32)], axis=1),
        ],
        axis=0,
    )
    if gather:
        smr[0] = vec
        c = cx.send(smr.at[0], smr.at[1], cx.core)
        qb.far()
        c.wait_recv()
        smr[2] = smr[0] + smr[1]
        c = cx.send(smr.at[2], smr.at[3], cx.y)
        c.wait_recv()
        smr[4] = smr[2] + smr[3]
        c = cx.send(smr.at[4], smr.at[5], cx.x)
        out_c[...] = qc.finish()
        pr.finish()
        qa.near()
        c.wait_recv()
        smz[cx.d] = smr[4] + smr[5]
        cs = [cx.send(smz.at[cx.d], smz.at[cx.d], cx.z(k)) for k in range(1, dp)]
        qa2.near()
        cyd.wait_recv()
        g = gbuf[0 : yst.shape[0], :unit_d] + yrc[...].astype(f32)
        unit = out_dqkv.shape[2]
        for t in range(3):
            out_dqkv[t] = g[:, t * unit : (t + 1) * unit]
        out_do[...] = g[:, 3 * unit :]
        out_b[...] = qb.finish()
        qa.far()
        for c in cs:
            c.wait_recv()
        vec = sum_in_order(smz, dp)
        qa2.far()
        g = jnp.concatenate([qa.finish(), qa2.finish()], axis=1)
        unit = out_qkv.shape[2]
        for t in range(3):
            out_qkv[t] = g[:, t * unit : (t + 1) * unit]
        out_o[...] = g[:, 3 * unit :].T
    else:
        cyd.wait_recv()
        out_dqkv[...] = gd[:, :unit_d] + yrc[...].astype(f32)
        out_do[...] = jnp.zeros(out_do.shape, f32)
        out_o[...] = jnp.zeros(out_o.shape, f32)
    eg[...] = vec[0:2]
    es[...] = vec[2:4]
    dg[...] = vec[8:10, :dw]
    dsh[...] = vec[10:12, :dw]
    mg[...] = vec[12:13, :dw]
    cin.wait_recv()
    cx.drain()


def sum_in_order(ref, n):
    out = ref[0]
    for i in range(1, n):
        out = out + ref[i]
    return out


class ProjSum:
    def __init__(self, cx, st, rc, zs, zr, acc, whole, out):
        self.cx, self.st, self.rc, self.zs, self.zr = cx, st, rc, zs, zr
        self.acc, self.whole, self.out = acc, whole, out
        self.R, self.C = out.shape

    def rows(self, start, size):
        return pl.ds(pl.multiple_of(start, 16), size)

    def core(self, part):
        cx, R = self.cx, self.R
        h = R // 2
        self.acc[...] = part
        self.o1 = cx.lo * h
        self.st[0:h] = self.acc[self.rows((1 - cx.lo) * h, h), :].astype(bf)
        self.c = cx.send(self.st.at[pl.ds(0, h)], self.rc.at[pl.ds(0, h)], cx.core)

    def step(self, prev_at, prev_size, bit, dev):
        cx, R = self.cx, self.R
        self.c.wait_recv()
        off = R - 2 * prev_size
        mine = self.rows(prev_at, prev_size)
        self.acc[mine, :] = self.acc[mine, :] + self.rc[off : off + prev_size, :].astype(f32)
        h = prev_size // 2
        noff = R - 2 * h
        self.st[noff : noff + h] = self.acc[self.rows(prev_at + (1 - bit) * h, h), :].astype(bf)
        self.c = cx.send(self.st.at[pl.ds(noff, h)], self.rc.at[pl.ds(noff, h)], dev)
        return prev_at + bit * h

    def y(self):
        self.o2 = self.step(self.o1, self.R // 2, self.cx.hi, self.cx.y)

    def x(self):
        self.o3 = self.step(self.o2, self.R // 4, self.cx.s, self.cx.x)

    def z(self):
        cx, R = self.cx, self.R
        size, unit = R // 8, self.C // cx.dp
        self.c.wait_recv()
        off = R - 2 * size
        total = self.acc[self.rows(self.o3, size), :] + self.rc[off : off + size, :].astype(f32)
        for e in range(cx.dp):
            self.zs[e] = total[:, e * unit : (e + 1) * unit].astype(bf)
        self.cs = []
        for k in range(1, cx.dp):
            to = lax.rem(cx.d + k, cx.dp)
            self.cs.append(cx.send(self.zs.at[to], self.zr.at[k - 1], cx.z(k)))

    def back_z(self):
        cx = self.cx
        unit = self.C // cx.dp
        total = self.zs[cx.d].astype(f32)
        for k in range(1, cx.dp):
            self.cs[k - 1].wait_recv()
            total = total + self.zr[k - 1].astype(f32)
        at = self.whole.at[self.rows(self.o3, self.R // 8), pl.ds(pl.multiple_of(cx.d * unit, 128), unit)]
        at[...] = total.astype(bf)
        self.cs = [cx.send(at, at, cx.z(k)) for k in range(1, cx.dp)]

    def back_x(self):
        for c in self.cs:
            c.wait_recv()
        at = self.rows(self.o3, self.R // 8)
        self.c = self.cx.send(self.whole.at[at], self.whole.at[at], self.cx.x)

    def back_y(self):
        self.c.wait_recv()
        at = self.rows(self.o2, self.R // 4)
        self.c = self.cx.send(self.whole.at[at], self.whole.at[at], self.cx.y)

    def back_core(self):
        self.c.wait_recv()
        at = self.rows(self.o1, self.R // 2)
        self.c = self.cx.send(self.whole.at[at], self.whole.at[at], self.cx.core)

    def finish(self):
        self.c.wait_recv()
        self.out[...] = self.whole[...].astype(f32)


def enc_backward(dp, gather, res, x, gains, proj, weights, saved, glow, gd, dsmall, ec, dc):
    wa, wb, wc = weights
    n1, n2, qkv, ctx, slope, active, mid, top = saved
    rows, width = x.shape[1:]
    total = 4 * rows
    V = pltpu.VMEM
    dd, dw = gd.shape[0], gd.shape[1] // 2
    er, dr = wa.shape[0] // (2 * dp), dd // (2 * dp)
    outs = [sds((2, rows, width // 2), f32)]
    if gather:
        outs += [sds((3, er, ec), f32), sds((ec, er), f32), sds((er, wb.shape[1]), f32), sds((er, wc.shape[1]), f32)]
        outs += [sds((3, dr, dc), f32), sds((dr, dc), f32)]
    else:
        outs += [sds(wa.shape, f32), sds((8, 128), f32), sds(wb.shape, f32), sds(wc.shape, f32)]
        outs += [sds((dd, dw), f32), sds((8, 128), f32)]
    outs += [sds((2, width), f32), sds((2, width), f32), sds(proj.shape, f32)]
    outs += [sds((1, dd), f32), sds((2, dd), f32), sds((2, dd), f32)]
    slots = (4, rows, width)
    hbm = (wc, slope, wb, active, n2, wa, ctx, qkv, n1)
    scratch = [
        pltpu.SemaphoreType.DMA((80,)),
        pltpu.SemaphoreType.DMA((80,)),
        pltpu.SemaphoreType.DMA((16,)),
    ]
    scratch += [V(a.shape, a.dtype) for a in hbm]
    scratch += [
        V(slots, bf),
        V(slots, bf),
        V((total, width), bf),
        V(slots, f32),
        V((2, 3, rows, width), bf),
        V((2, 3, rows, width), bf),
        V((dd // 2, 2 * dw) if gather else (8, 128), f32),
        V((dr if gather else dd, dw), bf),
        V((dr if gather else dd, dw), bf),
        V((rows, width), f32),
    ]
    if gather:
        cpad = ctx.shape[1]
        widths = (wa.shape[1] - cpad, cpad, wc.shape[1], wb.shape[1])
        for w in widths:
            scratch += scatter_scratch(dp, er, w)
        scratch += scatter_scratch(dp, dr, 2 * dw)
        scratch += [V((dp * er, w), f32) for w in widths]
        scratch += [
            V((6, 16, width), f32),
            V((dp, 16, width), f32),
            V(proj.shape, bf),
            V(proj.shape, bf),
            V((dp, proj.shape[0] // 8, proj.shape[1] // dp), bf),
            V((dp - 1, proj.shape[0] // 8, proj.shape[1] // dp), bf),
            V(proj.shape, f32),
            V(proj.shape, bf),
        ]
    return pl.pallas_call(
        functools.partial(enc_backward_kernel, dp, gather),
        out_shape=outs,
        in_specs=[SMEM] + vm(8) + anywhere(9),
        out_specs=vm(len(outs)),
        scratch_shapes=scratch,
        compiler_params=params(3),
        name="enc_backward",
    )(res, x, gains, proj, mid, top, glow, gd, dsmall, *hbm)


def place_kernel(n, *refs):
    for i in range(n):
        refs[n + i][...] = refs[i][...]


def place_outputs(arrays):
    n = len(arrays)
    return pl.pallas_call(
        functools.partial(place_kernel, n),
        out_shape=[sds(a.shape, a.dtype) for a in arrays],
        in_specs=vm(n),
        out_specs=vm(n),
        compiler_params=pltpu.CompilerParams(vmem_limit_bytes=60 << 20),
        name="place_outputs",
    )(*arrays)


def position_table(count, quarter):
    freq = (np.float32(10000.0) ** (-np.arange(quarter, dtype=np.float32) / np.float32(quarter))).astype(np.float32)
    angle = (np.arange(count, dtype=np.float32)[:, None] * freq[None, :]).astype(np.float32).astype(np.float64)
    return np.concatenate([np.sin(angle), np.cos(angle)], axis=1).astype(np.float32)


def per_device(
    x_visible,
    resolution,
    visible_index,
    enc_qkv_w,
    enc_out_w,
    enc_up_w,
    enc_down_w,
    enc_gains,
    enc_shifts,
    projection,
    mask_token,
    dec_qkv_w,
    dec_out_w,
    dec_up_w,
    dec_down_w,
    dec_gains,
    dec_shifts,
    cotangent,
):
    dp = lax.axis_size("dp")
    over = ("section", "dp")
    er, dr = enc_qkv_w.shape[0], dec_qkv_w.shape[0]
    de, dd = projection.shape
    ec, dc = enc_qkv_w.shape[2], dec_qkv_w.shape[2]
    gather = er % 16 == 0 and dr % 16 == 0 and dp == 4
    if gather:
        shards = [
            jnp.transpose(enc_qkv_w, (1, 0, 2)),
            enc_out_w,
            enc_up_w,
            enc_down_w.T,
            jnp.transpose(dec_qkv_w, (1, 0, 2)),
            dec_out_w.T,
        ]
        e_in, f_in = dec_up_w, dec_down_w.T
    else:
        whole = [
            lax.all_gather(w, over, axis=0, tiled=True)
            for w in (
                jnp.concatenate([enc_qkv_w.reshape(er, 3 * ec), enc_out_w.T], axis=1),
                enc_up_w,
                enc_down_w.T,
                jnp.concatenate([dec_qkv_w.reshape(dr, 3 * dc), dec_out_w.T], axis=1),
                dec_up_w,
                dec_down_w.T,
            )
        ]
        shards, (e_in, f_in) = whole[:4], whole[4:]
    weights, saved = enc_forward(
        dp,
        gather,
        resolution,
        x_visible,
        enc_gains,
        enc_shifts,
        projection,
        shards,
        de,
        dd,
        enc_up_w.shape[1],
        dec_up_w.shape[1],
    )
    table = jnp.asarray(position_table(COLS_BIG, dd // 4))
    out, glow, gd, ge, gf, dsmall = decoder(
        dp,
        gather,
        resolution,
        visible_index,
        saved[8],
        table,
        cotangent,
        dec_gains,
        dec_shifts,
        mask_token[None, :],
        weights[3],
        e_in,
        f_in,
    )
    back = enc_backward(
        dp,
        gather,
        resolution,
        x_visible,
        enc_gains,
        projection,
        weights[:3],
        saved[:8],
        glow,
        gd,
        dsmall,
        ec,
        dc,
    )
    if gather:
        got = place_outputs((out, ge, gf) + tuple(back))
        out, ge, gf, gin, gqkv, go, gb, gc, hqkv, ho, eg, es, pg, mg, dg, ds = got
        gqkv = jnp.transpose(gqkv, (1, 0, 2))
        hqkv = jnp.transpose(hqkv, (1, 0, 2))
        ho = ho.T
    else:
        gin, ga, _, gb, gc, hd, _, eg, es, pg, mg, dg, ds = back
        ga, gb, gc, hd, ge, gf = [
            lax.psum_scatter(g, over, scatter_dimension=0, tiled=True) for g in (ga, gb, gc, hd, ge, gf)
        ]
        eg, es, pg, mg, dg, ds = lax.psum((eg, es, pg, mg, dg, ds), ("section", "dp", "mp"))
        gqkv, go = ga[:, : 3 * ec].reshape(er, 3, ec), ga[:, 3 * ec :].T
        hqkv, ho = hd[:, : 3 * dc].reshape(dr, 3, dc), hd[:, 3 * dc :].T
    return (out, gin, gqkv, go, gb, gc.T, eg, es, pg, mg[0], hqkv, ho, ge, gf.T, dg, ds)


def solution(mesh):
    matrix_in = P(("section", "dp"), "mp")
    matrix_out = P("mp", ("section", "dp"))
    qkv = P(("section", "dp"), None, "mp")
    return jax.shard_map(
        per_device,
        mesh=mesh,
        in_specs=(
            P("dp", "mp", None),
            P("dp"),
            P("dp", None),
            qkv,
            matrix_out,
            matrix_in,
            matrix_out,
            P(),
            P(),
            P(),
            P(),
            qkv,
            matrix_out,
            matrix_in,
            matrix_out,
            P(),
            P(),
            P("dp", "mp", None),
        ),
        out_specs=(
            P("dp", "mp", "section"),
            P("dp", "mp", "section"),
            qkv,
            matrix_out,
            matrix_in,
            matrix_out,
            P(),
            P(),
            P(),
            P(),
            qkv,
            matrix_out,
            matrix_in,
            matrix_out,
            P(),
            P(),
        ),
        check_vma=False,
    )
```

```python
import functools
import math

import jax
import jax.numpy as jnp
import numpy as np
from jax import lax
from jax.experimental import pallas as pl
from jax.experimental.pallas import tpu as pltpu
from jax.sharding import PartitionSpec as P

HD_ENC = 64
HD_DEC = 32
COLS_SMALL = 32
COLS_BIG = 64
PATCHES = 2048
SMALL_PATCHES = 512
VIS = 512
VIS_SMALL = 128

MESH = pl.DeviceIdType.MESH
bf = jnp.bfloat16
f32 = jnp.float32
LOG2E = 1.4426950408889634
NEG = -1e30


def nn(a, b):
    return lax.dot_general(a, b, (((1,), (0,)), ((), ())), preferred_element_type=f32)


def nt(a, b):
    return lax.dot_general(a, b, (((1,), (1,)), ((), ())), preferred_element_type=f32)


def tn(a, b):
    return lax.dot_general(a, b, (((0,), (0,)), ((), ())), preferred_element_type=f32)


def norm_stats(stream):
    centre = stream - jnp.mean(stream, axis=-1, keepdims=True)
    inverse = lax.rsqrt(jnp.mean(centre * centre, axis=-1, keepdims=True) + 1e-06)
    return centre * inverse, inverse


def normalize(stream, gain, shift):
    scaled, _ = norm_stats(stream)
    return scaled * gain + shift


def normalize_back(stream, gain, grad_out):
    scaled, inverse = norm_stats(stream)
    f = grad_out * gain
    grad_in = inverse * (
        f
        - jnp.mean(f, axis=-1, keepdims=True)
        - scaled * jnp.mean(f * scaled, axis=-1, keepdims=True)
    )
    return (
        grad_in,
        jnp.sum(grad_out * scaled, axis=0, keepdims=True),
        jnp.sum(grad_out, axis=0, keepdims=True),
    )


def gelu_and_slope(a):
    x = jnp.abs(a) * 0.7071067811865476
    t = 1.0 / (1.0 + 0.3275911 * x)
    e = jnp.exp2(x * x * (-LOG2E))
    poly = ((((1.061405429 * t - 1.453152027) * t + 1.421413741) * t - 0.284496736) * t + 0.254829592) * t
    tail = 0.5 * poly * e
    phi = jnp.where(a >= 0, 1.0 - tail, tail)
    return a * phi, phi + a * e * 0.3989422804014327


class Ctx:
    def __init__(self, ss, rs, dp):
        self.ss, self.rs, self.n, self.dp = ss, rs, 0, dp
        self.s = lax.axis_index("section")
        self.d = lax.axis_index("dp")
        self.m = lax.axis_index("mp")
        m = self.m
        self.lo = lax.rem(m, 2)
        self.hi = m // 2
        self.m1 = m + 1 - 2 * self.lo
        self.m2 = lax.rem(m + 2, 4)
        self.m3 = lax.rem(self.m1 + 2, 4)
        self.core = {"mp": self.m1}
        self.y = {"mp": self.m2}
        self.x = {"section": 1 - self.s}
        self.pending = []

    def z(self, k):
        return {"dp": lax.rem(self.d + k, self.dp)}

    def barrier(self, peers):
        b = pltpu.get_barrier_semaphore()
        for p in peers:
            pl.semaphore_signal(b, inc=1, device_id=p, device_id_type=MESH)
        pl.semaphore_wait(b, len(peers))

    def send(self, src, dst, dev):
        i = self.n
        self.n += 1
        c = pltpu.make_async_remote_copy(
            src_ref=src,
            dst_ref=dst,
            send_sem=self.ss.at[i],
            recv_sem=self.rs.at[i],
            device_id=dev,
            device_id_type=MESH,
        )
        c.start()
        self.pending.append(c)
        return c

    def sent(self, c):
        c.wait_send()
        self.pending = [p for p in self.pending if p is not c]

    def drain(self):
        for c in self.pending:
            c.wait_send()
        self.pending = []


class GatherMp:
    def __init__(self, cx, buf):
        self.cx, self.buf = cx, buf
        m = cx.m
        self.c2 = cx.send(buf.at[m], buf.at[m], cx.y)
        self.c1 = cx.send(buf.at[m], buf.at[m], cx.core)

    def forward(self):
        cx, buf = self.cx, self.buf
        self.c2.wait_recv()
        self.c3 = cx.send(buf.at[cx.m2], buf.at[cx.m2], cx.core)

    def near(self):
        self.c1.wait_recv()

    def far(self):
        self.c3.wait_recv()

    def finish(self):
        self.forward()
        self.near()
        self.far()


class ReduceMp:
    def __init__(self, cx, part, stage, recv):
        self.cx, self.part, self.stage, self.recv = cx, part, stage, recv
        stage[0] = part[cx.m3].astype(bf)
        self.c3 = cx.send(stage.at[0], recv.at[0], cx.core)
        stage[1] = part[cx.m1].astype(bf)
        self.c1 = cx.send(stage.at[1], recv.at[1], cx.core)

    def middle(self):
        cx = self.cx
        self.c3.wait_recv()
        self.stage[2] = (self.part[cx.m2] + self.recv[0].astype(f32)).astype(bf)
        self.c2 = cx.send(self.stage.at[2], self.recv.at[2], cx.y)

    def finish(self):
        self.c1.wait_recv()
        own = self.part[self.cx.m] + self.recv[1].astype(f32)
        self.c2.wait_recv()
        return own + self.recv[2].astype(f32)


def reduce_mp(cx, part, stage, recv):
    r = ReduceMp(cx, part, stage, recv)
    r.middle()
    return r.finish()


class GatherW:
    def __init__(self, cx, shard, whole):
        self.cx, self.whole, self.rows = cx, whole, shard.shape[0]
        own = self.at(cx.s, cx.d)
        self.zs = [cx.send(shard, own, cx.z(k)) for k in range(1, cx.dp)]
        self.xs = [cx.send(shard, own, cx.x)]
        own[...] = shard[...]

    def at(self, s, d):
        start = (s * self.cx.dp + d) * self.rows
        return self.whole.at[pl.ds(pl.multiple_of(start, 16), self.rows)]

    def forward(self):
        cx = self.cx
        for k in range(1, cx.dp):
            self.zs[k - 1].wait_recv()
            block = self.at(cx.s, lax.rem(cx.d + cx.dp - k, cx.dp))
            self.xs.append(cx.send(block, block, cx.x))

    def finish(self):
        for c in self.xs:
            c.wait_recv()


class RelayW:
    def __init__(self, cx, shard, whole):
        self.cx, self.whole, self.rows = cx, whole, shard.shape[0]
        dp, d = cx.dp, cx.d
        self.base = cx.n
        cx.n += 4 * dp
        self.own = self.at(cx.s, d)

        @pl.when(d < dp - 1)
        def _():
            self.make(shard, self.own, 1, {"dp": d + 1}).start()

        @pl.when(d > 0)
        def _():
            self.make(shard, self.own, dp + 1, {"dp": d - 1}).start()

        self.make(shard, self.own, 2 * dp, cx.x).start()
        self.own[...] = shard[...]

    def at(self, s, d):
        start = (s * self.cx.dp + d) * self.rows
        return self.whole.at[pl.ds(pl.multiple_of(start, 16), self.rows)]

    def make(self, src, dst, i, dev):
        cx, i = self.cx, self.base + i
        return pltpu.make_async_remote_copy(
            src_ref=src,
            dst_ref=dst,
            send_sem=cx.ss.at[i],
            recv_sem=cx.rs.at[i],
            device_id=dev,
            device_id_type=MESH,
        )

    def hop(self, k):
        cx, dp, d = self.cx, self.cx.dp, self.cx.d

        @pl.when(d >= k)
        def _():
            b = self.at(cx.s, jnp.maximum(d - k, 0))
            self.make(b, b, k, cx.x).wait_recv()

            @pl.when(d < dp - 1)
            def _():
                self.make(b, b, k + 1, {"dp": d + 1}).start()

            self.make(b, b, 2 * dp + k, cx.x).start()

        @pl.when(d + k < dp)
        def _():
            b = self.at(cx.s, jnp.minimum(d + k, dp - 1))
            self.make(b, b, dp + k, cx.x).wait_recv()

            @pl.when(d > 0)
            def _():
                self.make(b, b, dp + k + 1, {"dp": d - 1}).start()

            self.make(b, b, 3 * dp + k, cx.x).start()

    def finish(self):
        cx, dp, d = self.cx, self.cx.dp, self.cx.d
        other = lambda e: self.at(1 - cx.s, jnp.clip(e, 0, dp - 1))
        self.make(self.own, other(d), 2 * dp, cx.x).wait_recv()
        for k in range(1, dp):

            @pl.when(d >= k)
            def _():
                self.make(self.own, other(d - k), 2 * dp + k, cx.x).wait_recv()

            @pl.when(d + k < dp)
            def _():
                self.make(self.own, other(d + k), 3 * dp + k, cx.x).wait_recv()

    def drain(self):
        cx, dp, d = self.cx, self.cx.dp, self.cx.d
        own = self.own
        self.make(own, own, 2 * dp, cx.x).wait_send()
        for k in range(1, dp):

            @pl.when(d >= k)
            def _():
                self.make(own, own, 2 * dp + k, cx.x).wait_send()

            @pl.when(d + k < dp)
            def _():
                self.make(own, own, 3 * dp + k, cx.x).wait_send()

            @pl.when((d < dp - 1) & (d >= k - 1))
            def _():
                self.make(own, own, k, cx.x).wait_send()

            @pl.when((d > 0) & (d + k - 1 < dp))
            def _():
                self.make(own, own, dp + k, cx.x).wait_send()


class Local:
    def __init__(self, sems):
        self.sems, self.n, self.pending = sems, 0, []

    def start(self, src, dst):
        c = pltpu.make_async_copy(src, dst, self.sems.at[self.n])
        self.n += 1
        c.start()
        self.pending.append(c)
        return c

    def drain(self):
        for c in self.pending:
            c.wait()


class ScatterW:
    def __init__(self, cx, rows, own, xs, xr, zs, zr):
        self.cx, self.rows, self.own = cx, rows, own
        self.xs, self.xr, self.zs, self.zr = xs, xr, zs, zr

    def start(self, theirs):
        self.xs[...] = theirs.astype(bf)
        self.c = self.cx.send(self.xs, self.xr, self.cx.x)

    def at(self, e):
        return pl.ds(pl.multiple_of(e * self.rows, 16), self.rows)

    def near(self):
        cx = self.cx
        self.c.wait_recv()
        low = lax.rem(cx.d, 2)
        for j in range(2):
            at = self.at(2 * j + 1 - low)
            self.zs[j] = (self.own[at, :] + self.xr[at, :].astype(f32)).astype(bf)
        self.c = cx.send(self.zs.at[pl.ds(0, 2)], self.zr.at[pl.ds(0, 2)], {"dp": cx.d + 1 - 2 * low})

    def far(self):
        cx = self.cx
        low, high = lax.rem(cx.d, 2), cx.d // 2
        self.c.wait_recv()
        at = self.at(2 * (1 - high) + low)
        total = self.own[at, :] + self.xr[at, :].astype(f32) + self.zr[1 - high].astype(f32)
        self.zs[2] = total.astype(bf)
        self.c = cx.send(self.zs.at[2], self.zr.at[2], cx.z(2))

    def finish(self):
        at = self.at(self.cx.d)
        own = self.own[at, :] + self.xr[at, :].astype(f32) + self.zr[self.cx.d // 2].astype(f32)
        self.c.wait_recv()
        return own + self.zr[2].astype(f32)


def scatter_scratch(dp, rows, cols):
    half = dp * rows
    return [
        pltpu.VMEM((half, cols), bf),
        pltpu.VMEM((half, cols), bf),
        pltpu.VMEM((3, rows, cols), bf),
        pltpu.VMEM((3, rows, cols), bf),
    ]


def iota(shape, dim):
    return lax.broadcasted_iota(jnp.int32, shape, dim)


def enc_forward_kernel(dp, gather, *refs):
    it = iter(refs)
    take = lambda n: [next(it) for _ in range(n)]
    res, x_all, gains, shifts, proj = take(5)
    if gather:
        eqkv, eout, eup, edown, dqkv, dout = take(6)
        ha, hb, hc = take(3)
    else:
        wa, wb, wc, wd_in = take(4)
    wd, h1, h2, hq, hctx, hslope, hact, hmid, top_out, low_all = take(10)
    ss, rs, ls, part, stage, recv, n1, n2, qkv, ctx, slope, active, mid_s = take(13)
    if gather:
        wa, wb, wc, sa, sd, sdf = take(6)
    cx = Ctx(ss, rs, dp)
    lc = Local(ls)
    peers = [cx.core, cx.y]
    if gather:
        peers += [cx.x] + [cx.z(k) for k in range(1, dp)]
        wide = eqkv.shape[2]
        for t in range(3):
            sa[:, t * wide : (t + 1) * wide] = eqkv[t]
        sa[:, 3 * wide :] = eout[...].astype(f32).T.astype(bf)
        wide = dqkv.shape[2]
        for t in range(3):
            sd[:, t * wide : (t + 1) * wide] = dqkv[t]
        sd[:, 3 * wide : 4 * wide] = dout[...]
        both = 4 * wide
    cx.barrier(peers)
    if gather:
        cut = sa.shape[1] // 2
        ga = RelayW(cx, sa.at[:, pl.ds(0, cut)], wa.at[:, pl.ds(0, cut)])
        ga2 = RelayW(cx, sa.at[:, pl.ds(cut, cut)], wa.at[:, pl.ds(cut, cut)])
    stream = x_all[cx.s].astype(f32)
    n1[cx.m] = normalize(stream, gains[0:1, :], shifts[0:1, :]).astype(bf)
    g1 = GatherMp(cx, n1)
    if gather:
        csd = cx.send(sd.at[:, pl.ds(0, both)], sdf, cx.y)
        ga.hop(1)
        ga2.hop(1)
        ga.hop(2)
        ga2.hop(2)
        gb = RelayW(cx, eup, wb)
    g1.finish()
    lc.start(n1, h1)
    if gather:
        ga.hop(3)
        ga2.hop(3)
        gc = RelayW(cx, edown, wc)
        gb.hop(1)
        ga.finish()
        ga2.finish()
        lc.start(wa, ha)
    rows = n1.shape[1]
    total = 4 * rows
    width = n1.shape[2]
    n1_all = n1[...].reshape(total, width)
    qkv[...] = nn(n1_all, wa[...]).astype(bf)
    lc.start(qkv, hq)
    if gather:
        gb.hop(2)
        gc.hop(1)
        csd.wait_recv()
        sd[:, both:] = sdf[...]
        gd = RelayW(cx, sd, wd)
    shown = jnp.where(res[cx.s] == 1, VIS, VIS_SMALL)
    bias = jnp.where(iota((1, total), 1) < shown, 0.0, NEG)
    scale2 = HD_ENC**-0.5 * LOG2E
    heads = (width // 4) // HD_ENC
    pieces = [jnp.zeros((total, HD_ENC), bf)]
    for h in range(heads):
        q = qkv[:, h * HD_ENC : (h + 1) * HD_ENC]
        k = qkv[:, (heads + h) * HD_ENC : (heads + h + 1) * HD_ENC]
        v = qkv[:, (2 * heads + h) * HD_ENC : (2 * heads + h + 1) * HD_ENC]
        sc = nt(q, k) + bias
        top = jnp.max(sc, axis=1, keepdims=True)
        e = jnp.exp2((sc - top) * scale2)
        tot = jnp.sum(e, axis=1, keepdims=True)
        pieces.append((nn(e.astype(bf), v) / tot).astype(bf))
        if gather and h == 0:
            gb.hop(3)
        if gather and h == 1:
            gc.hop(2)
    ctx[...] = jnp.concatenate(pieces, axis=1)
    lc.start(ctx, hctx)
    cpad = ctx.shape[1]
    part[...] = nt(ctx[...], wa[:, width - cpad :]).reshape(part.shape)
    r1 = ReduceMp(cx, part, stage.at[0], recv.at[0])
    if gather:
        gd.hop(1)
    r1.middle()
    if gather:
        gc.hop(3)
    mid = stream + r1.finish()
    mid_s[...] = mid
    lc.start(mid_s, hmid)
    n2[cx.m] = normalize(mid, gains[1:2, :], shifts[1:2, :]).astype(bf)
    g2 = GatherMp(cx, n2)
    if gather:
        gd.hop(2)
        gb.finish()
        lc.start(wb, hb)
    g2.finish()
    lc.start(n2, h2)
    hid = nn(n2[...].reshape(total, width), wb[...])
    act, slo = gelu_and_slope(hid)
    active[...] = act.astype(bf)
    slope[...] = slo.astype(bf)
    lc.start(active, hact)
    lc.start(slope, hslope)
    if gather:
        gc.finish()
        lc.start(wc, hc)
    part[...] = nt(active[...], wc[...]).reshape(part.shape)
    r2 = ReduceMp(cx, part, stage.at[1], recv.at[1])
    r2.middle()
    if gather:
        gd.hop(3)
    top = (mid_s[...] + r2.finish()).astype(bf)
    top_out[...] = top
    low_all[cx.m] = nn(top, proj[...]).astype(bf)
    g3 = GatherMp(cx, low_all)
    if gather:
        gd.finish()
    else:
        both = wd_in.shape[1]
        wd[:, :both] = wd_in[...]
        cd = cx.send(wd_in, wd.at[:, pl.ds(both, both)], cx.y)
        cd.wait_recv()
    g3.finish()
    cx.drain()
    if gather:
        for g in (ga, ga2, gb, gc, gd):
            g.drain()
    lc.drain()


def vm(n):
    return [pl.BlockSpec(memory_space=pltpu.VMEM)] * n


def anywhere(n):
    return [pl.BlockSpec(memory_space=pl.ANY)] * n


SMEM = pl.BlockSpec(memory_space=pltpu.SMEM)


def sds(shape, dtype):
    return jax.ShapeDtypeStruct(shape, dtype)


def params(cid):
    return pltpu.CompilerParams(collective_id=cid, has_side_effects=True, vmem_limit_bytes=60 << 20)


def enc_forward(dp, gather, res, x, gains, shifts, proj, shards, de, dd, wide, dwide):
    rows, width = x.shape[1:]
    total = 4 * rows
    slots = (4, rows, width)
    V = pltpu.VMEM
    outs = []
    if gather:
        outs += [sds((de, de), bf), sds((de, wide), bf), sds((de, wide), bf)]
    outs += [sds((dd, 2 * dwide), bf)]
    big = [sds(slots, bf), sds(slots, bf), sds((total, width), bf), sds((total, 256), bf)]
    big += [sds((total, wide), bf), sds((total, wide), bf), sds((rows, width), f32)]
    outs += big + [sds((rows, width), bf), sds((4, rows, dd), bf)]
    scratch = [
        pltpu.SemaphoreType.DMA((112,)),
        pltpu.SemaphoreType.DMA((112,)),
        pltpu.SemaphoreType.DMA((16,)),
        V(slots, f32),
        V((2, 3, rows, width), bf),
        V((2, 3, rows, width), bf),
    ] + [V(b.shape, b.dtype) for b in big]
    if gather:
        scratch += [V(o.shape, bf) for o in outs[:3]]
        scratch += [V((shards[2].shape[0], de), bf), V((shards[5].shape[0], 2 * dwide), bf)]
        scratch += [V((shards[5].shape[0], dwide), bf)]
    got = pl.pallas_call(
        functools.partial(enc_forward_kernel, dp, gather),
        out_shape=outs,
        in_specs=[SMEM] + vm(4 + len(shards)),
        out_specs=anywhere(3 if gather else 0) + vm(1) + anywhere(7) + vm(2),
        scratch_shapes=scratch,
        compiler_params=params(1),
        name="enc_forward",
    )(res, x, gains, shifts, proj, *shards)
    if not gather:
        got = list(shards[:3]) + list(got)
    return got[:4], got[4:]


def dec_kernel(dp, gather, *refs):
    it = iter(refs)
    take = lambda n: [next(it) for _ in range(n)]
    res, chosen, low_all, table, cot, gains, shifts, token, wd_both, e_in, f_in = take(11)
    out, glow, gd, out_e, out_f, small, kept = take(7)
    ss, rs, we_both, wf_both, own_e, own_f, yst, yrc = take(8)
    if gather:
        se, sf, sfar = take(3)
        scat = (take(4), take(4))
    unit = wd_both.shape[1] // 2
    wd, we, wf = [[w.at[:, pl.ds(unit * g, unit)] for g in range(2)] for w in (wd_both, we_both, wf_both)]
    (n1, n2, gm, gmid_low, qg, kg, vg, gg, vtx, kt, dqt, lse, acc_s, top_s, ctx, active, slope) = take(17)
    ct = dqt
    (dkv, mid_s, start_s, res_s, part, fstage, frecv, far, prod, pstage, precv, masks) = take(12)
    sc_s, mx_s = take(2), take(2)
    p_s, tops, ps = take(3)
    cx = Ctx(ss, rs, dp)
    cx.barrier([cx.core, cx.y, cx.x] + ([cx.z(k) for k in range(1, dp)] if gather else []))
    rows, width = n1.shape[1:]
    m, lo, hi, s = cx.m, cx.lo, cx.hi, cx.s
    big = res[s] == 1
    shown = jnp.where(big, VIS, VIS_SMALL)
    filled = jnp.where(big, PATCHES, SMALL_PATCHES)
    pos_col = iota((rows, 1), 0) + m * rows
    live = jnp.where(pos_col < filled, 1.0, 0.0)
    ccot = pltpu.make_async_copy(cot.at[s], gm.at[lo], ps.at[0])
    ccot.start()
    ccot.wait()
    gm[lo] = (gm[lo].astype(f32) * live).astype(bf)
    cgm = cx.send(gm.at[lo], gm.at[lo], cx.core)
    if gather:
        cef = [cx.send(e_in, sfar.at[0], cx.y), cx.send(f_in, sfar.at[1], cx.y)]
        se[:, :unit] = e_in[...]
        sf[:, :unit] = f_in[...]
    else:
        we[0][...] = e_in[...]
        wf[0][...] = f_in[...]
        cef = [cx.send(e_in, we[1], cx.y), cx.send(f_in, wf[1], cx.y)]
    vis = chosen.shape[-1]

    def place_rows():
        return jnp.where((pos_col == chosen[pl.ds(s, 1), :]) & (iota((1, vis), 1) < shown), 1.0, 0.0)

    place = place_rows()
    seen = jnp.sum(place, axis=1, keepdims=True)
    weight = live - seen
    placed = nn(place.astype(bf), low_all[...].reshape(vis, width))
    half = width // 2
    nb, ns = rows // COLS_BIG, rows // COLS_SMALL
    rb = table[pl.ds(pl.multiple_of(m * nb, 8), nb), :]
    rsm = table[pl.ds(pl.multiple_of(m * ns, 8), ns), :]
    big_rows = jnp.broadcast_to(rb[:, None, :], (nb, COLS_BIG, half)).reshape(rows, half)
    small_rows = jnp.broadcast_to(rsm[:, None, :], (ns, COLS_SMALL, half)).reshape(rows, half)
    big_cols = jnp.broadcast_to(table[0:COLS_BIG, :][None], (nb, COLS_BIG, half)).reshape(rows, half)
    small_cols = jnp.broadcast_to(table[0:COLS_SMALL, :][None], (ns, COLS_SMALL, half)).reshape(rows, half)
    base = placed + weight * token[...]
    start_s[:, :half] = base[:, :half] + live * jnp.where(big, big_rows, small_rows)
    start_s[:, half:] = base[:, half:] + live * jnp.where(big, big_cols, small_cols)
    n1[m] = normalize(start_s[...], gains[0:1, :], shifts[0:1, :]).astype(bf)
    g1 = GatherMp(cx, n1)

    lane = iota((1, 256), 1)
    for j in range(4):
        head_lane = (lane < 128) & (lane // 32 == j)
        off = lane - (128 + 8 * j)
        masks[0, j] = jnp.where(head_lane | ((off >= 0) & (off < 3)) | (lane == 160), 1.0, 0.0).astype(bf)
        masks[1, j] = jnp.where(head_lane | ((off >= 0) & (off < 2)), 1.0, 0.0).astype(bf)
    aug = iota((1, 128), 1)
    total = 4 * rows
    key_bias = jnp.where(iota((total, 1), 0) < filled, 0.0, NEG)
    kaug = jnp.where(aug == 32, key_bias, jnp.where(aug < 32, 1.0, 0.0)).astype(bf)
    vaug = jnp.broadcast_to(jnp.where(aug < 32, 1.0, 0.0), (total, 128)).astype(bf)
    qaug = jnp.broadcast_to(jnp.where(aug == 32, 1.0, 0.0), (2 * rows, 128)).astype(bf)
    for g in range(2):
        kg[g, :, 128:] = kaug
        vg[g, :, 128:] = vaug
        qg[g, :, 128:] = qaug
    vtx[:, 32:, :] = jnp.ones((8, 16, total), bf)

    def keys_values(i, groups):
        at = pl.ds(pl.multiple_of(i * rows, 128), rows)
        for g in groups:
            kv = nn(n1[i], wd[g][:, 128:384])
            kg[g, at, :128] = kv[:, :128].astype(bf)
            vg[g, at, :128] = kv[:, 128:].astype(bf)
            kvt = kv.T.astype(bf)
            for j in range(4):
                kt[4 * g + j, :, at] = kvt[32 * j : 32 * j + 32]
                vtx[4 * g + j, 0:32, at] = kvt[128 + 32 * j : 160 + 32 * j]

    g1.near()

    def near_rows_in(g):
        for r in range(2):
            qg[g, r * rows : (r + 1) * rows, :128] = nn(n1[2 * hi + r], wd[g][:, :128]).astype(bf)
        keys_values(cx.m, (g,))
        keys_values(cx.m1, (g,))

    if gather:
        gats = []
        for i, (sh, w) in enumerate(((se, we_both), (sf, wf_both))):
            cef[i].wait_recv()
            sh[:, unit:] = sfar[i]
            gats.append(GatherW(cx, sh, w))
    near_rows_in(0)
    near_rows_in(1)
    c2 = HD_DEC**-0.5 * LOG2E

    def score(h, i, to):
        g, j = h // 4, lax.rem(h, 4)
        at = pl.ds(pl.multiple_of(i * rows, 128), rows)
        sc = nt(kg[g, at, :] * masks[0, j], qg[g])
        sc_s[to][...] = sc
        mx_s[to][...] = jnp.max(sc, axis=0, keepdims=True)

    def slot(n, h):
        return 2 * lax.rem(h, 2) + n

    def keep(n, h, i):
        return pltpu.make_async_copy(p_s.at[slot(n, h)], kept.at[h, i], ps.at[slot(n, h)])

    def fetch(n, h, i):
        return pltpu.make_async_copy(kept.at[h, i], p_s.at[slot(n, h)], ps.at[slot(n, h)])

    def head_pass(first, last, blocks, heads):
        def body(h, _):
            g, j = h // 4, lax.rem(h, 4)
            if first:
                top, acc = None, None
            else:
                top, acc = top_s[pl.ds(h, 1), :], acc_s[h]
            ahead = ((h, blocks[1]), (jnp.minimum(h + 1, 7), blocks[0]))
            for n, i in enumerate(blocks):
                at = pl.ds(pl.multiple_of(i * rows, 128), rows)
                if first and heads[0] == 0:

                    @pl.when(h > 1)
                    def _():
                        keep(n, h, i).wait()

                else:
                    keep(n, h, i).wait()
                mj = mx_s[n][...]
                new = mj if top is None else jnp.maximum(top, mj)
                tops[pl.ds(4 * h + i, 1), :] = new
                score(*ahead[n], 1 - n)
                p = jnp.exp2((sc_s[n][...] - new) * c2).astype(bf)
                p_s[slot(n, h)] = p
                o = nn(vtx[h, :, at], p)
                keep(n, h, i).start()
                acc = o if acc is None else acc * jnp.exp2((top - new) * c2) + o
                top = new
            if last:
                tot = acc[32:33, :]
                ct[h] = acc[:32, :] / tot
                at = pl.ds(pl.multiple_of(8 * j, 8), 8)
                lse[g, at, :] = jnp.broadcast_to(top + jnp.log(tot) * (LOG2E / c2), (8, top.shape[1]))
            else:
                top_s[pl.ds(h, 1), :] = top
                acc_s[h] = acc
            return 0

        lax.fori_loop(*heads, body, 0)

    score(jnp.int32(0), cx.m, 0)
    head_pass(True, False, (cx.m, cx.m1), (0, 6))
    g1.forward()
    if gather:
        gats[0].forward()
    head_pass(True, False, (cx.m, cx.m1), (6, 8))
    keys_values(cx.m2, (0, 1))
    g1.far()
    keys_values(cx.m3, (0, 1))
    score(jnp.int32(0), cx.m2, 0)
    head_pass(False, True, (cx.m2, cx.m3), (0, 4))
    if gather:
        gats[1].forward()
    head_pass(False, True, (cx.m2, cx.m3), (4, 8))
    for n, i in enumerate((cx.m2, cx.m3)):
        for h in (0, 1):
            keep(n, 6 + h, i).wait()
            fetch(n, h, i).start()
    for g in range(2):
        ctx[:, 128 * g : 128 * g + 128] = ct[4 * g : 4 * g + 4].reshape(128, 2 * rows).T.astype(bf)

    def chip_rows(r):
        return pl.ds(pl.multiple_of(r * rows, 128), rows)

    def out_rows(r):
        return sum(nt(ctx[chip_rows(r), 128 * g : 128 * g + 128], wd[g][:, 384:]) for g in range(2))

    fstage[0] = out_rows(1 - lo).astype(bf)
    co = cx.send(fstage.at[0], frecv.at[0], cx.core)
    mid = start_s[...] + out_rows(lo)
    co.wait_recv()
    mid = mid + frecv[0].astype(f32)
    mid_s[...] = mid
    n2[lo] = normalize(mid, gains[1:2, :], shifts[1:2, :]).astype(bf)
    cn2 = cx.send(n2.at[lo], n2.at[lo], cx.core)

    def mlp_rows(r):
        at = chip_rows(r)
        x = n2[r]
        y = None
        for g in range(2):
            a, b = gelu_and_slope(nn(x, we[g][...]))
            cols = slice(width * g, width * (g + 1))
            a = a.astype(bf)
            active[at, cols] = a
            slope[at, cols] = b.astype(bf)
            t = nt(a, wf[g][...])
            y = t if y is None else y + t
        return y

    if gather:
        for q in gats:
            q.finish()
    else:
        for c in cef:
            c.wait_recv()
    res_s[...] = mlp_rows(lo)
    cn2.wait_recv()
    fstage[1] = mlp_rows(1 - lo).astype(bf)
    c = cx.send(fstage.at[1], frecv.at[1], cx.core)

    cgm.wait_recv()

    def mlp_back_rows(r):
        at = chip_rows(r)
        y = None
        for g in range(2):
            cols = slice(width * g, width * (g + 1))
            ga = nn(gm[r], wf[g][...])
            gh = (ga * slope[at, cols].astype(f32)).astype(bf)
            slope[at, cols] = gh
            t = nt(gh, we[g][...])
            y = t if y is None else y + t
        return y

    fstage[2] = mlp_back_rows(1 - lo).astype(bf)
    cb = cx.send(fstage.at[2], frecv.at[2], cx.core)
    c.wait_recv()
    result = mid_s[...] + res_s[...] + frecv[1].astype(f32)
    result = result * live
    left, right = result[:, :half], result[:, half:]
    out[s] = jnp.where(s == 0, left, right).astype(bf)
    prod[...] = jnp.where(s == 0, right, left).astype(bf)
    cprod = cx.send(prod, out.at[s], cx.x)
    own = mlp_back_rows(lo)
    half_rows = width // 2

    def start_scatter(left, right, own, i, out):
        def rows_of(sec):
            at = pl.ds(pl.multiple_of(sec * half_rows, 128), half_rows)
            return tn(left[:, :, at].reshape(2 * rows, half_rows), right[...])

        if gather:
            q = ScatterW(cx, half_rows // dp, own, *scat[i])
            q.start(rows_of(1 - s))
            own[...] = rows_of(s)
            return q
        for sec in (0, 1):
            t = rows_of(jnp.int32(sec))
            at = slice(sec * half_rows, (sec + 1) * half_rows)
            out[at] = t[:, :unit]
            yst[i, at] = t[:, unit:].astype(bf)
        return cx.send(yst.at[i], yrc.at[i], cx.y)

    q_f = start_scatter(gm, active, own_f, 0, out_f)
    cb.wait_recv()
    grad_mid, gain_mid, shift_mid = normalize_back(mid_s[...], gains[1:2, :], own + frecv[2].astype(f32))
    gmid = gm[lo].astype(f32) + grad_mid
    mid_s[...] = gmid
    gmid_low[lo] = gmid.astype(bf)
    cgmid = cx.send(gmid_low.at[lo], gmid_low.at[lo], cx.core)
    q_e = start_scatter(n2, slope, own_e, 1, out_e)
    cgmid.wait_recv()
    gmid_all = gmid_low[...].reshape(2 * rows, width)
    sel = jnp.where(iota((128, 128), 0) // 32 == iota((128, 128), 1) // 8, 1.0, 0.0).astype(bf)
    lane128 = iota((1, 128), 1)
    t8 = lax.rem(lane128, 8)
    for g in range(2):
        gcg = nn(gmid_all, wd[g][:, 384:]).astype(bf)
        gg[g, :, :128] = gcg
        prodd = gcg.astype(f32) * ctx[:, 128 * g : 128 * g + 128].astype(f32)
        ph = prodd.astype(bf)
        plow = (prodd - ph.astype(f32)).astype(bf)
        delta = nn(ph, sel) + nn(plow, sel)
        dh = delta.astype(bf).astype(f32)
        daug = jnp.where(t8 == 0, -dh, jnp.where(t8 == 1, dh - delta, 0.0))
        gg[g, :, 128:] = jnp.where(lane128 < 32, daug, 0.0).astype(bf)
        gd[:, unit * g + 384 : unit * g + 512] = tn(gmid_all, ctx[:, 128 * g : 128 * g + 128])

    scale = HD_DEC**-0.5
    dqt[...] = jnp.zeros_like(dqt)
    head_lane = lane128 // 32

    def back_pass(blocks, heads, after):
        def body(h, _):
            g, j = h // 4, lax.rem(h, 4)
            mine = head_lane == j
            total_row = lse[g, pl.ds(pl.multiple_of(8 * j, 8), 8), :][0:1]
            for n, i in enumerate(blocks):
                at = pl.ds(pl.multiple_of(i * rows, 128), rows)
                fetch(n, h, i).wait()
                dpt = nt(vg[g, at, :] * masks[1, j], gg[g])
                share = jnp.exp2((tops[pl.ds(4 * h + i, 1), :] - total_row) * c2)
                p = p_s[slot(n, h)].astype(f32) * share
                ds = (p * dpt).astype(bf)
                dv = nn(p.astype(bf), gg[g, :, :128])
                dk = nn(ds, qg[g, :, :128]) * scale
                dkv[g, at, :128] = jnp.where(mine, dk, dkv[g, at, :128].astype(f32)).astype(bf)
                dkv[g, at, 128:] = jnp.where(mine, dv, dkv[g, at, 128:].astype(f32)).astype(bf)
                dqt[h] += nn(kt[h, :, at], ds)

                @pl.when(h < 6)
                def _():
                    fetch(n, h + 2, i).start()

                if after:

                    @pl.when(h >= 6)
                    def _():
                        fetch(n, h - 6, after[n]).start()

            return 0

        lax.fori_loop(*heads, body, 0)

    dkv[...] = jnp.zeros_like(dkv)
    back_pass((cx.m2, cx.m3), (0, 6), (cx.m, cx.m1))
    if gather:
        q_f.near()
    back_pass((cx.m2, cx.m3), (6, 8), (cx.m, cx.m1))

    def far_rows(r):
        at = pl.ds(pl.multiple_of((2 * (1 - hi) + r) * rows, 128), rows)
        return sum(nt(dkv[g, at, :], wd[g][:, 128:384]) for g in range(2))

    cx.sent(co)
    fstage[0] = far_rows(1 - lo).astype(bf)
    cf = cx.send(fstage.at[0], frecv.at[0], cx.core)
    res_s[...] = far_rows(lo)
    back_pass((cx.m, cx.m1), (0, 2), None)
    cf.wait_recv()
    cx.sent(cb)
    fstage[2] = (res_s[...] + frecv[0].astype(f32)).astype(bf)
    cfar = cx.send(fstage.at[2], far, cx.y)
    if gather:
        q_f.far()
        q_e.near()
    back_pass((cx.m, cx.m1), (2, 6), None)
    if gather:
        q_e.far()
        t = q_f.finish()
        out_f[...] = t[:, :unit]
        yst[0] = t[:, unit:].astype(bf)
        cyf = cx.send(yst.at[0], yrc.at[0], cx.y)
    back_pass((cx.m, cx.m1), (6, 8), None)
    for g in range(2):
        ctx[:, 128 * g : 128 * g + 128] = (dqt[4 * g : 4 * g + 4].reshape(128, 2 * rows).T * scale).astype(bf)

    def near_rows(r):
        at = pl.ds(pl.multiple_of((2 * hi + r) * rows, 128), rows)
        return sum(
            nt(ctx[chip_rows(r), 128 * g : 128 * g + 128], wd[g][:, :128]) + nt(dkv[g, at, :], wd[g][:, 128:384])
            for g in range(2)
        )

    cx.sent(c)
    fstage[1] = near_rows(1 - lo).astype(bf)
    cn = cx.send(fstage.at[1], frecv.at[1], cx.core)
    near = near_rows(lo)
    n1_chip = n1[pl.ds(2 * hi, 2)].reshape(2 * rows, width)
    t = tn(n1_chip, ctx[...])
    gd[:, :128] = t[:, :128]
    gd[:, unit : unit + 128] = t[:, 128:]
    cn.wait_recv()
    if gather:
        t = q_e.finish()
        out_e[...] = t[:, :unit]
        yst[1] = t[:, unit:].astype(bf)
        cye = cx.send(yst.at[1], yrc.at[1], cx.y)
    near = near + frecv[1].astype(f32)
    cfar.wait_recv()
    grad_in, gain_in, shift_in = normalize_back(start_s[...], gains[0:1, :], near + far[...].astype(f32))
    gstart = (mid_s[...] + grad_in).astype(bf)
    token_term = jnp.sum(weight * gstart.astype(f32), axis=0, keepdims=True)
    small[0:1] = gain_in
    small[1:2] = gain_mid
    small[2:3] = shift_in
    small[3:4] = shift_mid
    small[4:5] = token_term
    small[5:8] = jnp.zeros((3, width), f32)
    part[...] = tn(place_rows().astype(bf), gstart).reshape(part.shape)
    reduce = ReduceMp(cx, part, pstage, precv)
    n1_all = n1[...].reshape(total, width)
    gd[:, 128:384] = tn(n1_all, dkv[0])
    reduce.middle()
    gd[:, unit + 128 : unit + 384] = tn(n1_all, dkv[1])
    for c, o, i in ((cyf, out_f, 0), (cye, out_e, 1)) if gather else ((q_f, out_f, 0), (q_e, out_e, 1)):
        c.wait_recv()
        o[...] = o[...] + yrc[i].astype(f32)
    glow[...] = reduce.finish().astype(bf)
    cprod.wait_recv()
    cx.drain()


def decoder(dp, gather, res, chosen, low_all, table, cot, gains, shifts, token, wd, e_in, f_in):
    rows, width = cot.shape[1:]
    vis = chosen.shape[-1]
    total, chip = 4 * rows, 2 * rows
    unit = wd.shape[1] // 2
    half = (width // 2, 2 * unit)
    outs = [
        sds((2, rows, width // 2), bf),
        sds((vis // 4, width), bf),
        sds(wd.shape, f32),
        sds(e_in.shape, f32),
        sds(f_in.shape, f32),
        sds((8, width), f32),
        sds((8, 4, rows, chip), bf),
    ]
    V = pltpu.VMEM
    extra = []
    if gather:
        pair = (e_in.shape[0], 2 * unit)
        extra = [V(pair, bf), V(pair, bf), V((2,) + e_in.shape, bf)] + 2 * scatter_scratch(dp, *pair)
    return pl.pallas_call(
        functools.partial(dec_kernel, dp, gather),
        out_shape=outs,
        in_specs=[SMEM] + vm(3) + anywhere(1) + vm(6),
        out_specs=vm(len(outs) - 1) + anywhere(1),
        scratch_shapes=[
            pltpu.SemaphoreType.DMA((64,)),
            pltpu.SemaphoreType.DMA((64,)),
            V(wd.shape, bf),
            V(wd.shape, bf),
            V(half, f32),
            V(half, f32),
            V((2,) + e_in.shape, bf),
            V((2,) + e_in.shape, bf),
        ]
        + extra
        + [
            V((4, rows, width), bf),
            V((2, rows, width), bf),
            V((2, rows, width), bf),
            V((2, rows, width), bf),
            V((2, chip, 256), bf),
            V((2, total, 256), bf),
            V((2, total, 256), bf),
            V((2, chip, 256), bf),
            V((8, 48, total), bf),
            V((8, 32, total), bf),
            V((8, 32, chip), f32),
            V((2, 32, chip), f32),
            V((8, 48, chip), f32),
            V((8, chip), f32),
            V((chip, 256), bf),
            V((chip, 2 * width), bf),
            V((chip, 2 * width), bf),
            V((2, total, 256), bf),
            V((rows, width), f32),
            V((rows, width), f32),
            V((rows, width), f32),
            V((4, vis // 4, width), f32),
            V((3, rows, width), bf),
            V((3, rows, width), bf),
            V((rows, width), bf),
            V((rows, width // 2), bf),
            V((3, vis // 4, width), bf),
            V((3, vis // 4, width), bf),
            V((2, 4, 1, 256), bf),
            V((rows, chip), f32),
            V((rows, chip), f32),
            V((1, chip), f32),
            V((1, chip), f32),
            V((4, rows, chip), bf),
            V((32, chip), f32),
            pltpu.SemaphoreType.DMA((4,)),
        ],
        compiler_params=params(2),
        name="decoder",
    )(res, chosen, low_all, table, cot, gains, shifts, token, wd, e_in, f_in)


def enc_backward_kernel(dp, gather, *refs):
    it = iter(refs)
    take = lambda n: [next(it) for _ in range(n)]
    res, x_all, gains, proj, mid, top, glow, gd, dsmall = take(9)
    hbm = take(9)
    gin, out_qkv, out_o, out_b, out_c, out_dqkv, out_do = take(7)
    eg, es, pout, mg, dg, dsh = take(6)
    ss, rs, ls = take(3)
    vmem = take(9)
    gm, gmid_low, gqkv, part, stage, recv, gbuf, yst, yrc, gmid_half = take(10)
    if gather:
        scat = [take(4) for _ in range(5)]
        own_w = take(4)
        smr, smz, pst, prc, pzs, pzr, pacc, pwhole = take(8)
    lc = Local(ls)
    loads = [lc.start(h, v) for h, v in zip(hbm, vmem)]
    wc, slope, wb, active, n2, wa, ctx, qkv, n1 = vmem
    cx = Ctx(ss, rs, dp)
    peers = [cx.core, cx.y, cx.x]
    if gather:
        peers += [cx.z(k) for k in range(1, dp)]
    cx.barrier(peers)
    m, s = cx.m, cx.s
    rows, width = gm.shape[1:]
    total = 4 * rows
    half = width // 2
    g_top = nt(glow[...], proj[...])
    gm[m] = g_top.astype(bf)
    g1 = GatherMp(cx, gm)
    unit_d = gd.shape[1] // 2
    if gather:
        hd = gd.shape[0] // 2
        qd = ScatterW(cx, hd // dp, gbuf, *scat[4])
        qd.start(gd[pl.ds(pl.multiple_of((1 - s) * hd, 16), hd), :])
        gbuf[...] = gd[pl.ds(pl.multiple_of(s * hd, 16), hd), :]
    else:
        yst[...] = gd[:, unit_d:].astype(bf)
        cyd = cx.send(yst, yrc, cx.y)
    p_part = tn(top[...], glow[...])
    if gather:
        pr = ProjSum(cx, pst, prc, pzs, pzr, pacc, pwhole, pout)
        pr.core(p_part)
    else:
        pout[...] = p_part

    def grad_halves(i, terms, out):
        def rows_of(sec):
            at = pl.ds(pl.multiple_of(sec * half, 128), half)
            return sum(tn(left[:, :, at].reshape(total, half), right) for left, right in terms)

        if gather:
            q = ScatterW(cx, half // dp, own_w[i], *scat[i])
            q.start(rows_of(1 - s))
            own_w[i][...] = rows_of(s)
            return q
        for sec in (0, 1):
            out[sec * half : (sec + 1) * half] = rows_of(jnp.int32(sec))

    if gather:
        pr.y()
    g1.finish()
    gm_all = gm[...].reshape(total, width)
    loads[0].wait()
    loads[1].wait()
    gh = (nn(gm_all, wc[...]) * slope[...].astype(f32)).astype(bf)
    loads[2].wait()
    if gather:
        pr.x()
    part[...] = nt(gh, wb[...]).reshape(part.shape)
    r1 = ReduceMp(cx, part, stage.at[0], recv.at[0])
    if gather:
        pr.z()
    r1.middle()
    if gather:
        qd.near()
        pr.back_z()
    loads[3].wait()
    loads[4].wait()
    qc = grad_halves(2, [(gm, active[...])], out_c)
    if gather:
        pr.back_x()
    g_n2 = r1.finish()
    grad_mid, gain_mid, shift_mid = normalize_back(mid[...], gains[1:2, :], g_n2)
    gmid = g_top + grad_mid
    gmid_half[...] = gmid
    gmid_low[m] = gmid.astype(bf)
    g2 = GatherMp(cx, gmid_low)
    if gather:
        qd.far()
    qb = grad_halves(3, [(n2, gh)], out_b)
    g2.finish()
    for c in loads[5:]:
        c.wait()
    gmid_all = gmid_low[...].reshape(total, width)
    cpad = ctx.shape[1]
    cut = width - cpad
    gcx = nn(gmid_all, wa[:, cut:]).astype(bf)
    shown = jnp.where(res[s] == 1, VIS, VIS_SMALL)
    bias = jnp.where(iota((1, total), 1) < shown, 0.0, NEG)
    scale = HD_ENC**-0.5
    scale2 = scale * LOG2E
    heads = (width // 4) // HD_ENC
    for h in range(heads):
        q = qkv[:, h * HD_ENC : (h + 1) * HD_ENC]
        k = qkv[:, (heads + h) * HD_ENC : (heads + h + 1) * HD_ENC]
        v = qkv[:, (2 * heads + h) * HD_ENC : (2 * heads + h + 1) * HD_ENC]
        go = gcx[:, (h + 1) * HD_ENC : (h + 2) * HD_ENC]
        co = ctx[:, (h + 1) * HD_ENC : (h + 2) * HD_ENC]
        scr = nt(q, k) + bias
        e = jnp.exp2((scr - jnp.max(scr, axis=1, keepdims=True)) * scale2)
        p = e / jnp.sum(e, axis=1, keepdims=True)
        delta = jnp.sum(go.astype(f32) * co.astype(f32), axis=1, keepdims=True)
        gs = (p * (nt(go, v) - delta) * scale).astype(bf)
        gqkv[:, h * HD_ENC : (h + 1) * HD_ENC] = nn(gs, k).astype(bf)
        gqkv[:, (heads + h) * HD_ENC : (heads + h + 1) * HD_ENC] = tn(gs, q).astype(bf)
        gqkv[:, (2 * heads + h) * HD_ENC : (2 * heads + h + 1) * HD_ENC] = tn(p.astype(bf), go).astype(bf)
        if gather and h == 0:
            pr.back_y()
        if gather and h == 1:
            qc.near()
    gqkv[:, 3 * heads * HD_ENC :] = jnp.zeros((total, width - 3 * heads * HD_ENC), bf)
    part[...] = nt(gqkv[...], wa[...]).reshape(part.shape)
    r2 = ReduceMp(cx, part, stage.at[1], recv.at[1])
    cols = (pl.ds(0, cut), pl.ds(cut, cpad))
    outs = (None, None) if gather else [out_qkv.at[:, c] for c in cols]
    qa = grad_halves(0, [(n1, gqkv[:, :cut])], outs[0])
    r2.middle()
    if gather:
        qc.far()
    qa2 = grad_halves(1, [(n1, gqkv[:, cut:]), (gmid_low, ctx[...])], outs[1])
    if gather:
        pr.back_core()
        qb.near()
        g = qd.finish()
        gbuf[0 : yst.shape[0], :unit_d] = g[:, :unit_d]
        yst[...] = g[:, unit_d:].astype(bf)
        cyd = cx.send(yst, yrc, cx.y)
    g_n1 = r2.finish()
    stream = x_all[s].astype(f32)
    grad_in, gain_in, shift_in = normalize_back(stream, gains[0:1, :], g_n1)
    grad = gmid_half[...] + grad_in
    part[0, :, :half] = grad[:, :half]
    part[1, :, :half] = grad[:, half:]
    gin[s] = part[s, :, :half]
    cin = cx.send(part.at[1 - s, :, pl.ds(0, half)], gin.at[s], cx.x)
    dw = dsmall.shape[1]
    vec = jnp.concatenate(
        [
            gain_in,
            gain_mid,
            shift_in,
            shift_mid,
            jnp.zeros((4, width), f32),
            jnp.concatenate([dsmall[...], jnp.zeros((8, width - dw), f32)], axis=1),
        ],
        axis=0,
    )
    if gather:
        smr[0] = vec
        c = cx.send(smr.at[0], smr.at[1], cx.core)
        qb.far()
        c.wait_recv()
        smr[2] = smr[0] + smr[1]
        c = cx.send(smr.at[2], smr.at[3], cx.y)
        c.wait_recv()
        smr[4] = smr[2] + smr[3]
        c = cx.send(smr.at[4], smr.at[5], cx.x)
        out_c[...] = qc.finish()
        pr.finish()
        qa.near()
        c.wait_recv()
        smz[cx.d] = smr[4] + smr[5]
        cs = [cx.send(smz.at[cx.d], smz.at[cx.d], cx.z(k)) for k in range(1, dp)]
        qa2.near()
        cyd.wait_recv()
        g = gbuf[0 : yst.shape[0], :unit_d] + yrc[...].astype(f32)
        unit = out_dqkv.shape[2]
        for t in range(3):
            out_dqkv[t] = g[:, t * unit : (t + 1) * unit]
        out_do[...] = g[:, 3 * unit :]
        out_b[...] = qb.finish()
        qa.far()
        for c in cs:
            c.wait_recv()
        vec = sum_in_order(smz, dp)
        qa2.far()
        g = jnp.concatenate([qa.finish(), qa2.finish()], axis=1)
        unit = out_qkv.shape[2]
        for t in range(3):
            out_qkv[t] = g[:, t * unit : (t + 1) * unit]
        out_o[...] = g[:, 3 * unit :].T
    else:
        cyd.wait_recv()
        out_dqkv[...] = gd[:, :unit_d] + yrc[...].astype(f32)
        out_do[...] = jnp.zeros(out_do.shape, f32)
        out_o[...] = jnp.zeros(out_o.shape, f32)
    eg[...] = vec[0:2]
    es[...] = vec[2:4]
    dg[...] = vec[8:10, :dw]
    dsh[...] = vec[10:12, :dw]
    mg[...] = vec[12:13, :dw]
    cin.wait_recv()
    cx.drain()


def sum_in_order(ref, n):
    out = ref[0]
    for i in range(1, n):
        out = out + ref[i]
    return out


class ProjSum:
    def __init__(self, cx, st, rc, zs, zr, acc, whole, out):
        self.cx, self.st, self.rc, self.zs, self.zr = cx, st, rc, zs, zr
        self.acc, self.whole, self.out = acc, whole, out
        self.R, self.C = out.shape

    def rows(self, start, size):
        return pl.ds(pl.multiple_of(start, 16), size)

    def core(self, part):
        cx, R = self.cx, self.R
        h = R // 2
        self.acc[...] = part
        self.o1 = cx.lo * h
        self.st[0:h] = self.acc[self.rows((1 - cx.lo) * h, h), :].astype(bf)
        self.c = cx.send(self.st.at[pl.ds(0, h)], self.rc.at[pl.ds(0, h)], cx.core)

    def step(self, prev_at, prev_size, bit, dev):
        cx, R = self.cx, self.R
        self.c.wait_recv()
        off = R - 2 * prev_size
        mine = self.rows(prev_at, prev_size)
        self.acc[mine, :] = self.acc[mine, :] + self.rc[off : off + prev_size, :].astype(f32)
        h = prev_size // 2
        noff = R - 2 * h
        self.st[noff : noff + h] = self.acc[self.rows(prev_at + (1 - bit) * h, h), :].astype(bf)
        self.c = cx.send(self.st.at[pl.ds(noff, h)], self.rc.at[pl.ds(noff, h)], dev)
        return prev_at + bit * h

    def y(self):
        self.o2 = self.step(self.o1, self.R // 2, self.cx.hi, self.cx.y)

    def x(self):
        self.o3 = self.step(self.o2, self.R // 4, self.cx.s, self.cx.x)

    def z(self):
        cx, R = self.cx, self.R
        size, unit = R // 8, self.C // cx.dp
        self.c.wait_recv()
        off = R - 2 * size
        total = self.acc[self.rows(self.o3, size), :] + self.rc[off : off + size, :].astype(f32)
        for e in range(cx.dp):
            self.zs[e] = total[:, e * unit : (e + 1) * unit].astype(bf)
        self.cs = []
        for k in range(1, cx.dp):
            to = lax.rem(cx.d + k, cx.dp)
            self.cs.append(cx.send(self.zs.at[to], self.zr.at[k - 1], cx.z(k)))

    def back_z(self):
        cx = self.cx
        unit = self.C // cx.dp
        total = self.zs[cx.d].astype(f32)
        for k in range(1, cx.dp):
            self.cs[k - 1].wait_recv()
            total = total + self.zr[k - 1].astype(f32)
        at = self.whole.at[self.rows(self.o3, self.R // 8), pl.ds(pl.multiple_of(cx.d * unit, 128), unit)]
        at[...] = total.astype(bf)
        self.cs = [cx.send(at, at, cx.z(k)) for k in range(1, cx.dp)]

    def back_x(self):
        for c in self.cs:
            c.wait_recv()
        at = self.rows(self.o3, self.R // 8)
        self.c = self.cx.send(self.whole.at[at], self.whole.at[at], self.cx.x)

    def back_y(self):
        self.c.wait_recv()
        at = self.rows(self.o2, self.R // 4)
        self.c = self.cx.send(self.whole.at[at], self.whole.at[at], self.cx.y)

    def back_core(self):
        self.c.wait_recv()
        at = self.rows(self.o1, self.R // 2)
        self.c = self.cx.send(self.whole.at[at], self.whole.at[at], self.cx.core)

    def finish(self):
        self.c.wait_recv()
        self.out[...] = self.whole[...].astype(f32)


def enc_backward(dp, gather, res, x, gains, proj, weights, saved, glow, gd, dsmall, ec, dc):
    wa, wb, wc = weights
    n1, n2, qkv, ctx, slope, active, mid, top = saved
    rows, width = x.shape[1:]
    total = 4 * rows
    V = pltpu.VMEM
    dd, dw = gd.shape[0], gd.shape[1] // 2
    er, dr = wa.shape[0] // (2 * dp), dd // (2 * dp)
    outs = [sds((2, rows, width // 2), f32)]
    if gather:
        outs += [sds((3, er, ec), f32), sds((ec, er), f32), sds((er, wb.shape[1]), f32), sds((er, wc.shape[1]), f32)]
        outs += [sds((3, dr, dc), f32), sds((dr, dc), f32)]
    else:
        outs += [sds(wa.shape, f32), sds((8, 128), f32), sds(wb.shape, f32), sds(wc.shape, f32)]
        outs += [sds((dd, dw), f32), sds((8, 128), f32)]
    outs += [sds((2, width), f32), sds((2, width), f32), sds(proj.shape, f32)]
    outs += [sds((1, dd), f32), sds((2, dd), f32), sds((2, dd), f32)]
    slots = (4, rows, width)
    hbm = (wc, slope, wb, active, n2, wa, ctx, qkv, n1)
    scratch = [
        pltpu.SemaphoreType.DMA((80,)),
        pltpu.SemaphoreType.DMA((80,)),
        pltpu.SemaphoreType.DMA((16,)),
    ]
    scratch += [V(a.shape, a.dtype) for a in hbm]
    scratch += [
        V(slots, bf),
        V(slots, bf),
        V((total, width), bf),
        V(slots, f32),
        V((2, 3, rows, width), bf),
        V((2, 3, rows, width), bf),
        V((dd // 2, 2 * dw) if gather else (8, 128), f32),
        V((dr if gather else dd, dw), bf),
        V((dr if gather else dd, dw), bf),
        V((rows, width), f32),
    ]
    if gather:
        cpad = ctx.shape[1]
        widths = (wa.shape[1] - cpad, cpad, wc.shape[1], wb.shape[1])
        for w in widths:
            scratch += scatter_scratch(dp, er, w)
        scratch += scatter_scratch(dp, dr, 2 * dw)
        scratch += [V((dp * er, w), f32) for w in widths]
        scratch += [
            V((6, 16, width), f32),
            V((dp, 16, width), f32),
            V(proj.shape, bf),
            V(proj.shape, bf),
            V((dp, proj.shape[0] // 8, proj.shape[1] // dp), bf),
            V((dp - 1, proj.shape[0] // 8, proj.shape[1] // dp), bf),
            V(proj.shape, f32),
            V(proj.shape, bf),
        ]
    return pl.pallas_call(
        functools.partial(enc_backward_kernel, dp, gather),
        out_shape=outs,
        in_specs=[SMEM] + vm(8) + anywhere(9),
        out_specs=vm(len(outs)),
        scratch_shapes=scratch,
        compiler_params=params(3),
        name="enc_backward",
    )(res, x, gains, proj, mid, top, glow, gd, dsmall, *hbm)


def place_kernel(n, *refs):
    for i in range(n):
        refs[n + i][...] = refs[i][...]


def place_outputs(arrays):
    n = len(arrays)
    return pl.pallas_call(
        functools.partial(place_kernel, n),
        out_shape=[sds(a.shape, a.dtype) for a in arrays],
        in_specs=vm(n),
        out_specs=vm(n),
        compiler_params=pltpu.CompilerParams(vmem_limit_bytes=60 << 20),
        name="place_outputs",
    )(*arrays)


def position_table(count, quarter):
    freq = (np.float32(10000.0) ** (-np.arange(quarter, dtype=np.float32) / np.float32(quarter))).astype(np.float32)
    angle = (np.arange(count, dtype=np.float32)[:, None] * freq[None, :]).astype(np.float32).astype(np.float64)
    return np.concatenate([np.sin(angle), np.cos(angle)], axis=1).astype(np.float32)


def per_device(
    x_visible,
    resolution,
    visible_index,
    enc_qkv_w,
    enc_out_w,
    enc_up_w,
    enc_down_w,
    enc_gains,
    enc_shifts,
    projection,
    mask_token,
    dec_qkv_w,
    dec_out_w,
    dec_up_w,
    dec_down_w,
    dec_gains,
    dec_shifts,
    cotangent,
):
    dp = lax.axis_size("dp")
    over = ("section", "dp")
    er, dr = enc_qkv_w.shape[0], dec_qkv_w.shape[0]
    de, dd = projection.shape
    ec, dc = enc_qkv_w.shape[2], dec_qkv_w.shape[2]
    gather = er % 16 == 0 and dr % 16 == 0 and dp == 4
    if gather:
        shards = [
            jnp.transpose(enc_qkv_w, (1, 0, 2)),
            enc_out_w,
            enc_up_w,
            enc_down_w.T,
            jnp.transpose(dec_qkv_w, (1, 0, 2)),
            dec_out_w.T,
        ]
        e_in, f_in = dec_up_w, dec_down_w.T
    else:
        whole = [
            lax.all_gather(w, over, axis=0, tiled=True)
            for w in (
                jnp.concatenate([enc_qkv_w.reshape(er, 3 * ec), enc_out_w.T], axis=1),
                enc_up_w,
                enc_down_w.T,
                jnp.concatenate([dec_qkv_w.reshape(dr, 3 * dc), dec_out_w.T], axis=1),
                dec_up_w,
                dec_down_w.T,
            )
        ]
        shards, (e_in, f_in) = whole[:4], whole[4:]
    weights, saved = enc_forward(
        dp,
        gather,
        resolution,
        x_visible,
        enc_gains,
        enc_shifts,
        projection,
        shards,
        de,
        dd,
        enc_up_w.shape[1],
        dec_up_w.shape[1],
    )
    table = jnp.asarray(position_table(COLS_BIG, dd // 4))
    out, glow, gd, ge, gf, dsmall, _ = decoder(
        dp,
        gather,
        resolution,
        visible_index,
        saved[8],
        table,
        cotangent,
        dec_gains,
        dec_shifts,
        mask_token[None, :],
        weights[3],
        e_in,
        f_in,
    )
    back = enc_backward(
        dp,
        gather,
        resolution,
        x_visible,
        enc_gains,
        projection,
        weights[:3],
        saved[:8],
        glow,
        gd,
        dsmall,
        ec,
        dc,
    )
    if gather:
        got = place_outputs((out, ge, gf) + tuple(back))
        out, ge, gf, gin, gqkv, go, gb, gc, hqkv, ho, eg, es, pg, mg, dg, ds = got
        gqkv = jnp.transpose(gqkv, (1, 0, 2))
        hqkv = jnp.transpose(hqkv, (1, 0, 2))
        ho = ho.T
    else:
        gin, ga, _, gb, gc, hd, _, eg, es, pg, mg, dg, ds = back
        ga, gb, gc, hd, ge, gf = [
            lax.psum_scatter(g, over, scatter_dimension=0, tiled=True) for g in (ga, gb, gc, hd, ge, gf)
        ]
        eg, es, pg, mg, dg, ds = lax.psum((eg, es, pg, mg, dg, ds), ("section", "dp", "mp"))
        gqkv, go = ga[:, : 3 * ec].reshape(er, 3, ec), ga[:, 3 * ec :].T
        hqkv, ho = hd[:, : 3 * dc].reshape(dr, 3, dc), hd[:, 3 * dc :].T
    return (out, gin, gqkv, go, gb, gc.T, eg, es, pg, mg[0], hqkv, ho, ge, gf.T, dg, ds)


def solution(mesh):
    matrix_in = P(("section", "dp"), "mp")
    matrix_out = P("mp", ("section", "dp"))
    qkv = P(("section", "dp"), None, "mp")
    return jax.shard_map(
        per_device,
        mesh=mesh,
        in_specs=(
            P("dp", "mp", None),
            P("dp"),
            P("dp", None),
            qkv,
            matrix_out,
            matrix_in,
            matrix_out,
            P(),
            P(),
            P(),
            P(),
            qkv,
            matrix_out,
            matrix_in,
            matrix_out,
            P(),
            P(),
            P("dp", "mp", None),
        ),
        out_specs=(
            P("dp", "mp", "section"),
            P("dp", "mp", "section"),
            qkv,
            matrix_out,
            matrix_in,
            matrix_out,
            P(),
            P(),
            P(),
            P(),
            qkv,
            matrix_out,
            matrix_in,
            matrix_out,
            P(),
            P(),
        ),
        check_vma=False,
    )
```

```python
import functools
import math

import jax
import jax.numpy as jnp
import numpy as np
from jax import lax
from jax.experimental import pallas as pl
from jax.experimental.pallas import tpu as pltpu
from jax.sharding import PartitionSpec as P

HD_ENC = 64
HD_DEC = 32
COLS_SMALL = 32
COLS_BIG = 64
PATCHES = 2048
SMALL_PATCHES = 512
VIS = 512
VIS_SMALL = 128

MESH = pl.DeviceIdType.MESH
bf = jnp.bfloat16
f32 = jnp.float32
LOG2E = 1.4426950408889634
NEG = -1e30


def nn(a, b):
    return lax.dot_general(a, b, (((1,), (0,)), ((), ())), preferred_element_type=f32)


def nt(a, b):
    return lax.dot_general(a, b, (((1,), (1,)), ((), ())), preferred_element_type=f32)


def tn(a, b):
    return lax.dot_general(a, b, (((0,), (0,)), ((), ())), preferred_element_type=f32)


def norm_stats(stream):
    centre = stream - jnp.mean(stream, axis=-1, keepdims=True)
    inverse = lax.rsqrt(jnp.mean(centre * centre, axis=-1, keepdims=True) + 1e-06)
    return centre * inverse, inverse


def normalize(stream, gain, shift):
    scaled, _ = norm_stats(stream)
    return scaled * gain + shift


def normalize_back(stream, gain, grad_out):
    scaled, inverse = norm_stats(stream)
    f = grad_out * gain
    grad_in = inverse * (
        f
        - jnp.mean(f, axis=-1, keepdims=True)
        - scaled * jnp.mean(f * scaled, axis=-1, keepdims=True)
    )
    return (
        grad_in,
        jnp.sum(grad_out * scaled, axis=0, keepdims=True),
        jnp.sum(grad_out, axis=0, keepdims=True),
    )


def gelu_and_slope(a):
    x = jnp.abs(a) * 0.7071067811865476
    t = 1.0 / (1.0 + 0.3275911 * x)
    e = jnp.exp2(x * x * (-LOG2E))
    poly = ((((1.061405429 * t - 1.453152027) * t + 1.421413741) * t - 0.284496736) * t + 0.254829592) * t
    tail = 0.5 * poly * e
    phi = jnp.where(a >= 0, 1.0 - tail, tail)
    return a * phi, phi + a * e * 0.3989422804014327


class Ctx:
    def __init__(self, ss, rs, dp):
        self.ss, self.rs, self.n, self.dp = ss, rs, 0, dp
        self.s = lax.axis_index("section")
        self.d = lax.axis_index("dp")
        self.m = lax.axis_index("mp")
        m = self.m
        self.lo = lax.rem(m, 2)
        self.hi = m // 2
        self.m1 = m + 1 - 2 * self.lo
        self.m2 = lax.rem(m + 2, 4)
        self.m3 = lax.rem(self.m1 + 2, 4)
        self.core = {"mp": self.m1}
        self.y = {"mp": self.m2}
        self.x = {"section": 1 - self.s}
        self.pending = []

    def z(self, k):
        return {"dp": lax.rem(self.d + k, self.dp)}

    def barrier(self, peers):
        b = pltpu.get_barrier_semaphore()
        for p in peers:
            pl.semaphore_signal(b, inc=1, device_id=p, device_id_type=MESH)
        pl.semaphore_wait(b, len(peers))

    def send(self, src, dst, dev):
        i = self.n
        self.n += 1
        c = pltpu.make_async_remote_copy(
            src_ref=src,
            dst_ref=dst,
            send_sem=self.ss.at[i],
            recv_sem=self.rs.at[i],
            device_id=dev,
            device_id_type=MESH,
        )
        c.start()
        self.pending.append(c)
        return c

    def sent(self, c):
        c.wait_send()
        self.pending = [p for p in self.pending if p is not c]

    def drain(self):
        for c in self.pending:
            c.wait_send()
        self.pending = []


class GatherMp:
    def __init__(self, cx, buf):
        self.cx, self.buf = cx, buf
        m = cx.m
        self.c2 = cx.send(buf.at[m], buf.at[m], cx.y)
        self.c1 = cx.send(buf.at[m], buf.at[m], cx.core)

    def forward(self):
        cx, buf = self.cx, self.buf
        self.c2.wait_recv()
        self.c3 = cx.send(buf.at[cx.m2], buf.at[cx.m2], cx.core)

    def near(self):
        self.c1.wait_recv()

    def far(self):
        self.c3.wait_recv()

    def finish(self):
        self.forward()
        self.near()
        self.far()


class ReduceMp:
    def __init__(self, cx, part, stage, recv):
        self.cx, self.part, self.stage, self.recv = cx, part, stage, recv
        stage[0] = part[cx.m3].astype(bf)
        self.c3 = cx.send(stage.at[0], recv.at[0], cx.core)
        stage[1] = part[cx.m1].astype(bf)
        self.c1 = cx.send(stage.at[1], recv.at[1], cx.core)

    def middle(self):
        cx = self.cx
        self.c3.wait_recv()
        self.stage[2] = (self.part[cx.m2] + self.recv[0].astype(f32)).astype(bf)
        self.c2 = cx.send(self.stage.at[2], self.recv.at[2], cx.y)

    def finish(self):
        self.c1.wait_recv()
        own = self.part[self.cx.m] + self.recv[1].astype(f32)
        self.c2.wait_recv()
        return own + self.recv[2].astype(f32)


def reduce_mp(cx, part, stage, recv):
    r = ReduceMp(cx, part, stage, recv)
    r.middle()
    return r.finish()


class GatherW:
    def __init__(self, cx, shard, whole):
        self.cx, self.whole, self.rows = cx, whole, shard.shape[0]
        own = self.at(cx.s, cx.d)
        self.zs = [cx.send(shard, own, cx.z(k)) for k in range(1, cx.dp)]
        self.xs = [cx.send(shard, own, cx.x)]
        own[...] = shard[...]

    def at(self, s, d):
        start = (s * self.cx.dp + d) * self.rows
        return self.whole.at[pl.ds(pl.multiple_of(start, 16), self.rows)]

    def forward(self):
        cx = self.cx
        for k in range(1, cx.dp):
            self.zs[k - 1].wait_recv()
            block = self.at(cx.s, lax.rem(cx.d + cx.dp - k, cx.dp))
            self.xs.append(cx.send(block, block, cx.x))

    def finish(self):
        for c in self.xs:
            c.wait_recv()


class RelayW:
    def __init__(self, cx, shard, whole):
        self.cx, self.whole, self.rows = cx, whole, shard.shape[0]
        dp, d = cx.dp, cx.d
        self.base = cx.n
        cx.n += 4 * dp
        self.own = self.at(cx.s, d)

        @pl.when(d < dp - 1)
        def _():
            self.make(shard, self.own, 1, {"dp": d + 1}).start()

        @pl.when(d > 0)
        def _():
            self.make(shard, self.own, dp + 1, {"dp": d - 1}).start()

        self.make(shard, self.own, 2 * dp, cx.x).start()
        self.own[...] = shard[...]

    def at(self, s, d):
        start = (s * self.cx.dp + d) * self.rows
        return self.whole.at[pl.ds(pl.multiple_of(start, 16), self.rows)]

    def make(self, src, dst, i, dev):
        cx, i = self.cx, self.base + i
        return pltpu.make_async_remote_copy(
            src_ref=src,
            dst_ref=dst,
            send_sem=cx.ss.at[i],
            recv_sem=cx.rs.at[i],
            device_id=dev,
            device_id_type=MESH,
        )

    def hop(self, k):
        cx, dp, d = self.cx, self.cx.dp, self.cx.d

        @pl.when(d >= k)
        def _():
            b = self.at(cx.s, jnp.maximum(d - k, 0))
            self.make(b, b, k, cx.x).wait_recv()

            @pl.when(d < dp - 1)
            def _():
                self.make(b, b, k + 1, {"dp": d + 1}).start()

            self.make(b, b, 2 * dp + k, cx.x).start()

        @pl.when(d + k < dp)
        def _():
            b = self.at(cx.s, jnp.minimum(d + k, dp - 1))
            self.make(b, b, dp + k, cx.x).wait_recv()

            @pl.when(d > 0)
            def _():
                self.make(b, b, dp + k + 1, {"dp": d - 1}).start()

            self.make(b, b, 3 * dp + k, cx.x).start()

    def finish(self):
        cx, dp, d = self.cx, self.cx.dp, self.cx.d
        other = lambda e: self.at(1 - cx.s, jnp.clip(e, 0, dp - 1))
        self.make(self.own, other(d), 2 * dp, cx.x).wait_recv()
        for k in range(1, dp):

            @pl.when(d >= k)
            def _():
                self.make(self.own, other(d - k), 2 * dp + k, cx.x).wait_recv()

            @pl.when(d + k < dp)
            def _():
                self.make(self.own, other(d + k), 3 * dp + k, cx.x).wait_recv()

    def drain(self):
        cx, dp, d = self.cx, self.cx.dp, self.cx.d
        own = self.own
        self.make(own, own, 2 * dp, cx.x).wait_send()
        for k in range(1, dp):

            @pl.when(d >= k)
            def _():
                self.make(own, own, 2 * dp + k, cx.x).wait_send()

            @pl.when(d + k < dp)
            def _():
                self.make(own, own, 3 * dp + k, cx.x).wait_send()

            @pl.when((d < dp - 1) & (d >= k - 1))
            def _():
                self.make(own, own, k, cx.x).wait_send()

            @pl.when((d > 0) & (d + k - 1 < dp))
            def _():
                self.make(own, own, dp + k, cx.x).wait_send()


class Local:
    def __init__(self, sems):
        self.sems, self.n, self.pending = sems, 0, []

    def start(self, src, dst):
        c = pltpu.make_async_copy(src, dst, self.sems.at[self.n])
        self.n += 1
        c.start()
        self.pending.append(c)
        return c

    def drain(self):
        for c in self.pending:
            c.wait()


class ScatterW:
    def __init__(self, cx, rows, own, xs, xr, zs, zr):
        self.cx, self.rows, self.own = cx, rows, own
        self.xs, self.xr, self.zs, self.zr = xs, xr, zs, zr

    def start(self, theirs):
        self.xs[...] = theirs.astype(bf)
        self.c = self.cx.send(self.xs, self.xr, self.cx.x)

    def at(self, e):
        return pl.ds(pl.multiple_of(e * self.rows, 16), self.rows)

    def near(self):
        cx = self.cx
        self.c.wait_recv()
        low = lax.rem(cx.d, 2)
        for j in range(2):
            at = self.at(2 * j + 1 - low)
            self.zs[j] = (self.own[at, :] + self.xr[at, :].astype(f32)).astype(bf)
        self.c = cx.send(self.zs.at[pl.ds(0, 2)], self.zr.at[pl.ds(0, 2)], {"dp": cx.d + 1 - 2 * low})

    def far(self):
        cx = self.cx
        low, high = lax.rem(cx.d, 2), cx.d // 2
        self.c.wait_recv()
        at = self.at(2 * (1 - high) + low)
        total = self.own[at, :] + self.xr[at, :].astype(f32) + self.zr[1 - high].astype(f32)
        self.zs[2] = total.astype(bf)
        self.c = cx.send(self.zs.at[2], self.zr.at[2], cx.z(2))

    def finish(self):
        at = self.at(self.cx.d)
        own = self.own[at, :] + self.xr[at, :].astype(f32) + self.zr[self.cx.d // 2].astype(f32)
        self.c.wait_recv()
        return own + self.zr[2].astype(f32)


def scatter_scratch(dp, rows, cols):
    half = dp * rows
    return [
        pltpu.VMEM((half, cols), bf),
        pltpu.VMEM((half, cols), bf),
        pltpu.VMEM((3, rows, cols), bf),
        pltpu.VMEM((3, rows, cols), bf),
    ]


def iota(shape, dim):
    return lax.broadcasted_iota(jnp.int32, shape, dim)


def enc_forward_kernel(dp, gather, *refs):
    it = iter(refs)
    take = lambda n: [next(it) for _ in range(n)]
    res, x_all, gains, shifts, proj = take(5)
    if gather:
        eqkv, eout, eup, edown, dqkv, dout = take(6)
        ha, hb, hc = take(3)
    else:
        wa, wb, wc, wd_in = take(4)
    wd, h1, h2, hq, hctx, hslope, hact, hmid, top_out, low_all = take(10)
    ss, rs, ls, part, stage, recv, n1, n2, qkv, ctx, slope, active, mid_s = take(13)
    if gather:
        wa, wb, wc, sa, sd, sdf = take(6)
    cx = Ctx(ss, rs, dp)
    lc = Local(ls)
    peers = [cx.core, cx.y]
    if gather:
        peers += [cx.x] + [cx.z(k) for k in range(1, dp)]
        wide = eqkv.shape[2]
        for t in range(3):
            sa[:, t * wide : (t + 1) * wide] = eqkv[t]
        sa[:, 3 * wide :] = eout[...].astype(f32).T.astype(bf)
        wide = dqkv.shape[2]
        for t in range(3):
            sd[:, t * wide : (t + 1) * wide] = dqkv[t]
        sd[:, 3 * wide : 4 * wide] = dout[...]
        both = 4 * wide
    cx.barrier(peers)
    if gather:
        cut = sa.shape[1] // 2
        ga = RelayW(cx, sa.at[:, pl.ds(0, cut)], wa.at[:, pl.ds(0, cut)])
        ga2 = RelayW(cx, sa.at[:, pl.ds(cut, cut)], wa.at[:, pl.ds(cut, cut)])
    stream = x_all[cx.s].astype(f32)
    n1[cx.m] = normalize(stream, gains[0:1, :], shifts[0:1, :]).astype(bf)
    g1 = GatherMp(cx, n1)
    if gather:
        csd = cx.send(sd.at[:, pl.ds(0, both)], sdf, cx.y)
        ga.hop(1)
        ga2.hop(1)
        ga.hop(2)
        ga2.hop(2)
        gb = RelayW(cx, eup, wb)
    g1.finish()
    lc.start(n1, h1)
    if gather:
        ga.hop(3)
        ga2.hop(3)
        gc = RelayW(cx, edown, wc)
        gb.hop(1)
        ga.finish()
        ga2.finish()
        lc.start(wa, ha)
    rows = n1.shape[1]
    total = 4 * rows
    width = n1.shape[2]
    n1_all = n1[...].reshape(total, width)
    qkv[...] = nn(n1_all, wa[...]).astype(bf)
    lc.start(qkv, hq)
    if gather:
        gb.hop(2)
        gc.hop(1)
        csd.wait_recv()
        sd[:, both:] = sdf[...]
        gd = RelayW(cx, sd, wd)
    shown = jnp.where(res[cx.s] == 1, VIS, VIS_SMALL)
    bias = jnp.where(iota((1, total), 1) < shown, 0.0, NEG)
    scale2 = HD_ENC**-0.5 * LOG2E
    heads = (width // 4) // HD_ENC
    pieces = [jnp.zeros((total, HD_ENC), bf)]
    for h in range(heads):
        q = qkv[:, h * HD_ENC : (h + 1) * HD_ENC]
        k = qkv[:, (heads + h) * HD_ENC : (heads + h + 1) * HD_ENC]
        v = qkv[:, (2 * heads + h) * HD_ENC : (2 * heads + h + 1) * HD_ENC]
        sc = nt(q, k) + bias
        top = jnp.max(sc, axis=1, keepdims=True)
        e = jnp.exp2((sc - top) * scale2)
        tot = jnp.sum(e, axis=1, keepdims=True)
        pieces.append((nn(e.astype(bf), v) / tot).astype(bf))
        if gather and h == 0:
            gb.hop(3)
        if gather and h == 1:
            gc.hop(2)
    ctx[...] = jnp.concatenate(pieces, axis=1)
    lc.start(ctx, hctx)
    cpad = ctx.shape[1]
    part[...] = nt(ctx[...], wa[:, width - cpad :]).reshape(part.shape)
    r1 = ReduceMp(cx, part, stage.at[0], recv.at[0])
    if gather:
        gd.hop(1)
    r1.middle()
    if gather:
        gc.hop(3)
    mid = stream + r1.finish()
    mid_s[...] = mid
    lc.start(mid_s, hmid)
    n2[cx.m] = normalize(mid, gains[1:2, :], shifts[1:2, :]).astype(bf)
    g2 = GatherMp(cx, n2)
    if gather:
        gd.hop(2)
        gb.finish()
        lc.start(wb, hb)
    g2.finish()
    lc.start(n2, h2)
    hid = nn(n2[...].reshape(total, width), wb[...])
    act, slo = gelu_and_slope(hid)
    active[...] = act.astype(bf)
    slope[...] = slo.astype(bf)
    lc.start(active, hact)
    lc.start(slope, hslope)
    if gather:
        gc.finish()
        lc.start(wc, hc)
    part[...] = nt(active[...], wc[...]).reshape(part.shape)
    r2 = ReduceMp(cx, part, stage.at[1], recv.at[1])
    r2.middle()
    if gather:
        gd.hop(3)
    top = (mid_s[...] + r2.finish()).astype(bf)
    top_out[...] = top
    low_all[cx.m] = nn(top, proj[...]).astype(bf)
    g3 = GatherMp(cx, low_all)
    if gather:
        gd.finish()
    else:
        both = wd_in.shape[1]
        wd[:, :both] = wd_in[...]
        cd = cx.send(wd_in, wd.at[:, pl.ds(both, both)], cx.y)
        cd.wait_recv()
    g3.finish()
    cx.drain()
    if gather:
        for g in (ga, ga2, gb, gc, gd):
            g.drain()
    lc.drain()


def vm(n):
    return [pl.BlockSpec(memory_space=pltpu.VMEM)] * n


def anywhere(n):
    return [pl.BlockSpec(memory_space=pl.ANY)] * n


SMEM = pl.BlockSpec(memory_space=pltpu.SMEM)


def sds(shape, dtype):
    return jax.ShapeDtypeStruct(shape, dtype)


def params(cid):
    return pltpu.CompilerParams(collective_id=cid, has_side_effects=True, vmem_limit_bytes=60 << 20)


def enc_forward(dp, gather, res, x, gains, shifts, proj, shards, de, dd, wide, dwide):
    rows, width = x.shape[1:]
    total = 4 * rows
    slots = (4, rows, width)
    V = pltpu.VMEM
    outs = []
    if gather:
        outs += [sds((de, de), bf), sds((de, wide), bf), sds((de, wide), bf)]
    outs += [sds((dd, 2 * dwide), bf)]
    big = [sds(slots, bf), sds(slots, bf), sds((total, width), bf), sds((total, 256), bf)]
    big += [sds((total, wide), bf), sds((total, wide), bf), sds((rows, width), f32)]
    outs += big + [sds((rows, width), bf), sds((4, rows, dd), bf)]
    scratch = [
        pltpu.SemaphoreType.DMA((112,)),
        pltpu.SemaphoreType.DMA((112,)),
        pltpu.SemaphoreType.DMA((16,)),
        V(slots, f32),
        V((2, 3, rows, width), bf),
        V((2, 3, rows, width), bf),
    ] + [V(b.shape, b.dtype) for b in big]
    if gather:
        scratch += [V(o.shape, bf) for o in outs[:3]]
        scratch += [V((shards[2].shape[0], de), bf), V((shards[5].shape[0], 2 * dwide), bf)]
        scratch += [V((shards[5].shape[0], dwide), bf)]
    got = pl.pallas_call(
        functools.partial(enc_forward_kernel, dp, gather),
        out_shape=outs,
        in_specs=[SMEM] + vm(4 + len(shards)),
        out_specs=anywhere(3 if gather else 0) + vm(1) + anywhere(7) + vm(2),
        scratch_shapes=scratch,
        compiler_params=params(1),
        name="enc_forward",
    )(res, x, gains, shifts, proj, *shards)
    if not gather:
        got = list(shards[:3]) + list(got)
    return got[:4], got[4:]


def dec_kernel(dp, gather, *refs):
    it = iter(refs)
    take = lambda n: [next(it) for _ in range(n)]
    res, chosen, low_all, table, cot, gains, shifts, token, wd_both, e_in, f_in = take(11)
    out, glow, gd, out_e, out_f, small, kept = take(7)
    ss, rs, we_both, wf_both, own_e, own_f, yst, yrc = take(8)
    if gather:
        se, sf, sfar = take(3)
        scat = (take(4), take(4))
    unit = wd_both.shape[1] // 2
    wd, we, wf = [[w.at[:, pl.ds(unit * g, unit)] for g in range(2)] for w in (wd_both, we_both, wf_both)]
    (n1, n2, gm, gmid_low, qg, kg, vg, gg, vtx, kt, dqt, lse, acc_s, top_s, ctx, active, slope) = take(17)
    ct = dqt
    (dkv, mid_s, start_s, res_s, part, fstage, frecv, far, prod, pstage, precv, masks) = take(12)
    sc_s, mx_s = take(2), take(2)
    p_s, tops, ps = take(3)
    cx = Ctx(ss, rs, dp)
    cx.barrier([cx.core, cx.y, cx.x] + ([cx.z(k) for k in range(1, dp)] if gather else []))
    rows, width = n1.shape[1:]
    m, lo, hi, s = cx.m, cx.lo, cx.hi, cx.s
    big = res[s] == 1
    shown = jnp.where(big, VIS, VIS_SMALL)
    filled = jnp.where(big, PATCHES, SMALL_PATCHES)
    pos_col = iota((rows, 1), 0) + m * rows
    live = jnp.where(pos_col < filled, 1.0, 0.0)
    ccot = pltpu.make_async_copy(cot.at[s], gm.at[lo], ps.at[0])
    ccot.start()
    ccot.wait()
    gm[lo] = (gm[lo].astype(f32) * live).astype(bf)
    cgm = cx.send(gm.at[lo], gm.at[lo], cx.core)
    if gather:
        cef = [cx.send(e_in, sfar.at[0], cx.y), cx.send(f_in, sfar.at[1], cx.y)]
        se[:, :unit] = e_in[...]
        sf[:, :unit] = f_in[...]
    else:
        we[0][...] = e_in[...]
        wf[0][...] = f_in[...]
        cef = [cx.send(e_in, we[1], cx.y), cx.send(f_in, wf[1], cx.y)]
    vis = chosen.shape[-1]

    def place_rows():
        return jnp.where((pos_col == chosen[pl.ds(s, 1), :]) & (iota((1, vis), 1) < shown), 1.0, 0.0)

    place = place_rows()
    seen = jnp.sum(place, axis=1, keepdims=True)
    weight = live - seen
    placed = nn(place.astype(bf), low_all[...].reshape(vis, width))
    half = width // 2
    nb, ns = rows // COLS_BIG, rows // COLS_SMALL
    rb = table[pl.ds(pl.multiple_of(m * nb, 8), nb), :]
    rsm = table[pl.ds(pl.multiple_of(m * ns, 8), ns), :]
    big_rows = jnp.broadcast_to(rb[:, None, :], (nb, COLS_BIG, half)).reshape(rows, half)
    small_rows = jnp.broadcast_to(rsm[:, None, :], (ns, COLS_SMALL, half)).reshape(rows, half)
    big_cols = jnp.broadcast_to(table[0:COLS_BIG, :][None], (nb, COLS_BIG, half)).reshape(rows, half)
    small_cols = jnp.broadcast_to(table[0:COLS_SMALL, :][None], (ns, COLS_SMALL, half)).reshape(rows, half)
    base = placed + weight * token[...]
    start_s[:, :half] = base[:, :half] + live * jnp.where(big, big_rows, small_rows)
    start_s[:, half:] = base[:, half:] + live * jnp.where(big, big_cols, small_cols)
    n1[m] = normalize(start_s[...], gains[0:1, :], shifts[0:1, :]).astype(bf)
    g1 = GatherMp(cx, n1)

    lane = iota((1, 256), 1)
    for j in range(4):
        head_lane = (lane < 128) & (lane // 32 == j)
        off = lane - (128 + 8 * j)
        masks[0, j] = jnp.where(head_lane | ((off >= 0) & (off < 3)) | (lane == 160), 1.0, 0.0).astype(bf)
        masks[1, j] = jnp.where(head_lane | ((off >= 0) & (off < 2)), 1.0, 0.0).astype(bf)
    aug = iota((1, 128), 1)
    total = 4 * rows
    key_bias = jnp.where(iota((total, 1), 0) < filled, 0.0, NEG)
    kaug = jnp.where(aug == 32, key_bias, jnp.where(aug < 32, 1.0, 0.0)).astype(bf)
    vaug = jnp.broadcast_to(jnp.where(aug < 32, 1.0, 0.0), (total, 128)).astype(bf)
    qaug = jnp.broadcast_to(jnp.where(aug == 32, 1.0, 0.0), (2 * rows, 128)).astype(bf)
    for g in range(2):
        kg[g, :, 128:] = kaug
        vg[g, :, 128:] = vaug
        qg[g, :, 128:] = qaug
    vtx[:, 32:, :] = jnp.ones((8, 16, total), bf)

    def keys_values(i, groups):
        at = pl.ds(pl.multiple_of(i * rows, 128), rows)
        for g in groups:
            kv = nn(n1[i], wd[g][:, 128:384])
            kg[g, at, :128] = kv[:, :128].astype(bf)
            vg[g, at, :128] = kv[:, 128:].astype(bf)
            kvt = kv.T.astype(bf)
            for j in range(4):
                kt[4 * g + j, :, at] = kvt[32 * j : 32 * j + 32]
                vtx[4 * g + j, 0:32, at] = kvt[128 + 32 * j : 160 + 32 * j]

    g1.near()

    def near_rows_in(g):
        for r in range(2):
            qg[g, r * rows : (r + 1) * rows, :128] = nn(n1[2 * hi + r], wd[g][:, :128]).astype(bf)
        keys_values(cx.m, (g,))
        keys_values(cx.m1, (g,))

    if gather:
        gats = []
        for i, (sh, w) in enumerate(((se, we_both), (sf, wf_both))):
            cef[i].wait_recv()
            sh[:, unit:] = sfar[i]
            gats.append(GatherW(cx, sh, w))
    near_rows_in(0)
    near_rows_in(1)
    c2 = HD_DEC**-0.5 * LOG2E

    def score(h, i, to):
        g, j = h // 4, lax.rem(h, 4)
        at = pl.ds(pl.multiple_of(i * rows, 128), rows)
        sc = nt(kg[g, at, :] * masks[0, j], qg[g])
        sc_s[to][...] = sc
        mx_s[to][...] = jnp.max(sc, axis=0, keepdims=True)

    def slot(n, h):
        return 2 * lax.rem(h, 2) + n

    def keep(n, h, i):
        return pltpu.make_async_copy(p_s.at[slot(n, h)], kept.at[h, i], ps.at[slot(n, h)])

    def fetch(n, h, i):
        return pltpu.make_async_copy(kept.at[h, i], p_s.at[slot(n, h)], ps.at[slot(n, h)])

    def head_pass(first, last, blocks, heads):
        def body(h, _):
            g, j = h // 4, lax.rem(h, 4)
            if first:
                top, acc = None, None
            else:
                top, acc = top_s[pl.ds(h, 1), :], acc_s[h]
            ahead = ((h, blocks[1]), (jnp.minimum(h + 1, 7), blocks[0]))
            for n, i in enumerate(blocks):
                at = pl.ds(pl.multiple_of(i * rows, 128), rows)
                if first and heads[0] == 0:

                    @pl.when(h > 1)
                    def _():
                        keep(n, h, i).wait()

                else:
                    keep(n, h, i).wait()
                mj = mx_s[n][...]
                new = mj if top is None else jnp.maximum(top, mj)
                tops[pl.ds(4 * h + i, 1), :] = new
                score(*ahead[n], 1 - n)
                p = jnp.exp2((sc_s[n][...] - new) * c2).astype(bf)
                p_s[slot(n, h)] = p
                o = nn(vtx[h, :, at], p)
                keep(n, h, i).start()
                acc = o if acc is None else acc * jnp.exp2((top - new) * c2) + o
                top = new
            if last:
                tot = acc[32:33, :]
                ct[h] = acc[:32, :] / tot
                at = pl.ds(pl.multiple_of(8 * j, 8), 8)
                lse[g, at, :] = jnp.broadcast_to(top + jnp.log(tot) * (LOG2E / c2), (8, top.shape[1]))
            else:
                top_s[pl.ds(h, 1), :] = top
                acc_s[h] = acc
            return 0

        lax.fori_loop(*heads, body, 0)

    score(jnp.int32(0), cx.m, 0)
    head_pass(True, False, (cx.m, cx.m1), (0, 6))
    g1.forward()
    if gather:
        gats[0].forward()
    head_pass(True, False, (cx.m, cx.m1), (6, 8))
    keys_values(cx.m2, (0, 1))
    g1.far()
    keys_values(cx.m3, (0, 1))
    score(jnp.int32(0), cx.m2, 0)
    head_pass(False, True, (cx.m2, cx.m3), (0, 4))
    if gather:
        gats[1].forward()
    head_pass(False, True, (cx.m2, cx.m3), (4, 8))
    for n, i in enumerate((cx.m2, cx.m3)):
        for h in (0, 1):
            keep(n, 6 + h, i).wait()
            fetch(n, h, i).start()
    for g in range(2):
        ctx[:, 128 * g : 128 * g + 128] = ct[4 * g : 4 * g + 4].reshape(128, 2 * rows).T.astype(bf)

    def chip_rows(r):
        return pl.ds(pl.multiple_of(r * rows, 128), rows)

    def out_rows(r):
        return sum(nt(ctx[chip_rows(r), 128 * g : 128 * g + 128], wd[g][:, 384:]) for g in range(2))

    fstage[0] = out_rows(1 - lo).astype(bf)
    co = cx.send(fstage.at[0], frecv.at[0], cx.core)
    mid = start_s[...] + out_rows(lo)
    co.wait_recv()
    mid = mid + frecv[0].astype(f32)
    mid_s[...] = mid
    n2[lo] = normalize(mid, gains[1:2, :], shifts[1:2, :]).astype(bf)
    cn2 = cx.send(n2.at[lo], n2.at[lo], cx.core)

    def mlp_rows(r):
        at = chip_rows(r)
        x = n2[r]
        y = None
        for g in range(2):
            a, b = gelu_and_slope(nn(x, we[g][...]))
            cols = slice(width * g, width * (g + 1))
            a = a.astype(bf)
            active[at, cols] = a
            slope[at, cols] = b.astype(bf)
            t = nt(a, wf[g][...])
            y = t if y is None else y + t
        return y

    if gather:
        for q in gats:
            q.finish()
    else:
        for c in cef:
            c.wait_recv()
    res_s[...] = mlp_rows(lo)
    cn2.wait_recv()
    fstage[1] = mlp_rows(1 - lo).astype(bf)
    c = cx.send(fstage.at[1], frecv.at[1], cx.core)

    cgm.wait_recv()

    def mlp_back_rows(r):
        at = chip_rows(r)
        y = None
        for g in range(2):
            cols = slice(width * g, width * (g + 1))
            ga = nn(gm[r], wf[g][...])
            gh = (ga * slope[at, cols].astype(f32)).astype(bf)
            slope[at, cols] = gh
            t = nt(gh, we[g][...])
            y = t if y is None else y + t
        return y

    fstage[2] = mlp_back_rows(1 - lo).astype(bf)
    cb = cx.send(fstage.at[2], frecv.at[2], cx.core)
    c.wait_recv()
    result = mid_s[...] + res_s[...] + frecv[1].astype(f32)
    result = result * live
    left, right = result[:, :half], result[:, half:]
    out[s] = jnp.where(s == 0, left, right).astype(bf)
    prod[...] = jnp.where(s == 0, right, left).astype(bf)
    cprod = cx.send(prod, out.at[s], cx.x)
    own = mlp_back_rows(lo)
    half_rows = width // 2

    def start_scatter(left, right, own, i, out):
        def rows_of(sec):
            at = pl.ds(pl.multiple_of(sec * half_rows, 128), half_rows)
            return tn(left[:, :, at].reshape(2 * rows, half_rows), right[...])

        if gather:
            q = ScatterW(cx, half_rows // dp, own, *scat[i])
            q.start(rows_of(1 - s))
            own[...] = rows_of(s)
            return q
        for sec in (0, 1):
            t = rows_of(jnp.int32(sec))
            at = slice(sec * half_rows, (sec + 1) * half_rows)
            out[at] = t[:, :unit]
            yst[i, at] = t[:, unit:].astype(bf)
        return cx.send(yst.at[i], yrc.at[i], cx.y)

    q_f = start_scatter(gm, active, own_f, 0, out_f)
    cb.wait_recv()
    grad_mid, gain_mid, shift_mid = normalize_back(mid_s[...], gains[1:2, :], own + frecv[2].astype(f32))
    gmid = gm[lo].astype(f32) + grad_mid
    mid_s[...] = gmid
    gmid_low[lo] = gmid.astype(bf)
    cgmid = cx.send(gmid_low.at[lo], gmid_low.at[lo], cx.core)
    q_e = start_scatter(n2, slope, own_e, 1, out_e)
    cgmid.wait_recv()
    gmid_all = gmid_low[...].reshape(2 * rows, width)
    sel = jnp.where(iota((128, 128), 0) // 32 == iota((128, 128), 1) // 8, 1.0, 0.0).astype(bf)
    lane128 = iota((1, 128), 1)
    t8 = lax.rem(lane128, 8)
    for g in range(2):
        gcg = nn(gmid_all, wd[g][:, 384:]).astype(bf)
        gg[g, :, :128] = gcg
        prodd = gcg.astype(f32) * ctx[:, 128 * g : 128 * g + 128].astype(f32)
        ph = prodd.astype(bf)
        plow = (prodd - ph.astype(f32)).astype(bf)
        delta = nn(ph, sel) + nn(plow, sel)
        dh = delta.astype(bf).astype(f32)
        daug = jnp.where(t8 == 0, -dh, jnp.where(t8 == 1, dh - delta, 0.0))
        gg[g, :, 128:] = jnp.where(lane128 < 32, daug, 0.0).astype(bf)
        gd[:, unit * g + 384 : unit * g + 512] = tn(gmid_all, ctx[:, 128 * g : 128 * g + 128])

    scale = HD_DEC**-0.5
    dqt[...] = jnp.zeros_like(dqt)
    head_lane = lane128 // 32

    def back_pass(blocks, heads, after):
        def body(h, _):
            g, j = h // 4, lax.rem(h, 4)
            mine = head_lane == j
            total_row = lse[g, pl.ds(pl.multiple_of(8 * j, 8), 8), :][0:1]
            for n, i in enumerate(blocks):
                at = pl.ds(pl.multiple_of(i * rows, 128), rows)
                fetch(n, h, i).wait()
                dpt = nt(vg[g, at, :] * masks[1, j], gg[g])
                share = jnp.exp2((tops[pl.ds(4 * h + i, 1), :] - total_row) * c2)
                p = p_s[slot(n, h)].astype(f32) * share
                ds = (p * dpt).astype(bf)
                dv = nn(p.astype(bf), gg[g, :, :128])
                dk = nn(ds, qg[g, :, :128]) * scale
                dkv[g, at, :128] = jnp.where(mine, dk, dkv[g, at, :128].astype(f32)).astype(bf)
                dkv[g, at, 128:] = jnp.where(mine, dv, dkv[g, at, 128:].astype(f32)).astype(bf)
                dqt[h] += nn(kt[h, :, at], ds)

                @pl.when(h < 6)
                def _():
                    fetch(n, h + 2, i).start()

                if after:

                    @pl.when(h >= 6)
                    def _():
                        fetch(n, h - 6, after[n]).start()

            return 0

        lax.fori_loop(*heads, body, 0)

    dkv[...] = jnp.zeros_like(dkv)
    back_pass((cx.m2, cx.m3), (0, 6), (cx.m, cx.m1))
    if gather:
        q_f.near()
    back_pass((cx.m2, cx.m3), (6, 8), (cx.m, cx.m1))

    def far_rows(r):
        at = pl.ds(pl.multiple_of((2 * (1 - hi) + r) * rows, 128), rows)
        return sum(nt(dkv[g, at, :], wd[g][:, 128:384]) for g in range(2))

    cx.sent(co)
    fstage[0] = far_rows(1 - lo).astype(bf)
    cf = cx.send(fstage.at[0], frecv.at[0], cx.core)
    res_s[...] = far_rows(lo)
    back_pass((cx.m, cx.m1), (0, 2), None)
    cf.wait_recv()
    cx.sent(cb)
    fstage[2] = (res_s[...] + frecv[0].astype(f32)).astype(bf)
    cfar = cx.send(fstage.at[2], far, cx.y)
    if gather:
        q_f.far()
        q_e.near()
    back_pass((cx.m, cx.m1), (2, 6), None)
    if gather:
        q_e.far()
        t = q_f.finish()
        out_f[...] = t[:, :unit]
        yst[0] = t[:, unit:].astype(bf)
        cyf = cx.send(yst.at[0], yrc.at[0], cx.y)
    back_pass((cx.m, cx.m1), (6, 8), None)
    for g in range(2):
        ctx[:, 128 * g : 128 * g + 128] = (dqt[4 * g : 4 * g + 4].reshape(128, 2 * rows).T * scale).astype(bf)

    def near_rows(r):
        at = pl.ds(pl.multiple_of((2 * hi + r) * rows, 128), rows)
        return sum(
            nt(ctx[chip_rows(r), 128 * g : 128 * g + 128], wd[g][:, :128]) + nt(dkv[g, at, :], wd[g][:, 128:384])
            for g in range(2)
        )

    cx.sent(c)
    fstage[1] = near_rows(1 - lo).astype(bf)
    cn = cx.send(fstage.at[1], frecv.at[1], cx.core)
    near = near_rows(lo)
    n1_chip = n1[pl.ds(2 * hi, 2)].reshape(2 * rows, width)
    t = tn(n1_chip, ctx[...])
    gd[:, :128] = t[:, :128]
    gd[:, unit : unit + 128] = t[:, 128:]
    cn.wait_recv()
    if gather:
        t = q_e.finish()
        out_e[...] = t[:, :unit]
        yst[1] = t[:, unit:].astype(bf)
        cye = cx.send(yst.at[1], yrc.at[1], cx.y)
    near = near + frecv[1].astype(f32)
    cfar.wait_recv()
    grad_in, gain_in, shift_in = normalize_back(start_s[...], gains[0:1, :], near + far[...].astype(f32))
    gstart = (mid_s[...] + grad_in).astype(bf)
    token_term = jnp.sum(weight * gstart.astype(f32), axis=0, keepdims=True)
    small[0:1] = gain_in
    small[1:2] = gain_mid
    small[2:3] = shift_in
    small[3:4] = shift_mid
    small[4:5] = token_term
    small[5:8] = jnp.zeros((3, width), f32)
    part[...] = tn(place_rows().astype(bf), gstart).reshape(part.shape)
    reduce = ReduceMp(cx, part, pstage, precv)
    n1_all = n1[...].reshape(total, width)
    gd[:, 128:384] = tn(n1_all, dkv[0])
    reduce.middle()
    gd[:, unit + 128 : unit + 384] = tn(n1_all, dkv[1])
    for c, o, i in ((cyf, out_f, 0), (cye, out_e, 1)) if gather else ((q_f, out_f, 0), (q_e, out_e, 1)):
        c.wait_recv()
        o[...] = o[...] + yrc[i].astype(f32)
    glow[...] = reduce.finish().astype(bf)
    cprod.wait_recv()
    cx.drain()


def decoder(dp, gather, res, chosen, low_all, table, cot, gains, shifts, token, wd, e_in, f_in):
    rows, width = cot.shape[1:]
    vis = chosen.shape[-1]
    total, chip = 4 * rows, 2 * rows
    unit = wd.shape[1] // 2
    half = (width // 2, 2 * unit)
    outs = [
        sds((2, rows, width // 2), bf),
        sds((vis // 4, width), bf),
        sds(wd.shape, f32),
        sds(e_in.shape, f32),
        sds(f_in.shape, f32),
        sds((8, width), f32),
        sds((8, 4, rows, chip), bf),
    ]
    V = pltpu.VMEM
    extra = []
    if gather:
        pair = (e_in.shape[0], 2 * unit)
        extra = [V(pair, bf), V(pair, bf), V((2,) + e_in.shape, bf)] + 2 * scatter_scratch(dp, *pair)
    return pl.pallas_call(
        functools.partial(dec_kernel, dp, gather),
        out_shape=outs,
        in_specs=[SMEM] + vm(3) + anywhere(1) + vm(6),
        out_specs=vm(len(outs) - 1) + anywhere(1),
        scratch_shapes=[
            pltpu.SemaphoreType.DMA((64,)),
            pltpu.SemaphoreType.DMA((64,)),
            V(wd.shape, bf),
            V(wd.shape, bf),
            V(half, f32),
            V(half, f32),
            V((2,) + e_in.shape, bf),
            V((2,) + e_in.shape, bf),
        ]
        + extra
        + [
            V((4, rows, width), bf),
            V((2, rows, width), bf),
            V((2, rows, width), bf),
            V((2, rows, width), bf),
            V((2, chip, 256), bf),
            V((2, total, 256), bf),
            V((2, total, 256), bf),
            V((2, chip, 256), bf),
            V((8, 48, total), bf),
            V((8, 32, total), bf),
            V((8, 32, chip), f32),
            V((2, 32, chip), f32),
            V((8, 48, chip), f32),
            V((8, chip), f32),
            V((chip, 256), bf),
            V((chip, 2 * width), bf),
            V((chip, 2 * width), bf),
            V((2, total, 256), bf),
            V((rows, width), f32),
            V((rows, width), f32),
            V((rows, width), f32),
            V((4, vis // 4, width), f32),
            V((3, rows, width), bf),
            V((3, rows, width), bf),
            V((rows, width), bf),
            V((rows, width // 2), bf),
            V((3, vis // 4, width), bf),
            V((3, vis // 4, width), bf),
            V((2, 4, 1, 256), bf),
            V((rows, chip), f32),
            V((rows, chip), f32),
            V((1, chip), f32),
            V((1, chip), f32),
            V((4, rows, chip), bf),
            V((32, chip), f32),
            pltpu.SemaphoreType.DMA((4,)),
        ],
        compiler_params=params(2),
        name="decoder",
    )(res, chosen, low_all, table, cot, gains, shifts, token, wd, e_in, f_in)


def enc_backward_kernel(dp, gather, *refs):
    it = iter(refs)
    take = lambda n: [next(it) for _ in range(n)]
    res, x_all, gains, proj, mid, top, glow, gd, dsmall = take(9)
    hbm = take(9)
    gin, out_qkv, out_o, out_b, out_c, out_dqkv, out_do = take(7)
    eg, es, pout, mg, dg, dsh = take(6)
    ss, rs, ls = take(3)
    vmem = take(9)
    gm, gmid_low, gqkv, part, stage, recv, gbuf, yst, yrc, gmid_half = take(10)
    if gather:
        scat = [take(4) for _ in range(5)]
        own_w = take(4)
        smr, smz, pst, prc, pzs, pzr, pacc, pwhole = take(8)
    lc = Local(ls)
    loads = [lc.start(h, v) for h, v in zip(hbm, vmem)]
    wc, slope, wb, active, n2, wa, ctx, qkv, n1 = vmem
    cx = Ctx(ss, rs, dp)
    peers = [cx.core, cx.y, cx.x]
    if gather:
        peers += [cx.z(k) for k in range(1, dp)]
    cx.barrier(peers)
    m, s = cx.m, cx.s
    rows, width = gm.shape[1:]
    total = 4 * rows
    half = width // 2
    g_top = nt(glow[...], proj[...])
    gm[m] = g_top.astype(bf)
    g1 = GatherMp(cx, gm)
    unit_d = gd.shape[1] // 2
    if gather:
        hd = gd.shape[0] // 2
        qd = ScatterW(cx, hd // dp, gbuf, *scat[4])
        qd.start(gd[pl.ds(pl.multiple_of((1 - s) * hd, 16), hd), :])
        gbuf[...] = gd[pl.ds(pl.multiple_of(s * hd, 16), hd), :]
    else:
        yst[...] = gd[:, unit_d:].astype(bf)
        cyd = cx.send(yst, yrc, cx.y)
    p_part = tn(top[...], glow[...])
    if gather:
        pr = ProjSum(cx, pst, prc, pzs, pzr, pacc, pwhole, pout)
        pr.core(p_part)
    else:
        pout[...] = p_part

    def rows_of(sec, terms):
        at = pl.ds(pl.multiple_of(sec * half, 128), half)
        return sum(tn(left[:, :, at].reshape(total, half), right) for left, right in terms)

    def grad_theirs(i, terms):
        if not gather:
            return None
        q = ScatterW(cx, half // dp, own_w[i], *scat[i])
        q.start(rows_of(1 - s, terms))
        return q

    def grad_ours(i, terms, out):
        if gather:
            own_w[i][...] = rows_of(s, terms)
            return
        for sec in (0, 1):
            out[sec * half : (sec + 1) * half] = rows_of(jnp.int32(sec), terms)

    if gather:
        pr.y()
    g1.finish()
    gm_all = gm[...].reshape(total, width)
    loads[0].wait()
    loads[1].wait()
    gh = (nn(gm_all, wc[...]) * slope[...].astype(f32)).astype(bf)
    if gather:
        pr.x()
    loads[2].wait()
    loads[3].wait()
    terms_c = [(gm, active[...])]
    qc = grad_theirs(2, terms_c)
    part[...] = nt(gh, wb[...]).reshape(part.shape)
    r1 = ReduceMp(cx, part, stage.at[0], recv.at[0])
    if gather:
        qd.near()
    r1.middle()
    if gather:
        pr.z()
    loads[4].wait()
    grad_ours(2, terms_c, out_c)
    g_n2 = r1.finish()
    grad_mid, gain_mid, shift_mid = normalize_back(mid[...], gains[1:2, :], g_n2)
    gmid = g_top + grad_mid
    gmid_half[...] = gmid
    gmid_low[m] = gmid.astype(bf)
    g2 = GatherMp(cx, gmid_low)
    if gather:
        pr.back_z()
        qd.far()
    terms_b = [(n2, gh)]
    qb = grad_theirs(3, terms_b)
    if gather:
        pr.back_x()
    grad_ours(3, terms_b, out_b)
    g2.finish()
    for c in loads[5:]:
        c.wait()
    gmid_all = gmid_low[...].reshape(total, width)
    cpad = ctx.shape[1]
    cut = width - cpad
    gcx = nn(gmid_all, wa[:, cut:]).astype(bf)
    shown = jnp.where(res[s] == 1, VIS, VIS_SMALL)
    bias = jnp.where(iota((1, total), 1) < shown, 0.0, NEG)
    scale = HD_ENC**-0.5
    scale2 = scale * LOG2E
    heads = (width // 4) // HD_ENC
    for h in range(heads):
        q = qkv[:, h * HD_ENC : (h + 1) * HD_ENC]
        k = qkv[:, (heads + h) * HD_ENC : (heads + h + 1) * HD_ENC]
        v = qkv[:, (2 * heads + h) * HD_ENC : (2 * heads + h + 1) * HD_ENC]
        go = gcx[:, (h + 1) * HD_ENC : (h + 2) * HD_ENC]
        co = ctx[:, (h + 1) * HD_ENC : (h + 2) * HD_ENC]
        scr = nt(q, k) + bias
        e = jnp.exp2((scr - jnp.max(scr, axis=1, keepdims=True)) * scale2)
        p = e / jnp.sum(e, axis=1, keepdims=True)
        delta = jnp.sum(go.astype(f32) * co.astype(f32), axis=1, keepdims=True)
        gs = (p * (nt(go, v) - delta) * scale).astype(bf)
        gqkv[:, h * HD_ENC : (h + 1) * HD_ENC] = nn(gs, k).astype(bf)
        gqkv[:, (heads + h) * HD_ENC : (heads + h + 1) * HD_ENC] = tn(gs, q).astype(bf)
        gqkv[:, (2 * heads + h) * HD_ENC : (2 * heads + h + 1) * HD_ENC] = tn(p.astype(bf), go).astype(bf)
        if gather and h == 0:
            qc.near()
    gqkv[:, 3 * heads * HD_ENC :] = jnp.zeros((total, width - 3 * heads * HD_ENC), bf)
    part[...] = nt(gqkv[...], wa[...]).reshape(part.shape)
    r2 = ReduceMp(cx, part, stage.at[1], recv.at[1])
    cols = (pl.ds(0, cut), pl.ds(cut, cpad))
    outs = (None, None) if gather else [out_qkv.at[:, c] for c in cols]
    terms_a = [(n1, gqkv[:, :cut])]
    terms_a2 = [(n1, gqkv[:, cut:]), (gmid_low, ctx[...])]
    qa = grad_theirs(0, terms_a)
    r2.middle()
    qa2 = grad_theirs(1, terms_a2)
    if gather:
        qb.near()
        qc.far()
        pr.back_y()
    grad_ours(0, terms_a, outs[0])
    grad_ours(1, terms_a2, outs[1])
    g_n1 = r2.finish()
    stream = x_all[s].astype(f32)
    grad_in, gain_in, shift_in = normalize_back(stream, gains[0:1, :], g_n1)
    grad = gmid_half[...] + grad_in
    dw = dsmall.shape[1]
    vec = jnp.concatenate(
        [
            gain_in,
            gain_mid,
            shift_in,
            shift_mid,
            jnp.zeros((4, width), f32),
            jnp.concatenate([dsmall[...], jnp.zeros((8, width - dw), f32)], axis=1),
        ],
        axis=0,
    )
    if gather:
        smr[0] = vec
        c = cx.send(smr.at[0], smr.at[1], cx.core)
        g = qd.finish()
        gbuf[0 : yst.shape[0], :unit_d] = g[:, :unit_d]
        yst[...] = g[:, unit_d:].astype(bf)
        c.wait_recv()
        smr[2] = smr[0] + smr[1]
        c = cx.send(smr.at[2], smr.at[3], cx.y)
        qb.far()
        qa.near()
        c.wait_recv()
        smr[4] = smr[2] + smr[3]
        c = cx.send(smr.at[4], smr.at[5], cx.x)
        pr.back_core()
        cyd = cx.send(yst, yrc, cx.y)
    part[0, :, :half] = grad[:, :half]
    part[1, :, :half] = grad[:, half:]
    gin[s] = part[s, :, :half]
    cin = cx.send(part.at[1 - s, :, pl.ds(0, half)], gin.at[s], cx.x)
    if gather:
        out_c[...] = qc.finish()
        qa2.near()
        qa.far()
        c.wait_recv()
        smz[cx.d] = smr[4] + smr[5]
        cs = [cx.send(smz.at[cx.d], smz.at[cx.d], cx.z(k)) for k in range(1, dp)]
        cyd.wait_recv()
        g = gbuf[0 : yst.shape[0], :unit_d] + yrc[...].astype(f32)
        unit = out_dqkv.shape[2]
        for t in range(3):
            out_dqkv[t] = g[:, t * unit : (t + 1) * unit]
        out_do[...] = g[:, 3 * unit :]
        qa2.far()
        pr.finish()
        out_b[...] = qb.finish()
        for c in cs:
            c.wait_recv()
        vec = sum_in_order(smz, dp)
        g = jnp.concatenate([qa.finish(), qa2.finish()], axis=1)
        unit = out_qkv.shape[2]
        for t in range(3):
            out_qkv[t] = g[:, t * unit : (t + 1) * unit]
        out_o[...] = g[:, 3 * unit :].T
    else:
        cyd.wait_recv()
        out_dqkv[...] = gd[:, :unit_d] + yrc[...].astype(f32)
        out_do[...] = jnp.zeros(out_do.shape, f32)
        out_o[...] = jnp.zeros(out_o.shape, f32)
    eg[...] = vec[0:2]
    es[...] = vec[2:4]
    dg[...] = vec[8:10, :dw]
    dsh[...] = vec[10:12, :dw]
    mg[...] = vec[12:13, :dw]
    cin.wait_recv()
    cx.drain()


def sum_in_order(ref, n):
    out = ref[0]
    for i in range(1, n):
        out = out + ref[i]
    return out


class ProjSum:
    def __init__(self, cx, st, rc, zs, zr, acc, whole, out):
        self.cx, self.st, self.rc, self.zs, self.zr = cx, st, rc, zs, zr
        self.acc, self.whole, self.out = acc, whole, out
        self.R, self.C = out.shape

    def rows(self, start, size):
        return pl.ds(pl.multiple_of(start, 16), size)

    def core(self, part):
        cx, R = self.cx, self.R
        h = R // 2
        self.acc[...] = part
        self.o1 = cx.lo * h
        self.st[0:h] = self.acc[self.rows((1 - cx.lo) * h, h), :].astype(bf)
        self.c = cx.send(self.st.at[pl.ds(0, h)], self.rc.at[pl.ds(0, h)], cx.core)

    def step(self, prev_at, prev_size, bit, dev):
        cx, R = self.cx, self.R
        self.c.wait_recv()
        off = R - 2 * prev_size
        mine = self.rows(prev_at, prev_size)
        self.acc[mine, :] = self.acc[mine, :] + self.rc[off : off + prev_size, :].astype(f32)
        h = prev_size // 2
        noff = R - 2 * h
        self.st[noff : noff + h] = self.acc[self.rows(prev_at + (1 - bit) * h, h), :].astype(bf)
        self.c = cx.send(self.st.at[pl.ds(noff, h)], self.rc.at[pl.ds(noff, h)], dev)
        return prev_at + bit * h

    def y(self):
        self.o2 = self.step(self.o1, self.R // 2, self.cx.hi, self.cx.y)

    def x(self):
        self.o3 = self.step(self.o2, self.R // 4, self.cx.s, self.cx.x)

    def z(self):
        cx, R = self.cx, self.R
        size, unit = R // 8, self.C // cx.dp
        self.c.wait_recv()
        off = R - 2 * size
        total = self.acc[self.rows(self.o3, size), :] + self.rc[off : off + size, :].astype(f32)
        for e in range(cx.dp):
            self.zs[e] = total[:, e * unit : (e + 1) * unit].astype(bf)
        self.cs = []
        for k in range(1, cx.dp):
            to = lax.rem(cx.d + k, cx.dp)
            self.cs.append(cx.send(self.zs.at[to], self.zr.at[k - 1], cx.z(k)))

    def back_z(self):
        cx = self.cx
        unit = self.C // cx.dp
        total = self.zs[cx.d].astype(f32)
        for k in range(1, cx.dp):
            self.cs[k - 1].wait_recv()
            total = total + self.zr[k - 1].astype(f32)
        at = self.whole.at[self.rows(self.o3, self.R // 8), pl.ds(pl.multiple_of(cx.d * unit, 128), unit)]
        at[...] = total.astype(bf)
        self.cs = [cx.send(at, at, cx.z(k)) for k in range(1, cx.dp)]

    def back_x(self):
        for c in self.cs:
            c.wait_recv()
        at = self.rows(self.o3, self.R // 8)
        self.c = self.cx.send(self.whole.at[at], self.whole.at[at], self.cx.x)

    def back_y(self):
        self.c.wait_recv()
        at = self.rows(self.o2, self.R // 4)
        self.c = self.cx.send(self.whole.at[at], self.whole.at[at], self.cx.y)

    def back_core(self):
        self.c.wait_recv()
        at = self.rows(self.o1, self.R // 2)
        self.c = self.cx.send(self.whole.at[at], self.whole.at[at], self.cx.core)

    def finish(self):
        self.c.wait_recv()
        self.out[...] = self.whole[...].astype(f32)


def enc_backward(dp, gather, res, x, gains, proj, weights, saved, glow, gd, dsmall, ec, dc):
    wa, wb, wc = weights
    n1, n2, qkv, ctx, slope, active, mid, top = saved
    rows, width = x.shape[1:]
    total = 4 * rows
    V = pltpu.VMEM
    dd, dw = gd.shape[0], gd.shape[1] // 2
    er, dr = wa.shape[0] // (2 * dp), dd // (2 * dp)
    outs = [sds((2, rows, width // 2), f32)]
    if gather:
        outs += [sds((3, er, ec), f32), sds((ec, er), f32), sds((er, wb.shape[1]), f32), sds((er, wc.shape[1]), f32)]
        outs += [sds((3, dr, dc), f32), sds((dr, dc), f32)]
    else:
        outs += [sds(wa.shape, f32), sds((8, 128), f32), sds(wb.shape, f32), sds(wc.shape, f32)]
        outs += [sds((dd, dw), f32), sds((8, 128), f32)]
    outs += [sds((2, width), f32), sds((2, width), f32), sds(proj.shape, f32)]
    outs += [sds((1, dd), f32), sds((2, dd), f32), sds((2, dd), f32)]
    slots = (4, rows, width)
    hbm = (wc, slope, wb, active, n2, wa, ctx, qkv, n1)
    scratch = [
        pltpu.SemaphoreType.DMA((80,)),
        pltpu.SemaphoreType.DMA((80,)),
        pltpu.SemaphoreType.DMA((16,)),
    ]
    scratch += [V(a.shape, a.dtype) for a in hbm]
    scratch += [
        V(slots, bf),
        V(slots, bf),
        V((total, width), bf),
        V(slots, f32),
        V((2, 3, rows, width), bf),
        V((2, 3, rows, width), bf),
        V((dd // 2, 2 * dw) if gather else (8, 128), f32),
        V((dr if gather else dd, dw), bf),
        V((dr if gather else dd, dw), bf),
        V((rows, width), f32),
    ]
    if gather:
        cpad = ctx.shape[1]
        widths = (wa.shape[1] - cpad, cpad, wc.shape[1], wb.shape[1])
        for w in widths:
            scratch += scatter_scratch(dp, er, w)
        scratch += scatter_scratch(dp, dr, 2 * dw)
        scratch += [V((dp * er, w), f32) for w in widths]
        scratch += [
            V((6, 16, width), f32),
            V((dp, 16, width), f32),
            V(proj.shape, bf),
            V(proj.shape, bf),
            V((dp, proj.shape[0] // 8, proj.shape[1] // dp), bf),
            V((dp - 1, proj.shape[0] // 8, proj.shape[1] // dp), bf),
            V(proj.shape, f32),
            V(proj.shape, bf),
        ]
    return pl.pallas_call(
        functools.partial(enc_backward_kernel, dp, gather),
        out_shape=outs,
        in_specs=[SMEM] + vm(8) + anywhere(9),
        out_specs=vm(len(outs)),
        scratch_shapes=scratch,
        compiler_params=params(3),
        name="enc_backward",
    )(res, x, gains, proj, mid, top, glow, gd, dsmall, *hbm)


def place_kernel(n, *refs):
    ins, outs, held = refs[:n], refs[n : 2 * n], refs[2 * n : 3 * n]
    sems = refs[3 * n]
    reads = [pltpu.make_async_copy(ins[i], held[i], sems.at[0, i]) for i in range(n)]
    writes = [pltpu.make_async_copy(held[i], outs[i], sems.at[1, i]) for i in range(n)]
    for c in reads:
        c.start()
    for r, w in zip(reads, writes):
        r.wait()
        w.start()
    for c in writes:
        c.wait()


def place_outputs(arrays):
    n = len(arrays)
    return pl.pallas_call(
        functools.partial(place_kernel, n),
        out_shape=[sds(a.shape, a.dtype) for a in arrays],
        in_specs=anywhere(n),
        out_specs=anywhere(n),
        scratch_shapes=[pltpu.VMEM(a.shape, a.dtype) for a in arrays] + [pltpu.SemaphoreType.DMA((2, n))],
        compiler_params=pltpu.CompilerParams(vmem_limit_bytes=60 << 20),
        name="place_outputs",
    )(*arrays)


def position_table(count, quarter):
    freq = (np.float32(10000.0) ** (-np.arange(quarter, dtype=np.float32) / np.float32(quarter))).astype(np.float32)
    angle = (np.arange(count, dtype=np.float32)[:, None] * freq[None, :]).astype(np.float32).astype(np.float64)
    return np.concatenate([np.sin(angle), np.cos(angle)], axis=1).astype(np.float32)


def per_device(
    x_visible,
    resolution,
    visible_index,
    enc_qkv_w,
    enc_out_w,
    enc_up_w,
    enc_down_w,
    enc_gains,
    enc_shifts,
    projection,
    mask_token,
    dec_qkv_w,
    dec_out_w,
    dec_up_w,
    dec_down_w,
    dec_gains,
    dec_shifts,
    cotangent,
):
    dp = lax.axis_size("dp")
    over = ("section", "dp")
    er, dr = enc_qkv_w.shape[0], dec_qkv_w.shape[0]
    de, dd = projection.shape
    ec, dc = enc_qkv_w.shape[2], dec_qkv_w.shape[2]
    gather = er % 16 == 0 and dr % 16 == 0 and dp == 4
    if gather:
        shards = [
            jnp.transpose(enc_qkv_w, (1, 0, 2)),
            enc_out_w,
            enc_up_w,
            enc_down_w.T,
            jnp.transpose(dec_qkv_w, (1, 0, 2)),
            dec_out_w.T,
        ]
        e_in, f_in = dec_up_w, dec_down_w.T
    else:
        whole = [
            lax.all_gather(w, over, axis=0, tiled=True)
            for w in (
                jnp.concatenate([enc_qkv_w.reshape(er, 3 * ec), enc_out_w.T], axis=1),
                enc_up_w,
                enc_down_w.T,
                jnp.concatenate([dec_qkv_w.reshape(dr, 3 * dc), dec_out_w.T], axis=1),
                dec_up_w,
                dec_down_w.T,
            )
        ]
        shards, (e_in, f_in) = whole[:4], whole[4:]
    weights, saved = enc_forward(
        dp,
        gather,
        resolution,
        x_visible,
        enc_gains,
        enc_shifts,
        projection,
        shards,
        de,
        dd,
        enc_up_w.shape[1],
        dec_up_w.shape[1],
    )
    table = jnp.asarray(position_table(COLS_BIG, dd // 4))
    out, glow, gd, ge, gf, dsmall, _ = decoder(
        dp,
        gather,
        resolution,
        visible_index,
        saved[8],
        table,
        cotangent,
        dec_gains,
        dec_shifts,
        mask_token[None, :],
        weights[3],
        e_in,
        f_in,
    )
    back = enc_backward(
        dp,
        gather,
        resolution,
        x_visible,
        enc_gains,
        projection,
        weights[:3],
        saved[:8],
        glow,
        gd,
        dsmall,
        ec,
        dc,
    )
    if gather:
        got = place_outputs((out, ge, gf) + tuple(back))
        out, ge, gf, gin, gqkv, go, gb, gc, hqkv, ho, eg, es, pg, mg, dg, ds = got
        gqkv = jnp.transpose(gqkv, (1, 0, 2))
        hqkv = jnp.transpose(hqkv, (1, 0, 2))
        ho = ho.T
    else:
        gin, ga, _, gb, gc, hd, _, eg, es, pg, mg, dg, ds = back
        ga, gb, gc, hd, ge, gf = [
            lax.psum_scatter(g, over, scatter_dimension=0, tiled=True) for g in (ga, gb, gc, hd, ge, gf)
        ]
        eg, es, pg, mg, dg, ds = lax.psum((eg, es, pg, mg, dg, ds), ("section", "dp", "mp"))
        gqkv, go = ga[:, : 3 * ec].reshape(er, 3, ec), ga[:, 3 * ec :].T
        hqkv, ho = hd[:, : 3 * dc].reshape(dr, 3, dc), hd[:, 3 * dc :].T
    return (out, gin, gqkv, go, gb, gc.T, eg, es, pg, mg[0], hqkv, ho, ge, gf.T, dg, ds)


def solution(mesh):
    matrix_in = P(("section", "dp"), "mp")
    matrix_out = P("mp", ("section", "dp"))
    qkv = P(("section", "dp"), None, "mp")
    return jax.shard_map(
        per_device,
        mesh=mesh,
        in_specs=(
            P("dp", "mp", None),
            P("dp"),
            P("dp", None),
            qkv,
            matrix_out,
            matrix_in,
            matrix_out,
            P(),
            P(),
            P(),
            P(),
            qkv,
            matrix_out,
            matrix_in,
            matrix_out,
            P(),
            P(),
            P("dp", "mp", None),
        ),
        out_specs=(
            P("dp", "mp", "section"),
            P("dp", "mp", "section"),
            qkv,
            matrix_out,
            matrix_in,
            matrix_out,
            P(),
            P(),
            P(),
            P(),
            qkv,
            matrix_out,
            matrix_in,
            matrix_out,
            P(),
            P(),
        ),
        check_vma=False,
    )
```

```python
import functools
import math

import jax
import jax.numpy as jnp
import numpy as np
from jax import lax
from jax.experimental import pallas as pl
from jax.experimental.pallas import tpu as pltpu
from jax.sharding import PartitionSpec as P

HD_ENC = 64
HD_DEC = 32
COLS_SMALL = 32
COLS_BIG = 64
PATCHES = 2048
SMALL_PATCHES = 512
VIS = 512
VIS_SMALL = 128

MESH = pl.DeviceIdType.MESH
bf = jnp.bfloat16
f32 = jnp.float32
LOG2E = 1.4426950408889634
NEG = -1e30


def nn(a, b):
    return lax.dot_general(a, b, (((1,), (0,)), ((), ())), preferred_element_type=f32)


def nt(a, b):
    return lax.dot_general(a, b, (((1,), (1,)), ((), ())), preferred_element_type=f32)


def tn(a, b):
    return lax.dot_general(a, b, (((0,), (0,)), ((), ())), preferred_element_type=f32)


def norm_stats(stream):
    centre = stream - jnp.mean(stream, axis=-1, keepdims=True)
    inverse = lax.rsqrt(jnp.mean(centre * centre, axis=-1, keepdims=True) + 1e-06)
    return centre * inverse, inverse


def normalize(stream, gain, shift):
    scaled, _ = norm_stats(stream)
    return scaled * gain + shift


def normalize_back(stream, gain, grad_out):
    scaled, inverse = norm_stats(stream)
    f = grad_out * gain
    grad_in = inverse * (
        f
        - jnp.mean(f, axis=-1, keepdims=True)
        - scaled * jnp.mean(f * scaled, axis=-1, keepdims=True)
    )
    return (
        grad_in,
        jnp.sum(grad_out * scaled, axis=0, keepdims=True),
        jnp.sum(grad_out, axis=0, keepdims=True),
    )


def gelu_and_slope(a):
    x = jnp.abs(a) * 0.7071067811865476
    t = 1.0 / (1.0 + 0.3275911 * x)
    e = jnp.exp2(x * x * (-LOG2E))
    poly = ((((1.061405429 * t - 1.453152027) * t + 1.421413741) * t - 0.284496736) * t + 0.254829592) * t
    tail = 0.5 * poly * e
    phi = jnp.where(a >= 0, 1.0 - tail, tail)
    return a * phi, phi + a * e * 0.3989422804014327


class Ctx:
    def __init__(self, ss, rs, dp):
        self.ss, self.rs, self.n, self.dp = ss, rs, 0, dp
        self.s = lax.axis_index("section")
        self.d = lax.axis_index("dp")
        self.m = lax.axis_index("mp")
        m = self.m
        self.lo = lax.rem(m, 2)
        self.hi = m // 2
        self.m1 = m + 1 - 2 * self.lo
        self.m2 = lax.rem(m + 2, 4)
        self.m3 = lax.rem(self.m1 + 2, 4)
        self.core = {"mp": self.m1}
        self.y = {"mp": self.m2}
        self.x = {"section": 1 - self.s}
        self.pending = []

    def z(self, k):
        return {"dp": lax.rem(self.d + k, self.dp)}

    def barrier(self, peers):
        b = pltpu.get_barrier_semaphore()
        for p in peers:
            pl.semaphore_signal(b, inc=1, device_id=p, device_id_type=MESH)
        pl.semaphore_wait(b, len(peers))

    def send(self, src, dst, dev):
        i = self.n
        self.n += 1
        c = pltpu.make_async_remote_copy(
            src_ref=src,
            dst_ref=dst,
            send_sem=self.ss.at[i],
            recv_sem=self.rs.at[i],
            device_id=dev,
            device_id_type=MESH,
        )
        c.start()
        self.pending.append(c)
        return c

    def sent(self, c):
        c.wait_send()
        self.pending = [p for p in self.pending if p is not c]

    def drain(self):
        for c in self.pending:
            c.wait_send()
        self.pending = []


class GatherMp:
    def __init__(self, cx, buf):
        self.cx, self.buf = cx, buf
        m = cx.m
        self.c2 = cx.send(buf.at[m], buf.at[m], cx.y)
        self.c1 = cx.send(buf.at[m], buf.at[m], cx.core)

    def forward(self):
        cx, buf = self.cx, self.buf
        self.c2.wait_recv()
        self.c3 = cx.send(buf.at[cx.m2], buf.at[cx.m2], cx.core)

    def near(self):
        self.c1.wait_recv()

    def far(self):
        self.c3.wait_recv()

    def finish(self):
        self.forward()
        self.near()
        self.far()


class ReduceMp:
    def __init__(self, cx, part, stage, recv):
        self.cx, self.part, self.stage, self.recv = cx, part, stage, recv
        stage[0] = part[cx.m3].astype(bf)
        self.c3 = cx.send(stage.at[0], recv.at[0], cx.core)
        stage[1] = part[cx.m1].astype(bf)
        self.c1 = cx.send(stage.at[1], recv.at[1], cx.core)

    def middle(self):
        cx = self.cx
        self.c3.wait_recv()
        self.stage[2] = (self.part[cx.m2] + self.recv[0].astype(f32)).astype(bf)
        self.c2 = cx.send(self.stage.at[2], self.recv.at[2], cx.y)

    def finish(self):
        self.c1.wait_recv()
        own = self.part[self.cx.m] + self.recv[1].astype(f32)
        self.c2.wait_recv()
        return own + self.recv[2].astype(f32)


def reduce_mp(cx, part, stage, recv):
    r = ReduceMp(cx, part, stage, recv)
    r.middle()
    return r.finish()


class GatherW:
    def __init__(self, cx, shard, whole):
        self.cx, self.whole, self.rows = cx, whole, shard.shape[0]
        own = self.at(cx.s, cx.d)
        self.zs = [cx.send(shard, own, cx.z(k)) for k in range(1, cx.dp)]
        self.xs = [cx.send(shard, own, cx.x)]
        own[...] = shard[...]

    def at(self, s, d):
        start = (s * self.cx.dp + d) * self.rows
        return self.whole.at[pl.ds(pl.multiple_of(start, 16), self.rows)]

    def forward(self):
        cx = self.cx
        for k in range(1, cx.dp):
            self.zs[k - 1].wait_recv()
            block = self.at(cx.s, lax.rem(cx.d + cx.dp - k, cx.dp))
            self.xs.append(cx.send(block, block, cx.x))

    def finish(self):
        for c in self.xs:
            c.wait_recv()


class RelayW:
    def __init__(self, cx, shard, whole):
        self.cx, self.whole, self.rows = cx, whole, shard.shape[0]
        dp, d = cx.dp, cx.d
        self.base = cx.n
        cx.n += 4 * dp
        self.own = self.at(cx.s, d)

        @pl.when(d < dp - 1)
        def _():
            self.make(shard, self.own, 1, {"dp": d + 1}).start()

        @pl.when(d > 0)
        def _():
            self.make(shard, self.own, dp + 1, {"dp": d - 1}).start()

        self.make(shard, self.own, 2 * dp, cx.x).start()
        self.own[...] = shard[...]

    def at(self, s, d):
        start = (s * self.cx.dp + d) * self.rows
        return self.whole.at[pl.ds(pl.multiple_of(start, 16), self.rows)]

    def make(self, src, dst, i, dev):
        cx, i = self.cx, self.base + i
        return pltpu.make_async_remote_copy(
            src_ref=src,
            dst_ref=dst,
            send_sem=cx.ss.at[i],
            recv_sem=cx.rs.at[i],
            device_id=dev,
            device_id_type=MESH,
        )

    def hop(self, k):
        cx, dp, d = self.cx, self.cx.dp, self.cx.d

        @pl.when(d >= k)
        def _():
            b = self.at(cx.s, jnp.maximum(d - k, 0))
            self.make(b, b, k, cx.x).wait_recv()

            @pl.when(d < dp - 1)
            def _():
                self.make(b, b, k + 1, {"dp": d + 1}).start()

            self.make(b, b, 2 * dp + k, cx.x).start()

        @pl.when(d + k < dp)
        def _():
            b = self.at(cx.s, jnp.minimum(d + k, dp - 1))
            self.make(b, b, dp + k, cx.x).wait_recv()

            @pl.when(d > 0)
            def _():
                self.make(b, b, dp + k + 1, {"dp": d - 1}).start()

            self.make(b, b, 3 * dp + k, cx.x).start()

    def finish(self):
        cx, dp, d = self.cx, self.cx.dp, self.cx.d
        other = lambda e: self.at(1 - cx.s, jnp.clip(e, 0, dp - 1))
        self.make(self.own, other(d), 2 * dp, cx.x).wait_recv()
        for k in range(1, dp):

            @pl.when(d >= k)
            def _():
                self.make(self.own, other(d - k), 2 * dp + k, cx.x).wait_recv()

            @pl.when(d + k < dp)
            def _():
                self.make(self.own, other(d + k), 3 * dp + k, cx.x).wait_recv()

    def drain(self):
        cx, dp, d = self.cx, self.cx.dp, self.cx.d
        own = self.own
        self.make(own, own, 2 * dp, cx.x).wait_send()
        for k in range(1, dp):

            @pl.when(d >= k)
            def _():
                self.make(own, own, 2 * dp + k, cx.x).wait_send()

            @pl.when(d + k < dp)
            def _():
                self.make(own, own, 3 * dp + k, cx.x).wait_send()

            @pl.when((d < dp - 1) & (d >= k - 1))
            def _():
                self.make(own, own, k, cx.x).wait_send()

            @pl.when((d > 0) & (d + k - 1 < dp))
            def _():
                self.make(own, own, dp + k, cx.x).wait_send()


class Local:
    def __init__(self, sems):
        self.sems, self.n, self.pending = sems, 0, []

    def start(self, src, dst):
        c = pltpu.make_async_copy(src, dst, self.sems.at[self.n])
        self.n += 1
        c.start()
        self.pending.append(c)
        return c

    def drain(self):
        for c in self.pending:
            c.wait()


class ScatterW:
    def __init__(self, cx, rows, own, xs, xr, zs, zr):
        self.cx, self.rows, self.own = cx, rows, own
        self.xs, self.xr, self.zs, self.zr = xs, xr, zs, zr

    def start(self, theirs):
        self.xs[...] = theirs.astype(bf)
        self.c = self.cx.send(self.xs, self.xr, self.cx.x)

    def at(self, e):
        return pl.ds(pl.multiple_of(e * self.rows, 16), self.rows)

    def near(self):
        cx = self.cx
        self.c.wait_recv()
        low = lax.rem(cx.d, 2)
        for j in range(2):
            at = self.at(2 * j + 1 - low)
            self.zs[j] = (self.own[at, :] + self.xr[at, :].astype(f32)).astype(bf)
        self.c = cx.send(self.zs.at[pl.ds(0, 2)], self.zr.at[pl.ds(0, 2)], {"dp": cx.d + 1 - 2 * low})

    def far(self):
        cx = self.cx
        low, high = lax.rem(cx.d, 2), cx.d // 2
        self.c.wait_recv()
        at = self.at(2 * (1 - high) + low)
        total = self.own[at, :] + self.xr[at, :].astype(f32) + self.zr[1 - high].astype(f32)
        self.zs[2] = total.astype(bf)
        self.c = cx.send(self.zs.at[2], self.zr.at[2], cx.z(2))

    def finish(self):
        at = self.at(self.cx.d)
        own = self.own[at, :] + self.xr[at, :].astype(f32) + self.zr[self.cx.d // 2].astype(f32)
        self.c.wait_recv()
        return own + self.zr[2].astype(f32)


def scatter_scratch(dp, rows, cols):
    half = dp * rows
    return [
        pltpu.VMEM((half, cols), bf),
        pltpu.VMEM((half, cols), bf),
        pltpu.VMEM((3, rows, cols), bf),
        pltpu.VMEM((3, rows, cols), bf),
    ]


def iota(shape, dim):
    return lax.broadcasted_iota(jnp.int32, shape, dim)


def enc_forward_kernel(dp, gather, *refs):
    it = iter(refs)
    take = lambda n: [next(it) for _ in range(n)]
    res, x_all, gains, shifts, proj = take(5)
    if gather:
        eqkv, eout, eup, edown, dqkv, dout = take(6)
        ha, hb, hc = take(3)
    else:
        wa, wb, wc, wd_in = take(4)
    wd, h1, h2, hq, hctx, hslope, hact, hmid, top_out, low_all = take(10)
    ss, rs, ls, part, stage, recv, n1, n2, qkv, ctx, slope, active, mid_s = take(13)
    if gather:
        wa, wb, wc, sa, sd, sdf = take(6)
    cx = Ctx(ss, rs, dp)
    lc = Local(ls)
    peers = [cx.core, cx.y]
    if gather:
        peers += [cx.x] + [cx.z(k) for k in range(1, dp)]
        wide = eqkv.shape[2]
        for t in range(3):
            sa[:, t * wide : (t + 1) * wide] = eqkv[t]
        sa[:, 3 * wide :] = eout[...].astype(f32).T.astype(bf)
        wide = dqkv.shape[2]
        for t in range(3):
            sd[:, t * wide : (t + 1) * wide] = dqkv[t]
        sd[:, 3 * wide : 4 * wide] = dout[...]
        both = 4 * wide
    cx.barrier(peers)
    if gather:
        cut = sa.shape[1] // 2
        ga = RelayW(cx, sa.at[:, pl.ds(0, cut)], wa.at[:, pl.ds(0, cut)])
        ga2 = RelayW(cx, sa.at[:, pl.ds(cut, cut)], wa.at[:, pl.ds(cut, cut)])
    stream = x_all[cx.s].astype(f32)
    n1[cx.m] = normalize(stream, gains[0:1, :], shifts[0:1, :]).astype(bf)
    g1 = GatherMp(cx, n1)
    if gather:
        csd = cx.send(sd.at[:, pl.ds(0, both)], sdf, cx.y)
        ga.hop(1)
        ga2.hop(1)
        ga.hop(2)
        ga2.hop(2)
        gb = RelayW(cx, eup, wb)
    g1.finish()
    lc.start(n1, h1)
    if gather:
        ga.hop(3)
        ga2.hop(3)
        gc = RelayW(cx, edown, wc)
        gb.hop(1)
        ga.finish()
        ga2.finish()
        lc.start(wa, ha)
    rows = n1.shape[1]
    total = 4 * rows
    width = n1.shape[2]
    n1_all = n1[...].reshape(total, width)
    qkv[...] = nn(n1_all, wa[...]).astype(bf)
    lc.start(qkv, hq)
    if gather:
        gb.hop(2)
        gc.hop(1)
        csd.wait_recv()
        sd[:, both:] = sdf[...]
        gd = RelayW(cx, sd, wd)
    shown = jnp.where(res[cx.s] == 1, VIS, VIS_SMALL)
    bias = jnp.where(iota((1, total), 1) < shown, 0.0, NEG)
    scale2 = HD_ENC**-0.5 * LOG2E
    heads = (width // 4) // HD_ENC
    pieces = [jnp.zeros((total, HD_ENC), bf)]
    for h in range(heads):
        q = qkv[:, h * HD_ENC : (h + 1) * HD_ENC]
        k = qkv[:, (heads + h) * HD_ENC : (heads + h + 1) * HD_ENC]
        v = qkv[:, (2 * heads + h) * HD_ENC : (2 * heads + h + 1) * HD_ENC]
        sc = nt(q, k) + bias
        top = jnp.max(sc, axis=1, keepdims=True)
        e = jnp.exp2((sc - top) * scale2)
        tot = jnp.sum(e, axis=1, keepdims=True)
        pieces.append((nn(e.astype(bf), v) / tot).astype(bf))
        if gather and h == 0:
            gb.hop(3)
        if gather and h == 1:
            gc.hop(2)
    ctx[...] = jnp.concatenate(pieces, axis=1)
    lc.start(ctx, hctx)
    cpad = ctx.shape[1]
    part[...] = nt(ctx[...], wa[:, width - cpad :]).reshape(part.shape)
    r1 = ReduceMp(cx, part, stage.at[0], recv.at[0])
    if gather:
        gd.hop(1)
    r1.middle()
    if gather:
        gc.hop(3)
    mid = stream + r1.finish()
    mid_s[...] = mid
    lc.start(mid_s, hmid)
    n2[cx.m] = normalize(mid, gains[1:2, :], shifts[1:2, :]).astype(bf)
    g2 = GatherMp(cx, n2)
    if gather:
        gd.hop(2)
        gb.finish()
        lc.start(wb, hb)
    g2.finish()
    lc.start(n2, h2)
    hid = nn(n2[...].reshape(total, width), wb[...])
    act, slo = gelu_and_slope(hid)
    active[...] = act.astype(bf)
    slope[...] = slo.astype(bf)
    lc.start(active, hact)
    lc.start(slope, hslope)
    if gather:
        gc.finish()
        lc.start(wc, hc)
    part[...] = nt(active[...], wc[...]).reshape(part.shape)
    r2 = ReduceMp(cx, part, stage.at[1], recv.at[1])
    r2.middle()
    if gather:
        gd.hop(3)
    top = (mid_s[...] + r2.finish()).astype(bf)
    top_out[...] = top
    low_all[cx.m] = nn(top, proj[...]).astype(bf)
    g3 = GatherMp(cx, low_all)
    if gather:
        gd.finish()
    else:
        both = wd_in.shape[1]
        wd[:, :both] = wd_in[...]
        cd = cx.send(wd_in, wd.at[:, pl.ds(both, both)], cx.y)
        cd.wait_recv()
    g3.finish()
    cx.drain()
    if gather:
        for g in (ga, ga2, gb, gc, gd):
            g.drain()
    lc.drain()


def vm(n):
    return [pl.BlockSpec(memory_space=pltpu.VMEM)] * n


def anywhere(n):
    return [pl.BlockSpec(memory_space=pl.ANY)] * n


SMEM = pl.BlockSpec(memory_space=pltpu.SMEM)


def sds(shape, dtype):
    return jax.ShapeDtypeStruct(shape, dtype)


def params(cid):
    return pltpu.CompilerParams(collective_id=cid, has_side_effects=True, vmem_limit_bytes=60 << 20)


def enc_forward(dp, gather, res, x, gains, shifts, proj, shards, de, dd, wide, dwide):
    rows, width = x.shape[1:]
    total = 4 * rows
    slots = (4, rows, width)
    V = pltpu.VMEM
    outs = []
    if gather:
        outs += [sds((de, de), bf), sds((de, wide), bf), sds((de, wide), bf)]
    outs += [sds((dd, 2 * dwide), bf)]
    big = [sds(slots, bf), sds(slots, bf), sds((total, width), bf), sds((total, 256), bf)]
    big += [sds((total, wide), bf), sds((total, wide), bf), sds((rows, width), f32)]
    outs += big + [sds((rows, width), bf), sds((4, rows, dd), bf)]
    scratch = [
        pltpu.SemaphoreType.DMA((112,)),
        pltpu.SemaphoreType.DMA((112,)),
        pltpu.SemaphoreType.DMA((16,)),
        V(slots, f32),
        V((2, 3, rows, width), bf),
        V((2, 3, rows, width), bf),
    ] + [V(b.shape, b.dtype) for b in big]
    if gather:
        scratch += [V(o.shape, bf) for o in outs[:3]]
        scratch += [V((shards[2].shape[0], de), bf), V((shards[5].shape[0], 2 * dwide), bf)]
        scratch += [V((shards[5].shape[0], dwide), bf)]
    got = pl.pallas_call(
        functools.partial(enc_forward_kernel, dp, gather),
        out_shape=outs,
        in_specs=[SMEM] + vm(4 + len(shards)),
        out_specs=anywhere(3 if gather else 0) + vm(1) + anywhere(7) + vm(2),
        scratch_shapes=scratch,
        compiler_params=params(1),
        name="enc_forward",
    )(res, x, gains, shifts, proj, *shards)
    if not gather:
        got = list(shards[:3]) + list(got)
    return got[:4], got[4:]


def dec_kernel(dp, gather, *refs):
    it = iter(refs)
    take = lambda n: [next(it) for _ in range(n)]
    res, chosen, low_all, table, cot, gains, shifts, token, wd_both, e_in, f_in = take(11)
    out, glow, gd, out_e, out_f, small, kept = take(7)
    ss, rs, we_both, wf_both, own_e, own_f, yst, yrc = take(8)
    if gather:
        se, sf, sfar = take(3)
        scat = (take(4), take(4))
    unit = wd_both.shape[1] // 2
    wd, we, wf = [[w.at[:, pl.ds(unit * g, unit)] for g in range(2)] for w in (wd_both, we_both, wf_both)]
    (n1, n2, gm, gmid_low, qg, kg, vg, gg, vtx, kt, dqt, lse, acc_s, top_s, ctx, active, slope) = take(17)
    ct = dqt
    (dkv, mid_s, start_s, res_s, part, fstage, frecv, far, prod, pstage, precv, masks) = take(12)
    sc_s, mx_s = take(2), take(2)
    p_s, tops, ps = take(3)
    cx = Ctx(ss, rs, dp)
    cx.barrier([cx.core, cx.y, cx.x] + ([cx.z(k) for k in range(1, dp)] if gather else []))
    rows, width = n1.shape[1:]
    m, lo, hi, s = cx.m, cx.lo, cx.hi, cx.s
    big = res[s] == 1
    shown = jnp.where(big, VIS, VIS_SMALL)
    filled = jnp.where(big, PATCHES, SMALL_PATCHES)
    pos_col = iota((rows, 1), 0) + m * rows
    live = jnp.where(pos_col < filled, 1.0, 0.0)
    ccot = pltpu.make_async_copy(cot.at[s], gm.at[lo], ps.at[0])
    ccot.start()
    ccot.wait()
    gm[lo] = (gm[lo].astype(f32) * live).astype(bf)
    cgm = cx.send(gm.at[lo], gm.at[lo], cx.core)
    if gather:
        cef = [cx.send(e_in, sfar.at[0], cx.y), cx.send(f_in, sfar.at[1], cx.y)]
        se[:, :unit] = e_in[...]
        sf[:, :unit] = f_in[...]
    else:
        we[0][...] = e_in[...]
        wf[0][...] = f_in[...]
        cef = [cx.send(e_in, we[1], cx.y), cx.send(f_in, wf[1], cx.y)]
    vis = chosen.shape[-1]

    def place_rows():
        return jnp.where((pos_col == chosen[pl.ds(s, 1), :]) & (iota((1, vis), 1) < shown), 1.0, 0.0)

    place = place_rows()
    seen = jnp.sum(place, axis=1, keepdims=True)
    weight = live - seen
    placed = nn(place.astype(bf), low_all[...].reshape(vis, width))
    half = width // 2
    nb, ns = rows // COLS_BIG, rows // COLS_SMALL
    rb = table[pl.ds(pl.multiple_of(m * nb, 8), nb), :]
    rsm = table[pl.ds(pl.multiple_of(m * ns, 8), ns), :]
    big_rows = jnp.broadcast_to(rb[:, None, :], (nb, COLS_BIG, half)).reshape(rows, half)
    small_rows = jnp.broadcast_to(rsm[:, None, :], (ns, COLS_SMALL, half)).reshape(rows, half)
    big_cols = jnp.broadcast_to(table[0:COLS_BIG, :][None], (nb, COLS_BIG, half)).reshape(rows, half)
    small_cols = jnp.broadcast_to(table[0:COLS_SMALL, :][None], (ns, COLS_SMALL, half)).reshape(rows, half)
    base = placed + weight * token[...]
    start_s[:, :half] = base[:, :half] + live * jnp.where(big, big_rows, small_rows)
    start_s[:, half:] = base[:, half:] + live * jnp.where(big, big_cols, small_cols)
    n1[m] = normalize(start_s[...], gains[0:1, :], shifts[0:1, :]).astype(bf)
    g1 = GatherMp(cx, n1)

    lane = iota((1, 256), 1)
    for j in range(4):
        head_lane = (lane < 128) & (lane // 32 == j)
        off = lane - (128 + 8 * j)
        masks[0, j] = jnp.where(head_lane | ((off >= 0) & (off < 3)) | (lane == 160), 1.0, 0.0).astype(bf)
        masks[1, j] = jnp.where(head_lane | ((off >= 0) & (off < 2)), 1.0, 0.0).astype(bf)
    aug = iota((1, 128), 1)
    total = 4 * rows
    key_bias = jnp.where(iota((total, 1), 0) < filled, 0.0, NEG)
    kaug = jnp.where(aug == 32, key_bias, jnp.where(aug < 32, 1.0, 0.0)).astype(bf)
    vaug = jnp.broadcast_to(jnp.where(aug < 32, 1.0, 0.0), (total, 128)).astype(bf)
    qaug = jnp.broadcast_to(jnp.where(aug == 32, 1.0, 0.0), (2 * rows, 128)).astype(bf)
    for g in range(2):
        kg[g, :, 128:] = kaug
        vg[g, :, 128:] = vaug
        qg[g, :, 128:] = qaug
    vtx[:, 32:, :] = jnp.ones((8, 16, total), bf)

    def keys_values(i, groups):
        at = pl.ds(pl.multiple_of(i * rows, 128), rows)
        for g in groups:
            kv = nn(n1[i], wd[g][:, 128:384])
            kg[g, at, :128] = kv[:, :128].astype(bf)
            vg[g, at, :128] = kv[:, 128:].astype(bf)
            kvt = kv.T.astype(bf)
            for j in range(4):
                kt[4 * g + j, :, at] = kvt[32 * j : 32 * j + 32]
                vtx[4 * g + j, 0:32, at] = kvt[128 + 32 * j : 160 + 32 * j]

    g1.near()

    def near_rows_in(g):
        for r in range(2):
            qg[g, r * rows : (r + 1) * rows, :128] = nn(n1[2 * hi + r], wd[g][:, :128]).astype(bf)
        keys_values(cx.m, (g,))
        keys_values(cx.m1, (g,))

    if gather:
        gats = []
        for i, (sh, w) in enumerate(((se, we_both), (sf, wf_both))):
            cef[i].wait_recv()
            sh[:, unit:] = sfar[i]
            gats.append(GatherW(cx, sh, w))
    near_rows_in(0)
    near_rows_in(1)
    c2 = HD_DEC**-0.5 * LOG2E

    def score(h, i, to):
        g, j = h // 4, lax.rem(h, 4)
        at = pl.ds(pl.multiple_of(i * rows, 128), rows)
        sc = nt(kg[g, at, :] * masks[0, j], qg[g])
        sc_s[to][...] = sc
        mx_s[to][...] = jnp.max(sc, axis=0, keepdims=True)

    def slot(n, h):
        return 2 * lax.rem(h, 2) + n

    def keep(n, h, i):
        return pltpu.make_async_copy(p_s.at[slot(n, h)], kept.at[h, i], ps.at[slot(n, h)])

    def fetch(n, h, i):
        return pltpu.make_async_copy(kept.at[h, i], p_s.at[slot(n, h)], ps.at[slot(n, h)])

    def head_pass(first, last, blocks, heads):
        def body(h, _):
            g, j = h // 4, lax.rem(h, 4)
            if first:
                top, acc = None, None
            else:
                top, acc = top_s[pl.ds(h, 1), :], acc_s[h]
            ahead = ((h, blocks[1]), (jnp.minimum(h + 1, 7), blocks[0]))
            for n, i in enumerate(blocks):
                at = pl.ds(pl.multiple_of(i * rows, 128), rows)
                if first and heads[0] == 0:

                    @pl.when(h > 1)
                    def _():
                        keep(n, h, i).wait()

                else:
                    keep(n, h, i).wait()
                mj = mx_s[n][...]
                new = mj if top is None else jnp.maximum(top, mj)
                tops[pl.ds(4 * h + i, 1), :] = new
                score(*ahead[n], 1 - n)
                p = jnp.exp2((sc_s[n][...] - new) * c2).astype(bf)
                p_s[slot(n, h)] = p
                o = nn(vtx[h, :, at], p)
                keep(n, h, i).start()
                acc = o if acc is None else acc * jnp.exp2((top - new) * c2) + o
                top = new
            if last:
                tot = acc[32:33, :]
                ct[h] = acc[:32, :] / tot
                at = pl.ds(pl.multiple_of(8 * j, 8), 8)
                lse[g, at, :] = jnp.broadcast_to(top + jnp.log(tot) * (LOG2E / c2), (8, top.shape[1]))
            else:
                top_s[pl.ds(h, 1), :] = top
                acc_s[h] = acc
            return 0

        lax.fori_loop(*heads, body, 0)

    score(jnp.int32(0), cx.m, 0)
    head_pass(True, False, (cx.m, cx.m1), (0, 6))
    g1.forward()
    if gather:
        gats[0].forward()
    head_pass(True, False, (cx.m, cx.m1), (6, 8))
    keys_values(cx.m2, (0, 1))
    g1.far()
    keys_values(cx.m3, (0, 1))
    score(jnp.int32(0), cx.m2, 0)
    head_pass(False, True, (cx.m2, cx.m3), (0, 4))
    if gather:
        gats[1].forward()
    head_pass(False, True, (cx.m2, cx.m3), (4, 8))
    for n, i in enumerate((cx.m2, cx.m3)):
        for h in (0, 1):
            keep(n, 6 + h, i).wait()
            fetch(n, h, i).start()
    for g in range(2):
        ctx[:, 128 * g : 128 * g + 128] = ct[4 * g : 4 * g + 4].reshape(128, 2 * rows).T.astype(bf)

    def chip_rows(r):
        return pl.ds(pl.multiple_of(r * rows, 128), rows)

    def out_rows(r):
        return sum(nt(ctx[chip_rows(r), 128 * g : 128 * g + 128], wd[g][:, 384:]) for g in range(2))

    fstage[0] = out_rows(1 - lo).astype(bf)
    co = cx.send(fstage.at[0], frecv.at[0], cx.core)
    mid = start_s[...] + out_rows(lo)
    co.wait_recv()
    mid = mid + frecv[0].astype(f32)
    mid_s[...] = mid
    n2[lo] = normalize(mid, gains[1:2, :], shifts[1:2, :]).astype(bf)
    cn2 = cx.send(n2.at[lo], n2.at[lo], cx.core)

    def mlp_rows(r):
        at = chip_rows(r)
        x = n2[r]
        y = None
        for g in range(2):
            a, b = gelu_and_slope(nn(x, we[g][...]))
            cols = slice(width * g, width * (g + 1))
            a = a.astype(bf)
            active[at, cols] = a
            slope[at, cols] = b.astype(bf)
            t = nt(a, wf[g][...])
            y = t if y is None else y + t
        return y

    if gather:
        for q in gats:
            q.finish()
    else:
        for c in cef:
            c.wait_recv()
    res_s[...] = mlp_rows(lo)
    cn2.wait_recv()
    fstage[1] = mlp_rows(1 - lo).astype(bf)
    c = cx.send(fstage.at[1], frecv.at[1], cx.core)

    cgm.wait_recv()

    def mlp_back_rows(r):
        at = chip_rows(r)
        y = None
        for g in range(2):
            cols = slice(width * g, width * (g + 1))
            ga = nn(gm[r], wf[g][...])
            gh = (ga * slope[at, cols].astype(f32)).astype(bf)
            slope[at, cols] = gh
            t = nt(gh, we[g][...])
            y = t if y is None else y + t
        return y

    fstage[2] = mlp_back_rows(1 - lo).astype(bf)
    cb = cx.send(fstage.at[2], frecv.at[2], cx.core)
    c.wait_recv()
    result = mid_s[...] + res_s[...] + frecv[1].astype(f32)
    result = result * live
    left, right = result[:, :half], result[:, half:]
    out[s] = jnp.where(s == 0, left, right).astype(bf)
    prod[...] = jnp.where(s == 0, right, left).astype(bf)
    cprod = cx.send(prod, out.at[s], cx.x)
    own = mlp_back_rows(lo)
    half_rows = width // 2

    def start_scatter(left, right, own, i, out):
        def rows_of(sec):
            at = pl.ds(pl.multiple_of(sec * half_rows, 128), half_rows)
            return tn(left[:, :, at].reshape(2 * rows, half_rows), right[...])

        if gather:
            q = ScatterW(cx, half_rows // dp, own, *scat[i])
            q.start(rows_of(1 - s))
            own[...] = rows_of(s)
            return q
        for sec in (0, 1):
            t = rows_of(jnp.int32(sec))
            at = slice(sec * half_rows, (sec + 1) * half_rows)
            out[at] = t[:, :unit]
            yst[i, at] = t[:, unit:].astype(bf)
        return cx.send(yst.at[i], yrc.at[i], cx.y)

    q_f = start_scatter(gm, active, own_f, 0, out_f)
    cb.wait_recv()
    grad_mid, gain_mid, shift_mid = normalize_back(mid_s[...], gains[1:2, :], own + frecv[2].astype(f32))
    gmid = gm[lo].astype(f32) + grad_mid
    mid_s[...] = gmid
    gmid_low[lo] = gmid.astype(bf)
    cgmid = cx.send(gmid_low.at[lo], gmid_low.at[lo], cx.core)
    q_e = start_scatter(n2, slope, own_e, 1, out_e)
    cgmid.wait_recv()
    gmid_all = gmid_low[...].reshape(2 * rows, width)
    sel = jnp.where(iota((128, 128), 0) // 32 == iota((128, 128), 1) // 8, 1.0, 0.0).astype(bf)
    lane128 = iota((1, 128), 1)
    t8 = lax.rem(lane128, 8)
    for g in range(2):
        gcg = nn(gmid_all, wd[g][:, 384:]).astype(bf)
        gg[g, :, :128] = gcg
        prodd = gcg.astype(f32) * ctx[:, 128 * g : 128 * g + 128].astype(f32)
        ph = prodd.astype(bf)
        plow = (prodd - ph.astype(f32)).astype(bf)
        delta = nn(ph, sel) + nn(plow, sel)
        dh = delta.astype(bf).astype(f32)
        daug = jnp.where(t8 == 0, -dh, jnp.where(t8 == 1, dh - delta, 0.0))
        gg[g, :, 128:] = jnp.where(lane128 < 32, daug, 0.0).astype(bf)
        gd[:, unit * g + 384 : unit * g + 512] = tn(gmid_all, ctx[:, 128 * g : 128 * g + 128])

    scale = HD_DEC**-0.5
    dqt[...] = jnp.zeros_like(dqt)
    head_lane = lane128 // 32

    def back_pass(blocks, heads, after):
        def body(h, _):
            g, j = h // 4, lax.rem(h, 4)
            mine = head_lane == j
            total_row = lse[g, pl.ds(pl.multiple_of(8 * j, 8), 8), :][0:1]
            for n, i in enumerate(blocks):
                at = pl.ds(pl.multiple_of(i * rows, 128), rows)
                fetch(n, h, i).wait()
                dpt = nt(vg[g, at, :] * masks[1, j], gg[g])
                share = jnp.exp2((tops[pl.ds(4 * h + i, 1), :] - total_row) * c2)
                p = p_s[slot(n, h)].astype(f32) * share
                ds = (p * dpt).astype(bf)
                dv = nn(p.astype(bf), gg[g, :, :128])
                dk = nn(ds, qg[g, :, :128]) * scale
                dkv[g, at, :128] = jnp.where(mine, dk, dkv[g, at, :128].astype(f32)).astype(bf)
                dkv[g, at, 128:] = jnp.where(mine, dv, dkv[g, at, 128:].astype(f32)).astype(bf)
                dqt[h] += nn(kt[h, :, at], ds)

                @pl.when(h < 6)
                def _():
                    fetch(n, h + 2, i).start()

                if after:

                    @pl.when(h >= 6)
                    def _():
                        fetch(n, h - 6, after[n]).start()

            return 0

        lax.fori_loop(*heads, body, 0)

    dkv[...] = jnp.zeros_like(dkv)
    back_pass((cx.m2, cx.m3), (0, 6), (cx.m, cx.m1))
    if gather:
        q_f.near()
    back_pass((cx.m2, cx.m3), (6, 8), (cx.m, cx.m1))

    def far_rows(r):
        at = pl.ds(pl.multiple_of((2 * (1 - hi) + r) * rows, 128), rows)
        return sum(nt(dkv[g, at, :], wd[g][:, 128:384]) for g in range(2))

    cx.sent(co)
    fstage[0] = far_rows(1 - lo).astype(bf)
    cf = cx.send(fstage.at[0], frecv.at[0], cx.core)
    res_s[...] = far_rows(lo)
    back_pass((cx.m, cx.m1), (0, 2), None)
    cf.wait_recv()
    cx.sent(cb)
    fstage[2] = (res_s[...] + frecv[0].astype(f32)).astype(bf)
    cfar = cx.send(fstage.at[2], far, cx.y)
    if gather:
        q_f.far()
        q_e.near()
    back_pass((cx.m, cx.m1), (2, 6), None)
    if gather:
        q_e.far()
        t = q_f.finish()
        out_f[...] = t[:, :unit]
        yst[0] = t[:, unit:].astype(bf)
        cyf = cx.send(yst.at[0], yrc.at[0], cx.y)
    back_pass((cx.m, cx.m1), (6, 8), None)
    for g in range(2):
        ctx[:, 128 * g : 128 * g + 128] = (dqt[4 * g : 4 * g + 4].reshape(128, 2 * rows).T * scale).astype(bf)

    def near_rows(r):
        at = pl.ds(pl.multiple_of((2 * hi + r) * rows, 128), rows)
        return sum(
            nt(ctx[chip_rows(r), 128 * g : 128 * g + 128], wd[g][:, :128]) + nt(dkv[g, at, :], wd[g][:, 128:384])
            for g in range(2)
        )

    cx.sent(c)
    fstage[1] = near_rows(1 - lo).astype(bf)
    cn = cx.send(fstage.at[1], frecv.at[1], cx.core)
    near = near_rows(lo)
    n1_chip = n1[pl.ds(2 * hi, 2)].reshape(2 * rows, width)
    t = tn(n1_chip, ctx[...])
    gd[:, :128] = t[:, :128]
    gd[:, unit : unit + 128] = t[:, 128:]
    cn.wait_recv()
    if gather:
        t = q_e.finish()
        out_e[...] = t[:, :unit]
        yst[1] = t[:, unit:].astype(bf)
        cye = cx.send(yst.at[1], yrc.at[1], cx.y)
    near = near + frecv[1].astype(f32)
    cfar.wait_recv()
    grad_in, gain_in, shift_in = normalize_back(start_s[...], gains[0:1, :], near + far[...].astype(f32))
    gstart = (mid_s[...] + grad_in).astype(bf)
    token_term = jnp.sum(weight * gstart.astype(f32), axis=0, keepdims=True)
    small[0:1] = gain_in
    small[1:2] = gain_mid
    small[2:3] = shift_in
    small[3:4] = shift_mid
    small[4:5] = token_term
    small[5:8] = jnp.zeros((3, width), f32)
    part[...] = tn(place_rows().astype(bf), gstart).reshape(part.shape)
    reduce = ReduceMp(cx, part, pstage, precv)
    n1_all = n1[...].reshape(total, width)
    gd[:, 128:384] = tn(n1_all, dkv[0])
    reduce.middle()
    gd[:, unit + 128 : unit + 384] = tn(n1_all, dkv[1])
    for c, o, i in ((cyf, out_f, 0), (cye, out_e, 1)) if gather else ((q_f, out_f, 0), (q_e, out_e, 1)):
        c.wait_recv()
        o[...] = o[...] + yrc[i].astype(f32)
    glow[...] = reduce.finish().astype(bf)
    cprod.wait_recv()
    cx.drain()


def decoder(dp, gather, res, chosen, low_all, table, cot, gains, shifts, token, wd, e_in, f_in):
    rows, width = cot.shape[1:]
    vis = chosen.shape[-1]
    total, chip = 4 * rows, 2 * rows
    unit = wd.shape[1] // 2
    half = (width // 2, 2 * unit)
    outs = [
        sds((2, rows, width // 2), bf),
        sds((vis // 4, width), bf),
        sds(wd.shape, f32),
        sds(e_in.shape, f32),
        sds(f_in.shape, f32),
        sds((8, width), f32),
        sds((8, 4, rows, chip), bf),
    ]
    V = pltpu.VMEM
    extra = []
    if gather:
        pair = (e_in.shape[0], 2 * unit)
        extra = [V(pair, bf), V(pair, bf), V((2,) + e_in.shape, bf)] + 2 * scatter_scratch(dp, *pair)
    return pl.pallas_call(
        functools.partial(dec_kernel, dp, gather),
        out_shape=outs,
        in_specs=[SMEM] + vm(3) + anywhere(1) + vm(6),
        out_specs=vm(len(outs) - 1) + anywhere(1),
        scratch_shapes=[
            pltpu.SemaphoreType.DMA((64,)),
            pltpu.SemaphoreType.DMA((64,)),
            V(wd.shape, bf),
            V(wd.shape, bf),
            V(half, f32),
            V(half, f32),
            V((2,) + e_in.shape, bf),
            V((2,) + e_in.shape, bf),
        ]
        + extra
        + [
            V((4, rows, width), bf),
            V((2, rows, width), bf),
            V((2, rows, width), bf),
            V((2, rows, width), bf),
            V((2, chip, 256), bf),
            V((2, total, 256), bf),
            V((2, total, 256), bf),
            V((2, chip, 256), bf),
            V((8, 48, total), bf),
            V((8, 32, total), bf),
            V((8, 32, chip), f32),
            V((2, 32, chip), f32),
            V((8, 48, chip), f32),
            V((8, chip), f32),
            V((chip, 256), bf),
            V((chip, 2 * width), bf),
            V((chip, 2 * width), bf),
            V((2, total, 256), bf),
            V((rows, width), f32),
            V((rows, width), f32),
            V((rows, width), f32),
            V((4, vis // 4, width), f32),
            V((3, rows, width), bf),
            V((3, rows, width), bf),
            V((rows, width), bf),
            V((rows, width // 2), bf),
            V((3, vis // 4, width), bf),
            V((3, vis // 4, width), bf),
            V((2, 4, 1, 256), bf),
            V((rows, chip), f32),
            V((rows, chip), f32),
            V((1, chip), f32),
            V((1, chip), f32),
            V((4, rows, chip), bf),
            V((32, chip), f32),
            pltpu.SemaphoreType.DMA((4,)),
        ],
        compiler_params=params(2),
        name="decoder",
    )(res, chosen, low_all, table, cot, gains, shifts, token, wd, e_in, f_in)


def enc_backward_kernel(dp, gather, *refs):
    it = iter(refs)
    take = lambda n: [next(it) for _ in range(n)]
    res, x_all, gains, proj, mid, top, glow, gd, dsmall = take(9)
    hbm = take(9)
    gin, out_qkv, out_o, out_b, out_c, out_dqkv, out_do = take(7)
    eg, es, pout, mg, dg, dsh = take(6)
    ss, rs, ls = take(3)
    vmem = take(9)
    glows, gm, gmid_low, gqkv, part, stage, recv, gbuf, yst, yrc, gmid_half = take(11)
    if gather:
        scat = [take(4) for _ in range(5)]
        own_w = take(4)
        smr, smz, pst, prc, pzs, pzr, pacc, pwhole = take(8)
    lc = Local(ls)
    loads = [lc.start(h, v) for h, v in zip(hbm, vmem)]
    wc, slope, wb, active, n2, wa, ctx, qkv, n1 = vmem
    cx = Ctx(ss, rs, dp)
    peers = [cx.core, cx.y, cx.x]
    if gather:
        peers += [cx.z(k) for k in range(1, dp)]
    cx.barrier(peers)
    m, s = cx.m, cx.s
    rows, width = gm.shape[1:]
    total = 4 * rows
    half = width // 2
    glows[m] = glow[...]
    g1 = GatherMp(cx, glows)
    g_top = nt(glow[...], proj[...])
    unit_d = gd.shape[1] // 2
    if gather:
        hd = gd.shape[0] // 2
        qd = ScatterW(cx, hd // dp, gbuf, *scat[4])
        qd.start(gd[pl.ds(pl.multiple_of((1 - s) * hd, 16), hd), :])
        gbuf[...] = gd[pl.ds(pl.multiple_of(s * hd, 16), hd), :]
    else:
        yst[...] = gd[:, unit_d:].astype(bf)
        cyd = cx.send(yst, yrc, cx.y)
    p_part = tn(top[...], glow[...])
    if gather:
        pr = ProjSum(cx, pst, prc, pzs, pzr, pacc, pwhole, pout)
        pr.core(p_part)
    else:
        pout[...] = p_part

    def rows_of(sec, terms):
        at = pl.ds(pl.multiple_of(sec * half, 128), half)
        return sum(tn(left[:, :, at].reshape(total, half), right) for left, right in terms)

    def grad_theirs(i, terms):
        if not gather:
            return None
        q = ScatterW(cx, half // dp, own_w[i], *scat[i])
        q.start(rows_of(1 - s, terms))
        return q

    def grad_ours(i, terms, out):
        if gather:
            own_w[i][...] = rows_of(s, terms)
            return
        for sec in (0, 1):
            out[sec * half : (sec + 1) * half] = rows_of(jnp.int32(sec), terms)

    if gather:
        pr.y()
    g1.finish()
    gm_all = nt(glows[...].reshape(total, glow.shape[1]), proj[...]).astype(bf)
    gm[...] = gm_all.reshape(gm.shape)
    loads[0].wait()
    loads[1].wait()
    gh = (nn(gm_all, wc[...]) * slope[...].astype(f32)).astype(bf)
    if gather:
        pr.x()
    loads[2].wait()
    loads[3].wait()
    terms_c = [(gm, active[...])]
    qc = grad_theirs(2, terms_c)
    part[...] = nt(gh, wb[...]).reshape(part.shape)
    r1 = ReduceMp(cx, part, stage.at[0], recv.at[0])
    if gather:
        qd.near()
    r1.middle()
    if gather:
        pr.z()
    loads[4].wait()
    grad_ours(2, terms_c, out_c)
    g_n2 = r1.finish()
    grad_mid, gain_mid, shift_mid = normalize_back(mid[...], gains[1:2, :], g_n2)
    gmid = g_top + grad_mid
    gmid_half[...] = gmid
    gmid_low[m] = gmid.astype(bf)
    g2 = GatherMp(cx, gmid_low)
    if gather:
        pr.back_z()
        qd.far()
    terms_b = [(n2, gh)]
    qb = grad_theirs(3, terms_b)
    if gather:
        pr.back_x()
    grad_ours(3, terms_b, out_b)
    g2.finish()
    for c in loads[5:]:
        c.wait()
    gmid_all = gmid_low[...].reshape(total, width)
    cpad = ctx.shape[1]
    cut = width - cpad
    gcx = nn(gmid_all, wa[:, cut:]).astype(bf)
    shown = jnp.where(res[s] == 1, VIS, VIS_SMALL)
    bias = jnp.where(iota((1, total), 1) < shown, 0.0, NEG)
    scale = HD_ENC**-0.5
    scale2 = scale * LOG2E
    heads = (width // 4) // HD_ENC
    for h in range(heads):
        q = qkv[:, h * HD_ENC : (h + 1) * HD_ENC]
        k = qkv[:, (heads + h) * HD_ENC : (heads + h + 1) * HD_ENC]
        v = qkv[:, (2 * heads + h) * HD_ENC : (2 * heads + h + 1) * HD_ENC]
        go = gcx[:, (h + 1) * HD_ENC : (h + 2) * HD_ENC]
        co = ctx[:, (h + 1) * HD_ENC : (h + 2) * HD_ENC]
        scr = nt(q, k) + bias
        e = jnp.exp2((scr - jnp.max(scr, axis=1, keepdims=True)) * scale2)
        p = e / jnp.sum(e, axis=1, keepdims=True)
        delta = jnp.sum(go.astype(f32) * co.astype(f32), axis=1, keepdims=True)
        gs = (p * (nt(go, v) - delta) * scale).astype(bf)
        gqkv[:, h * HD_ENC : (h + 1) * HD_ENC] = nn(gs, k).astype(bf)
        gqkv[:, (heads + h) * HD_ENC : (heads + h + 1) * HD_ENC] = tn(gs, q).astype(bf)
        gqkv[:, (2 * heads + h) * HD_ENC : (2 * heads + h + 1) * HD_ENC] = tn(p.astype(bf), go).astype(bf)
        if gather and h == 0:
            qc.near()
    gqkv[:, 3 * heads * HD_ENC :] = jnp.zeros((total, width - 3 * heads * HD_ENC), bf)
    part[...] = nt(gqkv[...], wa[...]).reshape(part.shape)
    r2 = ReduceMp(cx, part, stage.at[1], recv.at[1])
    cols = (pl.ds(0, cut), pl.ds(cut, cpad))
    outs = (None, None) if gather else [out_qkv.at[:, c] for c in cols]
    terms_a = [(n1, gqkv[:, :cut])]
    terms_a2 = [(n1, gqkv[:, cut:]), (gmid_low, ctx[...])]
    qa = grad_theirs(0, terms_a)
    r2.middle()
    qa2 = grad_theirs(1, terms_a2)
    if gather:
        qb.near()
        qc.far()
        pr.back_y()
    grad_ours(0, terms_a, outs[0])
    grad_ours(1, terms_a2, outs[1])
    g_n1 = r2.finish()
    stream = x_all[s].astype(f32)
    grad_in, gain_in, shift_in = normalize_back(stream, gains[0:1, :], g_n1)
    grad = gmid_half[...] + grad_in
    dw = dsmall.shape[1]
    vec = jnp.concatenate(
        [
            gain_in,
            gain_mid,
            shift_in,
            shift_mid,
            jnp.zeros((4, width), f32),
            jnp.concatenate([dsmall[...], jnp.zeros((8, width - dw), f32)], axis=1),
        ],
        axis=0,
    )
    if gather:
        smr[0] = vec
        c = cx.send(smr.at[0], smr.at[1], cx.core)
        g = qd.finish()
        gbuf[0 : yst.shape[0], :unit_d] = g[:, :unit_d]
        yst[...] = g[:, unit_d:].astype(bf)
        c.wait_recv()
        smr[2] = smr[0] + smr[1]
        c = cx.send(smr.at[2], smr.at[3], cx.y)
        qb.far()
        qa.near()
        c.wait_recv()
        smr[4] = smr[2] + smr[3]
        c = cx.send(smr.at[4], smr.at[5], cx.x)
        pr.back_core()
        cyd = cx.send(yst, yrc, cx.y)
    part[0, :, :half] = grad[:, :half]
    part[1, :, :half] = grad[:, half:]
    gin[s] = part[s, :, :half]
    cin = cx.send(part.at[1 - s, :, pl.ds(0, half)], gin.at[s], cx.x)
    if gather:
        out_c[...] = qc.finish()
        qa2.near()
        qa.far()
        c.wait_recv()
        smz[cx.d] = smr[4] + smr[5]
        cs = [cx.send(smz.at[cx.d], smz.at[cx.d], cx.z(k)) for k in range(1, dp)]
        cyd.wait_recv()
        g = gbuf[0 : yst.shape[0], :unit_d] + yrc[...].astype(f32)
        unit = out_dqkv.shape[2]
        for t in range(3):
            out_dqkv[t] = g[:, t * unit : (t + 1) * unit]
        out_do[...] = g[:, 3 * unit :]
        qa2.far()
        pr.finish()
        out_b[...] = qb.finish()
        for c in cs:
            c.wait_recv()
        vec = sum_in_order(smz, dp)
        g = jnp.concatenate([qa.finish(), qa2.finish()], axis=1)
        unit = out_qkv.shape[2]
        for t in range(3):
            out_qkv[t] = g[:, t * unit : (t + 1) * unit]
        out_o[...] = g[:, 3 * unit :].T
    else:
        cyd.wait_recv()
        out_dqkv[...] = gd[:, :unit_d] + yrc[...].astype(f32)
        out_do[...] = jnp.zeros(out_do.shape, f32)
        out_o[...] = jnp.zeros(out_o.shape, f32)
    eg[...] = vec[0:2]
    es[...] = vec[2:4]
    dg[...] = vec[8:10, :dw]
    dsh[...] = vec[10:12, :dw]
    mg[...] = vec[12:13, :dw]
    cin.wait_recv()
    cx.drain()


def sum_in_order(ref, n):
    out = ref[0]
    for i in range(1, n):
        out = out + ref[i]
    return out


class ProjSum:
    def __init__(self, cx, st, rc, zs, zr, acc, whole, out):
        self.cx, self.st, self.rc, self.zs, self.zr = cx, st, rc, zs, zr
        self.acc, self.whole, self.out = acc, whole, out
        self.R, self.C = out.shape

    def rows(self, start, size):
        return pl.ds(pl.multiple_of(start, 16), size)

    def core(self, part):
        cx, R = self.cx, self.R
        h = R // 2
        self.acc[...] = part
        self.o1 = cx.lo * h
        self.st[0:h] = self.acc[self.rows((1 - cx.lo) * h, h), :].astype(bf)
        self.c = cx.send(self.st.at[pl.ds(0, h)], self.rc.at[pl.ds(0, h)], cx.core)

    def step(self, prev_at, prev_size, bit, dev):
        cx, R = self.cx, self.R
        self.c.wait_recv()
        off = R - 2 * prev_size
        mine = self.rows(prev_at, prev_size)
        self.acc[mine, :] = self.acc[mine, :] + self.rc[off : off + prev_size, :].astype(f32)
        h = prev_size // 2
        noff = R - 2 * h
        self.st[noff : noff + h] = self.acc[self.rows(prev_at + (1 - bit) * h, h), :].astype(bf)
        self.c = cx.send(self.st.at[pl.ds(noff, h)], self.rc.at[pl.ds(noff, h)], dev)
        return prev_at + bit * h

    def y(self):
        self.o2 = self.step(self.o1, self.R // 2, self.cx.hi, self.cx.y)

    def x(self):
        self.o3 = self.step(self.o2, self.R // 4, self.cx.s, self.cx.x)

    def z(self):
        cx, R = self.cx, self.R
        size, unit = R // 8, self.C // cx.dp
        self.c.wait_recv()
        off = R - 2 * size
        total = self.acc[self.rows(self.o3, size), :] + self.rc[off : off + size, :].astype(f32)
        for e in range(cx.dp):
            self.zs[e] = total[:, e * unit : (e + 1) * unit].astype(bf)
        self.cs = []
        for k in range(1, cx.dp):
            to = lax.rem(cx.d + k, cx.dp)
            self.cs.append(cx.send(self.zs.at[to], self.zr.at[k - 1], cx.z(k)))

    def back_z(self):
        cx = self.cx
        unit = self.C // cx.dp
        total = self.zs[cx.d].astype(f32)
        for k in range(1, cx.dp):
            self.cs[k - 1].wait_recv()
            total = total + self.zr[k - 1].astype(f32)
        at = self.whole.at[self.rows(self.o3, self.R // 8), pl.ds(pl.multiple_of(cx.d * unit, 128), unit)]
        at[...] = total.astype(bf)
        self.cs = [cx.send(at, at, cx.z(k)) for k in range(1, cx.dp)]

    def back_x(self):
        for c in self.cs:
            c.wait_recv()
        at = self.rows(self.o3, self.R // 8)
        self.c = self.cx.send(self.whole.at[at], self.whole.at[at], self.cx.x)

    def back_y(self):
        self.c.wait_recv()
        at = self.rows(self.o2, self.R // 4)
        self.c = self.cx.send(self.whole.at[at], self.whole.at[at], self.cx.y)

    def back_core(self):
        self.c.wait_recv()
        at = self.rows(self.o1, self.R // 2)
        self.c = self.cx.send(self.whole.at[at], self.whole.at[at], self.cx.core)

    def finish(self):
        self.c.wait_recv()
        self.out[...] = self.whole[...].astype(f32)


def enc_backward(dp, gather, res, x, gains, proj, weights, saved, glow, gd, dsmall, ec, dc):
    wa, wb, wc = weights
    n1, n2, qkv, ctx, slope, active, mid, top = saved
    rows, width = x.shape[1:]
    total = 4 * rows
    V = pltpu.VMEM
    dd, dw = gd.shape[0], gd.shape[1] // 2
    er, dr = wa.shape[0] // (2 * dp), dd // (2 * dp)
    outs = [sds((2, rows, width // 2), f32)]
    if gather:
        outs += [sds((3, er, ec), f32), sds((ec, er), f32), sds((er, wb.shape[1]), f32), sds((er, wc.shape[1]), f32)]
        outs += [sds((3, dr, dc), f32), sds((dr, dc), f32)]
    else:
        outs += [sds(wa.shape, f32), sds((8, 128), f32), sds(wb.shape, f32), sds(wc.shape, f32)]
        outs += [sds((dd, dw), f32), sds((8, 128), f32)]
    outs += [sds((2, width), f32), sds((2, width), f32), sds(proj.shape, f32)]
    outs += [sds((1, dd), f32), sds((2, dd), f32), sds((2, dd), f32)]
    slots = (4, rows, width)
    hbm = (wc, slope, wb, active, n2, wa, ctx, qkv, n1)
    scratch = [
        pltpu.SemaphoreType.DMA((80,)),
        pltpu.SemaphoreType.DMA((80,)),
        pltpu.SemaphoreType.DMA((16,)),
    ]
    scratch += [V(a.shape, a.dtype) for a in hbm]
    scratch += [
        V((4,) + glow.shape, bf),
        V(slots, bf),
        V(slots, bf),
        V((total, width), bf),
        V(slots, f32),
        V((2, 3, rows, width), bf),
        V((2, 3, rows, width), bf),
        V((dd // 2, 2 * dw) if gather else (8, 128), f32),
        V((dr if gather else dd, dw), bf),
        V((dr if gather else dd, dw), bf),
        V((rows, width), f32),
    ]
    if gather:
        cpad = ctx.shape[1]
        widths = (wa.shape[1] - cpad, cpad, wc.shape[1], wb.shape[1])
        for w in widths:
            scratch += scatter_scratch(dp, er, w)
        scratch += scatter_scratch(dp, dr, 2 * dw)
        scratch += [V((dp * er, w), f32) for w in widths]
        scratch += [
            V((6, 16, width), f32),
            V((dp, 16, width), f32),
            V(proj.shape, bf),
            V(proj.shape, bf),
            V((dp, proj.shape[0] // 8, proj.shape[1] // dp), bf),
            V((dp - 1, proj.shape[0] // 8, proj.shape[1] // dp), bf),
            V(proj.shape, f32),
            V(proj.shape, bf),
        ]
    return pl.pallas_call(
        functools.partial(enc_backward_kernel, dp, gather),
        out_shape=outs,
        in_specs=[SMEM] + vm(8) + anywhere(9),
        out_specs=vm(len(outs)),
        scratch_shapes=scratch,
        compiler_params=params(3),
        name="enc_backward",
    )(res, x, gains, proj, mid, top, glow, gd, dsmall, *hbm)


def place_kernel(n, *refs):
    ins, outs, held = refs[:n], refs[n : 2 * n], refs[2 * n : 3 * n]
    sems = refs[3 * n]
    reads = [pltpu.make_async_copy(ins[i], held[i], sems.at[0, i]) for i in range(n)]
    writes = [pltpu.make_async_copy(held[i], outs[i], sems.at[1, i]) for i in range(n)]
    for c in reads:
        c.start()
    for r, w in zip(reads, writes):
        r.wait()
        w.start()
    for c in writes:
        c.wait()


def place_outputs(arrays):
    n = len(arrays)
    return pl.pallas_call(
        functools.partial(place_kernel, n),
        out_shape=[sds(a.shape, a.dtype) for a in arrays],
        in_specs=anywhere(n),
        out_specs=anywhere(n),
        scratch_shapes=[pltpu.VMEM(a.shape, a.dtype) for a in arrays] + [pltpu.SemaphoreType.DMA((2, n))],
        compiler_params=pltpu.CompilerParams(vmem_limit_bytes=60 << 20),
        name="place_outputs",
    )(*arrays)


def position_table(count, quarter):
    freq = (np.float32(10000.0) ** (-np.arange(quarter, dtype=np.float32) / np.float32(quarter))).astype(np.float32)
    angle = (np.arange(count, dtype=np.float32)[:, None] * freq[None, :]).astype(np.float32).astype(np.float64)
    return np.concatenate([np.sin(angle), np.cos(angle)], axis=1).astype(np.float32)


def per_device(
    x_visible,
    resolution,
    visible_index,
    enc_qkv_w,
    enc_out_w,
    enc_up_w,
    enc_down_w,
    enc_gains,
    enc_shifts,
    projection,
    mask_token,
    dec_qkv_w,
    dec_out_w,
    dec_up_w,
    dec_down_w,
    dec_gains,
    dec_shifts,
    cotangent,
):
    dp = lax.axis_size("dp")
    over = ("section", "dp")
    er, dr = enc_qkv_w.shape[0], dec_qkv_w.shape[0]
    de, dd = projection.shape
    ec, dc = enc_qkv_w.shape[2], dec_qkv_w.shape[2]
    gather = er % 16 == 0 and dr % 16 == 0 and dp == 4
    if gather:
        shards = [
            jnp.transpose(enc_qkv_w, (1, 0, 2)),
            enc_out_w,
            enc_up_w,
            enc_down_w.T,
            jnp.transpose(dec_qkv_w, (1, 0, 2)),
            dec_out_w.T,
        ]
        e_in, f_in = dec_up_w, dec_down_w.T
    else:
        whole = [
            lax.all_gather(w, over, axis=0, tiled=True)
            for w in (
                jnp.concatenate([enc_qkv_w.reshape(er, 3 * ec), enc_out_w.T], axis=1),
                enc_up_w,
                enc_down_w.T,
                jnp.concatenate([dec_qkv_w.reshape(dr, 3 * dc), dec_out_w.T], axis=1),
                dec_up_w,
                dec_down_w.T,
            )
        ]
        shards, (e_in, f_in) = whole[:4], whole[4:]
    weights, saved = enc_forward(
        dp,
        gather,
        resolution,
        x_visible,
        enc_gains,
        enc_shifts,
        projection,
        shards,
        de,
        dd,
        enc_up_w.shape[1],
        dec_up_w.shape[1],
    )
    table = jnp.asarray(position_table(COLS_BIG, dd // 4))
    out, glow, gd, ge, gf, dsmall, _ = decoder(
        dp,
        gather,
        resolution,
        visible_index,
        saved[8],
        table,
        cotangent,
        dec_gains,
        dec_shifts,
        mask_token[None, :],
        weights[3],
        e_in,
        f_in,
    )
    back = enc_backward(
        dp,
        gather,
        resolution,
        x_visible,
        enc_gains,
        projection,
        weights[:3],
        saved[:8],
        glow,
        gd,
        dsmall,
        ec,
        dc,
    )
    if gather:
        got = place_outputs((out, ge, gf) + tuple(back))
        out, ge, gf, gin, gqkv, go, gb, gc, hqkv, ho, eg, es, pg, mg, dg, ds = got
        gqkv = jnp.transpose(gqkv, (1, 0, 2))
        hqkv = jnp.transpose(hqkv, (1, 0, 2))
        ho = ho.T
    else:
        gin, ga, _, gb, gc, hd, _, eg, es, pg, mg, dg, ds = back
        ga, gb, gc, hd, ge, gf = [
            lax.psum_scatter(g, over, scatter_dimension=0, tiled=True) for g in (ga, gb, gc, hd, ge, gf)
        ]
        eg, es, pg, mg, dg, ds = lax.psum((eg, es, pg, mg, dg, ds), ("section", "dp", "mp"))
        gqkv, go = ga[:, : 3 * ec].reshape(er, 3, ec), ga[:, 3 * ec :].T
        hqkv, ho = hd[:, : 3 * dc].reshape(dr, 3, dc), hd[:, 3 * dc :].T
    return (out, gin, gqkv, go, gb, gc.T, eg, es, pg, mg[0], hqkv, ho, ge, gf.T, dg, ds)


def solution(mesh):
    matrix_in = P(("section", "dp"), "mp")
    matrix_out = P("mp", ("section", "dp"))
    qkv = P(("section", "dp"), None, "mp")
    return jax.shard_map(
        per_device,
        mesh=mesh,
        in_specs=(
            P("dp", "mp", None),
            P("dp"),
            P("dp", None),
            qkv,
            matrix_out,
            matrix_in,
            matrix_out,
            P(),
            P(),
            P(),
            P(),
            qkv,
            matrix_out,
            matrix_in,
            matrix_out,
            P(),
            P(),
            P("dp", "mp", None),
        ),
        out_specs=(
            P("dp", "mp", "section"),
            P("dp", "mp", "section"),
            qkv,
            matrix_out,
            matrix_in,
            matrix_out,
            P(),
            P(),
            P(),
            P(),
            qkv,
            matrix_out,
            matrix_in,
            matrix_out,
            P(),
            P(),
        ),
        check_vma=False,
    )
```
